32 devices in a mesh: grp: 2 (over y), gx: 4 (over z), gy: 2 (over x), gz: 2 (over core).
Axes of the slice: x: 2, y: 2, z: 4, core: 2. Of those that a mesh axis runs over, the one named last changes fastest.
Arguments:
- tokens: bfloat16 [72, 8192], P(('grp', 'gy', 'gz'), 'gx'), parts along dimension 0, may hold values from -6 to 6
- gate_weight: bfloat16 [8192, 26624], P('gx', ('gy', 'gz')), may hold values from -0.0625 to 0.0625
- up_weight: bfloat16 [8192, 26624], P('gx', ('gy', 'gz')), may hold values from -0.0625 to 0.0625
- down_weight: bfloat16 [26624, 8192], P(('gy', 'gz'), 'gx'), may hold values from -0.0390625 to 0.0390625
Outputs:
- mixed: bfloat16 [72, 8192], P(('grp', 'gy', 'gz'), 'gx'), parts along dimension 0
The draws below stay inside these ranges and needn't reach their ends.
There are 2 independent parts, one for each index of `grp`. The reference program is written for one: setup_inputs(seed, part) draws one part's arguments, and reference() takes and returns one part's arrays. A program takes and returns all parts, laid end to end along the dimension named above; an argument that names none is the same for every part. Nothing has to cross between parts.
All inputs are finite; a program needn't handle non-finite values.
Results may differ from the reference program's by a relative error of at most 0.019.
Values may be sent and summed in bfloat16 or wider, within the bound.
No kernel may reach another device: no remote copies, remote signals or barrier semaphores. Data moves between devices by JAX's collectives and lax.ppermute only.
A program may use at most 192 MiB of HBM per device.

```python
import jax
import jax.numpy as jnp
from jax import lax

D = 8192
FF = 26624
TOKENS = 36
N_GX = 4


def level_of(own_key, extent, pieces, smallest, high):
    def one(position, shards_of):
        steps = jax.random.uniform(jax.random.fold_in(jax.random.fold_in(own_key, 6), position), (shards_of,), jnp.float32, smallest / len(pieces), high / len(pieces))
        return jnp.repeat(jnp.exp(steps), extent[position] // shards_of).reshape((-1,) + (1,) * (len(extent) - position - 1))

    factor_of = one(*pieces[0])
    for cut in pieces[1:]:
        factor_of = factor_of * one(*cut)
    return factor_of


def scatter_about(own_key, dims, deviation, reach, cuts=(), held_as=jnp.bfloat16):
    entries = deviation * jax.random.normal(own_key, dims, jnp.float32)
    if cuts:
        entries = entries * level_of(own_key, dims, cuts, -0.22, 0.18)
    return jnp.clip(entries, -reach, reach).astype(held_as)


def setup_inputs(seed: int = 0, part: int = 0) -> dict:
    key_of = jax.random.split(jax.random.key(seed), 5)
    part_splits = jax.random.split(jax.random.fold_in(key_of[4], part), 5)
    return {
        "tokens": scatter_about(part_splits[0], (TOKENS, D), 1.0, 6.0, ((0, 4), (1, 4))),
        "gate_weight": scatter_about(key_of[1], (D, FF), D ** -0.5, 0.0625, ((0, 4), (1, 4))),
        "up_weight": scatter_about(key_of[2], (D, FF), D ** -0.5, 0.0625, ((0, 4), (1, 4))),
        "down_weight": scatter_about(key_of[3], (FF, D), FF ** -0.5, 0.0390625, ((0, 4), (1, 4))),
    }


def block_sum(activations, weight):
    row_count = activations.shape[0]
    out_width = weight.shape[1]
    left_blocks = activations.reshape(row_count, N_GX, D // N_GX).transpose(1, 0, 2)
    weight_blocks = weight.reshape(N_GX, D // N_GX, out_width)

    def advance(running, operands):
        block_term = jnp.dot(operands[0], operands[1], preferred_element_type=jnp.float32).astype(jnp.bfloat16)
        block_term = lax.optimization_barrier(block_term)
        return running + block_term.astype(jnp.float32), None

    start_sum = jnp.zeros((row_count, out_width), jnp.float32)
    running, _ = lax.scan(advance, start_sum, (left_blocks, weight_blocks))
    return running


def reference(tokens, gate_weight, up_weight, down_weight):
    gate = block_sum(tokens, gate_weight)
    up = block_sum(tokens, up_weight)
    hidden = (jax.nn.silu(gate) * up).astype(jnp.bfloat16)
    return jnp.dot(hidden, down_weight, preferred_element_type=jnp.float32).astype(jnp.bfloat16)
```

```python
import functools

import jax
import jax.numpy as jnp
from jax import lax
from jax.experimental import pallas as pl
from jax.experimental.pallas import tpu as pltpu
from jax.sharding import PartitionSpec as P

MIB = 1 << 20
TOKEN_AXES = ("gy", "gz")
ANY = pl.BlockSpec(memory_space=pl.ANY)
WHOLE = pl.BlockSpec(memory_space=pltpu.VMEM)
SCALARS = pl.BlockSpec(memory_space=pltpu.SMEM)


def activate(gate, up):
    return (jax.nn.silu(gate) * up).astype(jnp.bfloat16)


def pieces_of(total, step):
    return [(start, min(step, total - start)) for start in range(0, total, step)]


def gate_up_kernel(width, depth_step, starts, x_ref, gate_ref, up_ref, _, *rest):
    outs, (held, total, sems) = rest[:-3], rest[-3:]
    blocks = len(outs)
    parts = pieces_of(x_ref.shape[1], depth_step)
    copies = []
    for b in range(blocks):
        columns = pl.ds(pl.multiple_of(starts[b], 128), width)
        for k, (row, rows) in enumerate(parts):
            for w, weight in enumerate((gate_ref, up_ref)):
                copy = pltpu.make_async_copy(
                    weight.at[pl.ds(row, rows), columns],
                    held.at[b, w, pl.ds(row, rows)],
                    sems.at[b, w, k],
                )
                copy.start()
                copies.append((b, w, k, row, rows, copy))
    for b, w, k, row, rows, copy in copies:
        copy.wait()
        term = jnp.dot(
            x_ref[:, row : row + rows],
            held[b, w, row : row + rows, :],
            preferred_element_type=jnp.float32,
        )
        if k == 0:
            total[w] = term
        elif k < len(parts) - 1:
            total[w] += term
        else:
            outs[b][:, w * width : (w + 1) * width] = (total[w] + term).astype(jnp.bfloat16)


def gate_up(features, gate_weight, up_weight, starts, width, after):
    rows, depth = features.shape
    blocks = starts.shape[0]
    step = 256
    return pl.pallas_call(
        functools.partial(gate_up_kernel, width, step),
        out_shape=[jax.ShapeDtypeStruct((rows, 2 * width), jnp.bfloat16)] * blocks,
        in_specs=[SCALARS, WHOLE, ANY, ANY, ANY],
        out_specs=[WHOLE] * blocks,
        scratch_shapes=[
            pltpu.VMEM((blocks, 2, depth, width), jnp.bfloat16),
            pltpu.VMEM((2, rows, width), jnp.float32),
            pltpu.SemaphoreType.DMA((blocks, 2, len(pieces_of(depth, step)))),
        ],
        compiler_params=pltpu.CompilerParams(vmem_limit_bytes=48 * MIB),
        cost_estimate=pl.CostEstimate(
            flops=4 * rows * depth * width * blocks,
            bytes_accessed=4 * depth * width * blocks,
            transcendentals=0,
        ),
    )(starts, features, gate_weight, up_weight, after)


def down_kernel(first, depth_step, starts, *refs):
    blocks = starts.shape[0]
    hidden, refs = refs[:blocks], refs[blocks:]
    if not first:
        before, refs = refs[0], refs[1:]
    down_ref, outs, (held, total, sems) = refs[0], refs[1:-3], refs[-3:]
    width = hidden[0].shape[1]
    parts = pieces_of(width, depth_step)
    copies = []
    for b in range(blocks):
        for k, (row, rows) in enumerate(parts):
            source = pl.ds(pl.multiple_of(starts[b] + row, 128), rows)
            copy = pltpu.make_async_copy(
                down_ref.at[source], held.at[b, pl.ds(row, rows)], sems.at[b, k]
            )
            copy.start()
            copies.append((b, row, rows, copy))
    if first:
        total[...] = jnp.zeros_like(total)
    else:
        total[...] = before[...]
    for b, row, rows, copy in copies:
        copy.wait()
        total[...] += jnp.dot(
            hidden[b][:, row : row + rows],
            held[b, row : row + rows, :],
            preferred_element_type=jnp.float32,
        )
    if len(outs) == 1:
        outs[0][...] = total[...]
    else:
        tall = outs[0].shape[0]
        for r, out in enumerate(outs):
            out[...] = total[r * tall : (r + 1) * tall, :].astype(out.dtype)


def down(hidden, starts, before, down_weight, outs):
    rows, width = hidden[0].shape
    columns = down_weight.shape[1]
    blocks = len(hidden)
    step = 256
    if outs == 1:
        shapes = [jax.ShapeDtypeStruct((rows, columns), jnp.float32)]
    else:
        shapes = [jax.ShapeDtypeStruct((rows // outs, columns), jnp.bfloat16)] * outs
    carried = [] if before is None else [before]
    return pl.pallas_call(
        functools.partial(down_kernel, before is None, step),
        out_shape=shapes,
        in_specs=[SCALARS] + [WHOLE] * (blocks + len(carried)) + [ANY],
        out_specs=[WHOLE] * outs,
        scratch_shapes=[
            pltpu.VMEM((blocks, width, columns), jnp.bfloat16),
            pltpu.VMEM((rows, columns), jnp.float32),
            pltpu.SemaphoreType.DMA((blocks, len(pieces_of(width, step)))),
        ],
        compiler_params=pltpu.CompilerParams(vmem_limit_bytes=48 * MIB),
        cost_estimate=pl.CostEstimate(
            flops=2 * rows * columns * width * blocks,
            bytes_accessed=2 * columns * width * blocks,
            transcendentals=0,
        ),
    )(starts, *hidden, *carried, down_weight)


def swap(value, axes, size, distance):
    return lax.ppermute(value, axes, [(i, i ^ distance) for i in range(size)])


def direct(tokens, gate_weight, up_weight, down_weight):
    n_gx = lax.axis_size("gx")
    n_token = lax.axis_size(TOKEN_AXES)
    me = lax.axis_index("gx")
    width = gate_weight.shape[1] // n_gx
    features = jnp.concatenate(
        [tokens] + [swap(tokens, TOKEN_AXES, n_token, r) for r in range(1, n_token)], axis=0
    )

    def starts_of(distances):
        return jnp.stack([(me ^ d) * width for d in distances]).astype(jnp.int32)

    received = []
    after = tokens
    for d in range(n_gx - 1, 0, -1):
        (block,) = gate_up(features, gate_weight, up_weight, starts_of([d]), width, after)
        received.append(swap(block, "gx", n_gx, d))
        after = block
    (own,) = gate_up(features, gate_weight, up_weight, starts_of([0]), width, after)
    summed = own.astype(jnp.float32)
    for block in received:
        summed = summed + block.astype(jnp.float32)
    hidden = activate(summed[:, :width], summed[:, width:])

    blocks = [hidden] + [swap(hidden, "gx", n_gx, d) for d in range(1, n_gx)]
    half = n_gx // 2
    (partial_sum,) = down(blocks[:half], starts_of(range(half)), None, down_weight, 1)
    outs = down(blocks[half:], starts_of(range(half, n_gx)), partial_sum, down_weight, n_token)
    result = outs[0].astype(jnp.float32)
    for r in range(1, n_token):
        result = result + swap(outs[r], TOKEN_AXES, n_token, r).astype(jnp.float32)
    return result.astype(jnp.bfloat16)


def offloaded(tokens, gate_weight, up_weight, down_weight):
    features = lax.all_gather(tokens, TOKEN_AXES, axis=0, tiled=True)
    hidden_width = gate_weight.shape[1]
    gate_part = jnp.dot(features, gate_weight, preferred_element_type=jnp.float32)
    up_part = jnp.dot(features, up_weight, preferred_element_type=jnp.float32)
    summed = lax.psum(
        jnp.concatenate([gate_part, up_part], axis=1).astype(jnp.bfloat16), "gx"
    ).astype(jnp.float32)
    hidden = activate(summed[:, :hidden_width], summed[:, hidden_width:])
    partial_value = jnp.dot(hidden, down_weight, preferred_element_type=jnp.float32)
    return lax.psum_scatter(
        partial_value.astype(jnp.bfloat16), TOKEN_AXES, scatter_dimension=0, tiled=True
    )


def shards(tokens, gate_weight, up_weight, down_weight):
    n_gx = lax.axis_size("gx")
    n_token = lax.axis_size(TOKEN_AXES)
    powers = all(n > 1 and n & (n - 1) == 0 for n in (n_gx, n_token))
    blocks_fit = gate_weight.shape[1] % (128 * n_gx) == 0 and n_gx <= 4
    if powers and blocks_fit:
        return direct(tokens, gate_weight, up_weight, down_weight)
    return offloaded(tokens, gate_weight, up_weight, down_weight)


def solution(mesh):
    return jax.shard_map(
        shards,
        mesh=mesh,
        in_specs=(
            P(("grp", "gy", "gz"), "gx"),
            P("gx", ("gy", "gz")),
            P("gx", ("gy", "gz")),
            P(("gy", "gz"), "gx"),
        ),
        out_specs=P(("grp", "gy", "gz"), "gx"),
        check_vma=False,
    )
```

```python
import functools

import jax
import jax.numpy as jnp
from jax import lax
from jax.experimental import pallas as pl
from jax.experimental.pallas import tpu as pltpu
from jax.sharding import PartitionSpec as P

MIB = 1 << 20
TOKEN_AXES = ("gy", "gz")
ANY = pl.BlockSpec(memory_space=pl.ANY)
IN_HBM = pl.BlockSpec(memory_space=pltpu.HBM)
WHOLE = pl.BlockSpec(memory_space=pltpu.VMEM)
SCALARS = pl.BlockSpec(memory_space=pltpu.SMEM)


def activate(gate, up):
    return (jax.nn.silu(gate) * up).astype(jnp.bfloat16)


def pieces_of(total, step):
    return [(start, min(step, total - start)) for start in range(0, total, step)]


def in_hbm(value):
    return pltpu.with_memory_space_constraint(value, pltpu.HBM)


def in_vmem(value):
    return pltpu.with_memory_space_constraint(value, pltpu.VMEM)


def cost(nbytes):
    return pl.CostEstimate(flops=0, bytes_accessed=nbytes, transcendentals=0)


def fetch_gate_up_kernel(width, step, start_ref, gate_ref, up_ref, held, sems):
    columns = pl.ds(pl.multiple_of(start_ref[0], 128), width)
    copies = []
    for k, (row, rows) in enumerate(pieces_of(held.shape[1], step)):
        for w, weight in enumerate((gate_ref, up_ref)):
            copy = pltpu.make_async_copy(
                weight.at[pl.ds(row, rows), columns], held.at[w, pl.ds(row, rows)], sems.at[w, k]
            )
            copy.start()
            copies.append(copy)
    for copy in copies:
        copy.wait()


def fetch_gate_up(gate_weight, up_weight, start, width):
    depth, step = gate_weight.shape[0], 256
    return pl.pallas_call(
        functools.partial(fetch_gate_up_kernel, width, step),
        out_shape=pltpu.VMEM((2, depth, width), jnp.bfloat16),
        in_specs=[SCALARS, IN_HBM, IN_HBM],
        out_specs=WHOLE,
        scratch_shapes=[pltpu.SemaphoreType.DMA((2, len(pieces_of(depth, step))))],
        compiler_params=pltpu.CompilerParams(vmem_limit_bytes=8 * MIB),
        cost_estimate=cost(MIB),
    )(start, in_hbm(gate_weight), in_hbm(up_weight))


def gate_up_held_kernel(step, x_ref, held, out, total):
    width = held.shape[2]
    parts = pieces_of(x_ref.shape[1], step)
    for w in range(2):
        for k, (row, rows) in enumerate(parts):
            term = jnp.dot(
                x_ref[:, row : row + rows],
                held[w, row : row + rows, :],
                preferred_element_type=jnp.float32,
            )
            if k == 0:
                total[...] = term
            elif k < len(parts) - 1:
                total[...] += term
            else:
                out[:, w * width : (w + 1) * width] = (total[...] + term).astype(jnp.bfloat16)


def gate_up_held(features, held):
    rows = features.shape[0]
    width = held.shape[2]
    return pl.pallas_call(
        functools.partial(gate_up_held_kernel, 256),
        out_shape=jax.ShapeDtypeStruct((rows, 2 * width), jnp.bfloat16),
        in_specs=[WHOLE, WHOLE],
        out_specs=WHOLE,
        scratch_shapes=[pltpu.VMEM((rows, width), jnp.float32)],
        compiler_params=pltpu.CompilerParams(vmem_limit_bytes=8 * MIB),
        cost_estimate=cost(MIB),
    )(features, in_vmem(held))


def gate_up_kernel(width, step, start_ref, x_ref, gate_ref, up_ref, _, out, held, total, sems):
    parts = pieces_of(x_ref.shape[1], step)
    columns = pl.ds(pl.multiple_of(start_ref[0], 128), width)
    copies = []
    for k, (row, rows) in enumerate(parts):
        for w, weight in enumerate((gate_ref, up_ref)):
            copy = pltpu.make_async_copy(
                weight.at[pl.ds(row, rows), columns], held.at[w, pl.ds(row, rows)], sems.at[w, k]
            )
            copy.start()
            copies.append((w, k, row, rows, copy))
    for w, k, row, rows, copy in copies:
        copy.wait()
        term = jnp.dot(
            x_ref[:, row : row + rows],
            held[w, row : row + rows, :],
            preferred_element_type=jnp.float32,
        )
        if k == 0:
            total[w] = term
        elif k < len(parts) - 1:
            total[w] += term
        else:
            out[:, w * width : (w + 1) * width] = (total[w] + term).astype(jnp.bfloat16)


def gate_up(features, gate_weight, up_weight, start, width, after):
    rows, depth = features.shape
    step = 256
    return pl.pallas_call(
        functools.partial(gate_up_kernel, width, step),
        out_shape=jax.ShapeDtypeStruct((rows, 2 * width), jnp.bfloat16),
        in_specs=[SCALARS, WHOLE, IN_HBM, IN_HBM, ANY],
        out_specs=WHOLE,
        scratch_shapes=[
            pltpu.VMEM((2, depth, width), jnp.bfloat16),
            pltpu.VMEM((2, rows, width), jnp.float32),
            pltpu.SemaphoreType.DMA((2, len(pieces_of(depth, step)))),
        ],
        compiler_params=pltpu.CompilerParams(vmem_limit_bytes=24 * MIB),
        cost_estimate=cost(MIB),
    )(start, features, in_hbm(gate_weight), in_hbm(up_weight), after)


def fetch_down_kernel(step, own_ref, down_ref, own_out, held, sems):
    copies = []
    for k, (row, rows) in enumerate(pieces_of(held.shape[0], step)):
        copy = pltpu.make_async_copy(
            down_ref.at[pl.ds(row, rows)], held.at[pl.ds(row, rows)], sems.at[k]
        )
        copy.start()
        copies.append(copy)
    own_out[...] = own_ref[...].astype(jnp.float32)
    for copy in copies:
        copy.wait()


def fetch_down(own, down_weight):
    step = 512
    return pl.pallas_call(
        functools.partial(fetch_down_kernel, step),
        out_shape=(
            jax.ShapeDtypeStruct(own.shape, jnp.float32),
            pltpu.VMEM(down_weight.shape, jnp.bfloat16),
        ),
        in_specs=[WHOLE, IN_HBM],
        out_specs=(WHOLE, WHOLE),
        scratch_shapes=[pltpu.SemaphoreType.DMA((len(pieces_of(down_weight.shape[0], step)),))],
        compiler_params=pltpu.CompilerParams(vmem_limit_bytes=8 * MIB),
        cost_estimate=cost(MIB),
    )(own, in_hbm(down_weight))


def down_kernel(first, starts, *refs):
    blocks = starts.shape[0]
    hidden, refs = refs[:blocks], refs[blocks:]
    if not first:
        before, refs = refs[0], refs[1:]
    held, outs, total = refs[0], refs[1:-1], refs[-1]
    width = hidden[0].shape[1]
    for b in range(blocks):
        rows = pl.ds(pl.multiple_of(starts[b], 128), width)
        term = jnp.dot(hidden[b][...], held[rows, :], preferred_element_type=jnp.float32)
        if b == 0 and first:
            total[...] = term
        elif b == 0:
            total[...] = before[...] + term
        else:
            total[...] += term
    if len(outs) == 1:
        outs[0][...] = total[...]
    else:
        tall = outs[0].shape[0]
        for r, out in enumerate(outs):
            out[...] = total[r * tall : (r + 1) * tall, :].astype(out.dtype)


def down(hidden, starts, before, held, outs):
    rows = hidden[0].shape[0]
    columns = held.shape[1]
    if outs == 1:
        shapes = [jax.ShapeDtypeStruct((rows, columns), jnp.float32)]
    else:
        shapes = [jax.ShapeDtypeStruct((rows // outs, columns), jnp.bfloat16)] * outs
    carried = [] if before is None else [before]
    return pl.pallas_call(
        functools.partial(down_kernel, before is None),
        out_shape=shapes,
        in_specs=[SCALARS] + [WHOLE] * (len(hidden) + len(carried) + 1),
        out_specs=[WHOLE] * outs,
        scratch_shapes=[pltpu.VMEM((rows, columns), jnp.float32)],
        compiler_params=pltpu.CompilerParams(vmem_limit_bytes=8 * MIB),
        cost_estimate=cost(MIB),
    )(starts, *hidden, *carried, in_vmem(held))


def swap(value, axes, size, distance):
    return lax.ppermute(value, axes, [(i, i ^ distance) for i in range(size)])


def direct(tokens, gate_weight, up_weight, down_weight):
    n_gx = lax.axis_size("gx")
    n_token = lax.axis_size(TOKEN_AXES)
    me = lax.axis_index("gx")
    width = gate_weight.shape[1] // n_gx

    def starts_of(distances):
        return jnp.stack([(me ^ d) * width for d in distances]).astype(jnp.int32)

    held = fetch_gate_up(gate_weight, up_weight, starts_of([n_gx - 1]), width)
    features = jnp.concatenate(
        [tokens] + [swap(tokens, TOKEN_AXES, n_token, r) for r in range(1, n_token)], axis=0
    )

    received = []
    for d in range(n_gx - 1, -1, -1):
        if d == n_gx - 1:
            block = gate_up_held(features, held)
        else:
            block = gate_up(features, gate_weight, up_weight, starts_of([d]), width, block)
        if d:
            received.append(swap(block, "gx", n_gx, d))
    summed, down_held = fetch_down(block, down_weight)
    for term in received:
        summed = lax.optimization_barrier(summed + term.astype(jnp.float32))
    hidden = activate(summed[:, :width], summed[:, width:])

    blocks = [hidden] + [swap(hidden, "gx", n_gx, d) for d in range(1, n_gx)]
    half = n_gx // 2
    (partial_sum,) = down(blocks[:half], starts_of(range(half)), None, down_held, 1)
    outs = down(blocks[half:], starts_of(range(half, n_gx)), partial_sum, down_held, n_token)
    result = outs[0].astype(jnp.float32)
    for r in range(1, n_token):
        result = result + swap(outs[r], TOKEN_AXES, n_token, r).astype(jnp.float32)
    return result.astype(jnp.bfloat16)


def offloaded(tokens, gate_weight, up_weight, down_weight):
    features = lax.all_gather(tokens, TOKEN_AXES, axis=0, tiled=True)
    hidden_width = gate_weight.shape[1]
    gate_part = jnp.dot(features, gate_weight, preferred_element_type=jnp.float32)
    up_part = jnp.dot(features, up_weight, preferred_element_type=jnp.float32)
    summed = lax.psum(
        jnp.concatenate([gate_part, up_part], axis=1).astype(jnp.bfloat16), "gx"
    ).astype(jnp.float32)
    hidden = activate(summed[:, :hidden_width], summed[:, hidden_width:])
    partial_value = jnp.dot(hidden, down_weight, preferred_element_type=jnp.float32)
    return lax.psum_scatter(
        partial_value.astype(jnp.bfloat16), TOKEN_AXES, scatter_dimension=0, tiled=True
    )


def shards(tokens, gate_weight, up_weight, down_weight):
    n_gx = lax.axis_size("gx")
    n_token = lax.axis_size(TOKEN_AXES)
    powers = all(n > 1 and n & (n - 1) == 0 for n in (n_gx, n_token))
    blocks_fit = gate_weight.shape[1] % (128 * n_gx) == 0 and n_gx <= 4
    if powers and blocks_fit:
        return direct(tokens, gate_weight, up_weight, down_weight)
    return offloaded(tokens, gate_weight, up_weight, down_weight)


def solution(mesh):
    return jax.shard_map(
        shards,
        mesh=mesh,
        in_specs=(
            P(("grp", "gy", "gz"), "gx"),
            P("gx", ("gy", "gz")),
            P("gx", ("gy", "gz")),
            P(("gy", "gz"), "gx"),
        ),
        out_specs=P(("grp", "gy", "gz"), "gx"),
        check_vma=False,
    )
```

```python
import functools

import jax
import jax.numpy as jnp
from jax import lax
from jax.experimental import pallas as pl
from jax.experimental.pallas import tpu as pltpu
from jax.sharding import PartitionSpec as P

MIB = 1 << 20
STEP = 256
TOKEN_AXES = ("gy", "gz")
IN_HBM = pl.BlockSpec(memory_space=pltpu.HBM)
ANY = pl.BlockSpec(memory_space=pl.ANY)
WHOLE = pl.BlockSpec(memory_space=pltpu.VMEM)
SCALARS = pl.BlockSpec(memory_space=pltpu.SMEM)


def activate(gate, up):
    return (jax.nn.silu(gate) * up).astype(jnp.bfloat16)


def pieces_of(total, step):
    return [(start, min(step, total - start)) for start in range(0, total, step)]


def in_hbm(value):
    return pltpu.with_memory_space_constraint(value, pltpu.HBM)


def in_vmem(value):
    return pltpu.with_memory_space_constraint(value, pltpu.VMEM)


SMALL = pl.CostEstimate(flops=0, bytes_accessed=MIB, transcendentals=0)


def params(mib):
    return pltpu.CompilerParams(vmem_limit_bytes=mib * MIB)


def packed_pair_width(rows, width):
    return (rows // 8) * 2 * width + (width if rows % 8 else 0)


def pack_pair(out, gate, up):
    rows, width = gate.shape
    for g in range(rows // 8):
        for w, value in enumerate((gate, up)):
            at = (2 * g + w) * width
            out[:, at : at + width] = value[8 * g : 8 * g + 8].astype(out.dtype)
    if rows % 8:
        at = (rows // 8) * 2 * width
        tail = jnp.concatenate([gate[rows - 4 :], up[rows - 4 :]], axis=0)
        out[:, at : at + width] = tail.astype(out.dtype)


def start_copies(width, start_ref, gate_ref, up_ref, held, sems):
    columns = pl.ds(pl.multiple_of(start_ref[0], 128), width)
    copies = []
    for k, (row, rows) in enumerate(pieces_of(held.shape[1], STEP)):
        for w, weight in enumerate((gate_ref, up_ref)):
            copy = pltpu.make_async_copy(
                weight.at[pl.ds(row, rows), columns], held.at[w, pl.ds(row, rows)], sems.at[w, k]
            )
            copy.start()
            copies.append((w, row, rows, copy))
    return copies


def fetch_kernel(width, start_ref, gate_ref, up_ref, held, sems):
    for _, _, _, copy in start_copies(width, start_ref, gate_ref, up_ref, held, sems):
        copy.wait()


def fetch(gate_weight, up_weight, start, width):
    depth = gate_weight.shape[0]
    return pl.pallas_call(
        functools.partial(fetch_kernel, width),
        out_shape=pltpu.VMEM((2, depth, width), jnp.bfloat16),
        in_specs=[SCALARS, IN_HBM, IN_HBM],
        out_specs=WHOLE,
        scratch_shapes=[pltpu.SemaphoreType.DMA((2, len(pieces_of(depth, STEP))))],
        compiler_params=params(4),
        cost_estimate=SMALL,
    )(start, in_hbm(gate_weight), in_hbm(up_weight))


def multiply(x_ref, held, total, steps):
    for w, row, rows, copy in steps:
        if copy is not None:
            copy.wait()
        term = jnp.dot(
            x_ref[:, row : row + rows], held[w, row : row + rows, :], preferred_element_type=jnp.float32
        )
        if row == 0:
            total[w] = term
        else:
            total[w] += term


def held_kernel(x_ref, held, out, total):
    parts = pieces_of(x_ref.shape[1], STEP)
    multiply(x_ref, held, total, [(w, row, rows, None) for w in range(2) for row, rows in parts])
    pack_pair(out, total[0], total[1])


def gate_up_held(features, held):
    rows, width = features.shape[0], held.shape[2]
    return pl.pallas_call(
        held_kernel,
        out_shape=jax.ShapeDtypeStruct((8, packed_pair_width(rows, width)), jnp.bfloat16),
        in_specs=[WHOLE, WHOLE],
        out_specs=WHOLE,
        scratch_shapes=[pltpu.VMEM((2, rows, width), jnp.float32)],
        compiler_params=params(8),
        cost_estimate=SMALL,
    )(features, in_vmem(held))


def stream_kernel(width, start_ref, x_ref, gate_ref, up_ref, _, out, held, total, sems):
    copies = start_copies(width, start_ref, gate_ref, up_ref, held, sems)
    multiply(x_ref, held, total, copies)
    pack_pair(out, total[0], total[1])


def gate_up_stream(features, gate_weight, up_weight, start, width, after):
    rows, depth = features.shape
    return pl.pallas_call(
        functools.partial(stream_kernel, width),
        out_shape=jax.ShapeDtypeStruct((8, packed_pair_width(rows, width)), jnp.bfloat16),
        in_specs=[SCALARS, WHOLE, IN_HBM, IN_HBM, ANY],
        out_specs=WHOLE,
        scratch_shapes=[
            pltpu.VMEM((2, depth, width), jnp.bfloat16),
            pltpu.VMEM((2, rows, width), jnp.float32),
            pltpu.SemaphoreType.DMA((2, len(pieces_of(depth, STEP)))),
        ],
        compiler_params=params(18),
        cost_estimate=SMALL,
    )(start, features, in_hbm(gate_weight), in_hbm(up_weight), after)


def hidden_tail(rows, width):
    half = pl.cdiv(width // 2, 128) * 128
    return half if rows % 8 else 0


def activate_kernel(rows, width, summed, near, out):
    def pair(at):
        return summed[:, at : at + width] + near[:, at : at + width].astype(jnp.float32)

    for g in range(rows // 8):
        value = activate(pair(2 * g * width), pair((2 * g + 1) * width))
        out[:, g * width : (g + 1) * width] = value
    if rows % 8:
        last = pair((rows // 8) * 2 * width)
        value = activate(last[:4], last[4:]).astype(jnp.float32)
        half = hidden_tail(rows, width)
        right = jnp.concatenate([value[:, half:], jnp.zeros((4, 2 * half - width), jnp.float32)], axis=1)
        at = (rows // 8) * width
        out[:, at : at + half] = jnp.concatenate([value[:, :half], right], axis=0).astype(out.dtype)


def activate_packed(summed, near, rows, width):
    return pl.pallas_call(
        functools.partial(activate_kernel, rows, width),
        out_shape=jax.ShapeDtypeStruct(
            (8, (rows // 8) * width + hidden_tail(rows, width)), jnp.bfloat16
        ),
        in_specs=[WHOLE] * 2,
        out_specs=WHOLE,
        compiler_params=params(8),
        cost_estimate=SMALL,
    )(summed, near)


def down_kernel(first, rows, width, starts, *refs):
    blocks = starts.shape[0]
    hidden, refs = refs[:blocks], refs[blocks:]
    if not first:
        before, refs = refs[0], refs[1:]
    held, outs, (plain, total) = refs[0], refs[1:-2], refs[-2:]
    for b in range(blocks):
        for g in range(rows // 8):
            plain[8 * g : 8 * g + 8, :] = hidden[b][:, g * width : (g + 1) * width].astype(jnp.float32)
        if rows % 8:
            at, half = (rows // 8) * width, hidden_tail(rows, width)
            tail = hidden[b][:, at : at + half].astype(jnp.float32)
            plain[rows - 4 :, :half] = tail[:4]
            plain[rows - 4 :, half:] = tail[4:, : width - half]
        for row, tall in pieces_of(width, STEP):
            term = jnp.dot(
                plain[:, row : row + tall].astype(jnp.bfloat16),
                held[pl.ds(pl.multiple_of(starts[b] + row, 128), tall), :],
                preferred_element_type=jnp.float32,
            )
            if b == 0 and row == 0:
                total[...] = term if first else before[...] + term
            else:
                total[...] += term
    if len(outs) == 1:
        outs[0][...] = total[...]
    else:
        tall = outs[0].shape[0]
        for r, out in enumerate(outs):
            out[...] = total[r * tall : (r + 1) * tall, :].astype(out.dtype)


def down(hidden, starts, before, weight, rows, width, outs):
    columns = weight.shape[1]
    if outs == 1:
        shapes = [jax.ShapeDtypeStruct((rows, columns), jnp.float32)]
    else:
        shapes = [jax.ShapeDtypeStruct((rows // outs, columns), jnp.bfloat16)] * outs
    carried = [] if before is None else [before]
    return pl.pallas_call(
        functools.partial(down_kernel, before is None, rows, width),
        out_shape=shapes,
        in_specs=[SCALARS] + [WHOLE] * (len(hidden) + len(carried) + 1),
        out_specs=[WHOLE] * outs,
        scratch_shapes=[
            pltpu.VMEM((rows, width), jnp.float32),
            pltpu.VMEM((rows, columns), jnp.float32),
        ],
        compiler_params=params(8),
        cost_estimate=SMALL,
    )(starts, *hidden, *carried, in_vmem(weight))


def swap(value, axes, size, distance):
    return lax.ppermute(value, axes, [(i, i ^ distance) for i in range(size)])


def add(a, b):
    return a.astype(jnp.float32) + b.astype(jnp.float32)


def direct(tokens, gate_weight, up_weight, down_weight):
    n_gx = lax.axis_size("gx")
    n_token = lax.axis_size(TOKEN_AXES)
    me = lax.axis_index("gx")
    width = gate_weight.shape[1] // n_gx

    def starts_of(*distances):
        return jnp.stack([(me ^ d) * width for d in distances]).astype(jnp.int32)

    held = fetch(gate_weight, up_weight, starts_of(3), width)
    features = jnp.concatenate(
        [tokens] + [swap(tokens, TOKEN_AXES, n_token, r) for r in range(1, n_token)], axis=0
    )
    rows = features.shape[0]

    def block_for(d, after):
        return gate_up_stream(features, gate_weight, up_weight, starts_of(d), width, after)

    relayed = gate_up_held(features, held)
    arrived = swap(relayed, "gx", n_gx, 1)
    across = block_for(2, relayed)
    across = lax.optimization_barrier(add(across, arrived).astype(jnp.bfloat16))
    far = swap(across, "gx", n_gx, 2)
    beside = block_for(1, across)
    near = swap(beside, "gx", n_gx, 1)
    own = block_for(0, beside)
    summed = lax.optimization_barrier(add(own, far))
    hidden = activate_packed(summed, near, rows, width)

    first = [hidden, swap(hidden, "gx", n_gx, 1)]
    second = [swap(hidden, "gx", n_gx, d) for d in (2, 3)]
    (partial_sum,) = down(first, starts_of(0, 1), None, down_weight, rows, width, 1)
    outs = down(second, starts_of(2, 3), partial_sum, down_weight, rows, width, n_token)
    result = outs[0].astype(jnp.float32)
    for r in range(1, n_token):
        result = result + swap(outs[r], TOKEN_AXES, n_token, r).astype(jnp.float32)
    return result.astype(jnp.bfloat16)


def offloaded(tokens, gate_weight, up_weight, down_weight):
    features = lax.all_gather(tokens, TOKEN_AXES, axis=0, tiled=True)
    hidden_width = gate_weight.shape[1]
    gate_part = jnp.dot(features, gate_weight, preferred_element_type=jnp.float32)
    up_part = jnp.dot(features, up_weight, preferred_element_type=jnp.float32)
    summed = lax.psum(
        jnp.concatenate([gate_part, up_part], axis=1).astype(jnp.bfloat16), "gx"
    ).astype(jnp.float32)
    hidden = activate(summed[:, :hidden_width], summed[:, hidden_width:])
    partial_value = jnp.dot(hidden, down_weight, preferred_element_type=jnp.float32)
    return lax.psum_scatter(
        partial_value.astype(jnp.bfloat16), TOKEN_AXES, scatter_dimension=0, tiled=True
    )


def shards(tokens, gate_weight, up_weight, down_weight):
    n_gx = lax.axis_size("gx")
    n_token = lax.axis_size(TOKEN_AXES)
    rows = tokens.shape[0] * n_token
    tokens_fit = n_token > 1 and n_token & (n_token - 1) == 0 and rows % 4 == 0
    weights_fit = gate_weight.shape[1] % (128 * 4) == 0 and gate_weight.shape[0] % STEP == 0
    if n_gx == 4 and tokens_fit and weights_fit:
        return direct(tokens, gate_weight, up_weight, down_weight)
    return offloaded(tokens, gate_weight, up_weight, down_weight)


def solution(mesh):
    return jax.shard_map(
        shards,
        mesh=mesh,
        in_specs=(
            P(("grp", "gy", "gz"), "gx"),
            P("gx", ("gy", "gz")),
            P("gx", ("gy", "gz")),
            P(("gy", "gz"), "gx"),
        ),
        out_specs=P(("grp", "gy", "gz"), "gx"),
        check_vma=False,
    )
```

```python
import functools

import jax
import jax.numpy as jnp
from jax import lax
from jax.experimental import pallas as pl
from jax.experimental.pallas import tpu as pltpu
from jax.sharding import PartitionSpec as P

MIB = 1 << 20
STEP = 256
TOKEN_AXES = ("gy", "gz")
IN_HBM = pl.BlockSpec(memory_space=pltpu.HBM)
ANY = pl.BlockSpec(memory_space=pl.ANY)
WHOLE = pl.BlockSpec(memory_space=pltpu.VMEM)
SCALARS = pl.BlockSpec(memory_space=pltpu.SMEM)


def activate(gate, up):
    return (jax.nn.silu(gate) * up).astype(jnp.bfloat16)


def pieces_of(total, step):
    return [(start, min(step, total - start)) for start in range(0, total, step)]


def in_hbm(value):
    return pltpu.with_memory_space_constraint(value, pltpu.HBM)


def in_vmem(value):
    return pltpu.with_memory_space_constraint(value, pltpu.VMEM)


SMALL = pl.CostEstimate(flops=0, bytes_accessed=MIB, transcendentals=0)


def params(mib):
    return pltpu.CompilerParams(vmem_limit_bytes=mib * MIB)


def packed_pair_width(rows, width):
    return (rows // 8) * 2 * width + (width if rows % 8 else 0)


def pack_pair(out, gate, up):
    rows, width = gate.shape
    for g in range(rows // 8):
        for w, value in enumerate((gate, up)):
            at = (2 * g + w) * width
            out[:, at : at + width] = value[8 * g : 8 * g + 8].astype(out.dtype)
    if rows % 8:
        at = (rows // 8) * 2 * width
        tail = jnp.concatenate([gate[rows - 4 :], up[rows - 4 :]], axis=0)
        out[:, at : at + width] = tail.astype(out.dtype)


def start_copies(width, start_ref, gate_ref, up_ref, held, sems):
    columns = pl.ds(pl.multiple_of(start_ref[0], 128), width)
    copies = []
    for k, (row, rows) in enumerate(pieces_of(held.shape[1], STEP)):
        for w, weight in enumerate((gate_ref, up_ref)):
            copy = pltpu.make_async_copy(
                weight.at[pl.ds(row, rows), columns], held.at[w, pl.ds(row, rows)], sems.at[w, k]
            )
            copy.start()
            copies.append((w, row, rows, copy))
    return copies


def fetch_kernel(width, start_ref, gate_ref, up_ref, held, sems):
    for _, _, _, copy in start_copies(width, start_ref, gate_ref, up_ref, held, sems):
        copy.wait()


def fetch(gate_weight, up_weight, start, width):
    depth = gate_weight.shape[0]
    return pl.pallas_call(
        functools.partial(fetch_kernel, width),
        out_shape=pltpu.VMEM((2, depth, width), jnp.bfloat16),
        in_specs=[SCALARS, IN_HBM, IN_HBM],
        out_specs=WHOLE,
        scratch_shapes=[pltpu.SemaphoreType.DMA((2, len(pieces_of(depth, STEP))))],
        compiler_params=params(4),
        cost_estimate=SMALL,
    )(start, in_hbm(gate_weight), in_hbm(up_weight))


def multiply(x_ref, held, total, steps):
    for w, row, rows, copy in steps:
        if copy is not None:
            copy.wait()
        term = jnp.dot(
            x_ref[:, row : row + rows], held[w, row : row + rows, :], preferred_element_type=jnp.float32
        )
        if row == 0:
            total[w] = term
        else:
            total[w] += term


def held_kernel(x_ref, held, out, total):
    parts = pieces_of(x_ref.shape[1], STEP)
    multiply(x_ref, held, total, [(w, row, rows, None) for w in range(2) for row, rows in parts])
    pack_pair(out, total[0], total[1])


def gate_up_held(features, held):
    rows, width = features.shape[0], held.shape[2]
    return pl.pallas_call(
        held_kernel,
        out_shape=jax.ShapeDtypeStruct((8, packed_pair_width(rows, width)), jnp.bfloat16),
        in_specs=[WHOLE, WHOLE],
        out_specs=WHOLE,
        scratch_shapes=[pltpu.VMEM((2, rows, width), jnp.float32)],
        compiler_params=params(8),
        cost_estimate=SMALL,
    )(features, in_vmem(held))


def stream_kernel(width, start_ref, x_ref, gate_ref, up_ref, _, out, held, total, sems):
    copies = start_copies(width, start_ref, gate_ref, up_ref, held, sems)
    multiply(x_ref, held, total, copies)
    pack_pair(out, total[0], total[1])


def gate_up_stream(features, gate_weight, up_weight, start, width, after):
    rows, depth = features.shape
    return pl.pallas_call(
        functools.partial(stream_kernel, width),
        out_shape=jax.ShapeDtypeStruct((8, packed_pair_width(rows, width)), jnp.bfloat16),
        in_specs=[SCALARS, WHOLE, IN_HBM, IN_HBM, ANY],
        out_specs=WHOLE,
        scratch_shapes=[
            pltpu.VMEM((2, depth, width), jnp.bfloat16),
            pltpu.VMEM((2, rows, width), jnp.float32),
            pltpu.SemaphoreType.DMA((2, len(pieces_of(depth, STEP)))),
        ],
        compiler_params=params(18),
        cost_estimate=SMALL,
    )(start, features, in_hbm(gate_weight), in_hbm(up_weight), after)


def hidden_tail(rows, width):
    half = pl.cdiv(width // 2, 128) * 128
    return half if rows % 8 else 0


def activate_kernel(rows, width, summed, near, out):
    def pair(at):
        return summed[:, at : at + width] + near[:, at : at + width].astype(jnp.float32)

    for g in range(rows // 8):
        value = activate(pair(2 * g * width), pair((2 * g + 1) * width))
        out[:, g * width : (g + 1) * width] = value
    if rows % 8:
        last = pair((rows // 8) * 2 * width)
        value = activate(last[:4], last[4:]).astype(jnp.float32)
        half = hidden_tail(rows, width)
        right = jnp.concatenate([value[:, half:], jnp.zeros((4, 2 * half - width), jnp.float32)], axis=1)
        at = (rows // 8) * width
        out[:, at : at + half] = jnp.concatenate([value[:, :half], right], axis=0).astype(out.dtype)


def activate_packed(summed, near, rows, width):
    return pl.pallas_call(
        functools.partial(activate_kernel, rows, width),
        out_shape=jax.ShapeDtypeStruct(
            (8, (rows // 8) * width + hidden_tail(rows, width)), jnp.bfloat16
        ),
        in_specs=[WHOLE] * 2,
        out_specs=WHOLE,
        compiler_params=params(8),
        cost_estimate=SMALL,
    )(summed, near)


def down_kernel(first, last, rows, width, start, *refs):
    if last:
        slots, refs = refs[0], refs[1:]
    hidden, refs = refs[0], refs[1:]
    if not first:
        before, refs = refs[0], refs[1:]
    held, out, plain, total = refs
    for g in range(rows // 8):
        plain[8 * g : 8 * g + 8, :] = hidden[:, g * width : (g + 1) * width].astype(jnp.float32)
    if rows % 8:
        at, half = (rows // 8) * width, hidden_tail(rows, width)
        tail = hidden[:, at : at + half].astype(jnp.float32)
        plain[rows - 4 :, :half] = tail[:4]
        plain[rows - 4 :, half:] = tail[4:, : width - half]
    if not last:
        total = out
    for row, tall in pieces_of(width, STEP):
        term = jnp.dot(
            plain[:, row : row + tall].astype(jnp.bfloat16),
            held[pl.ds(pl.multiple_of(start[0] + row, 128), tall), :],
            preferred_element_type=jnp.float32,
        )
        if row == 0:
            total[...] = term if first else before[...] + term
        else:
            total[...] += term
    if last:
        tall = out.shape[1]
        for r in range(out.shape[0]):
            out[slots[r]] = total[r * tall : (r + 1) * tall, :].astype(out.dtype)


def down(hidden, start, before, weight, rows, width, slots):
    columns = weight.shape[1]
    scalars = [start] if slots is None else [start, slots]
    if slots is None:
        shape = jax.ShapeDtypeStruct((rows, columns), jnp.float32)
    else:
        shape = jax.ShapeDtypeStruct((slots.shape[0], rows // slots.shape[0], columns), jnp.bfloat16)
    carried = [] if before is None else [before]
    return pl.pallas_call(
        functools.partial(down_kernel, before is None, slots is not None, rows, width),
        out_shape=shape,
        in_specs=[SCALARS] * len(scalars) + [WHOLE] * (2 + len(carried)),
        out_specs=WHOLE,
        scratch_shapes=[
            pltpu.VMEM((rows, width), jnp.float32),
            pltpu.VMEM((rows, columns), jnp.float32),
        ],
        compiler_params=params(8),
        cost_estimate=SMALL,
    )(*scalars, hidden, *carried, in_vmem(weight))


def swap(value, axes, size, distance):
    return lax.ppermute(value, axes, [(i, i ^ distance) for i in range(size)])


def add(a, b):
    return a.astype(jnp.float32) + b.astype(jnp.float32)


def direct(tokens, gate_weight, up_weight, down_weight):
    n_gx = lax.axis_size("gx")
    n_token = lax.axis_size(TOKEN_AXES)
    me = lax.axis_index("gx")
    width = gate_weight.shape[1] // n_gx

    def starts_of(*distances):
        return jnp.stack([(me ^ d) * width for d in distances]).astype(jnp.int32)

    held = fetch(gate_weight, up_weight, starts_of(3), width)
    features = jnp.concatenate(
        [tokens] + [swap(tokens, TOKEN_AXES, n_token, r) for r in range(1, n_token)], axis=0
    )
    rows = features.shape[0]

    def block_for(d, after):
        return gate_up_stream(features, gate_weight, up_weight, starts_of(d), width, after)

    relayed = gate_up_held(features, held)
    arrived = swap(relayed, "gx", n_gx, 1)
    across = block_for(2, relayed)
    across = lax.optimization_barrier(add(across, arrived).astype(jnp.bfloat16))
    far = swap(across, "gx", n_gx, 2)
    beside = block_for(1, across)
    near = swap(beside, "gx", n_gx, 1)
    own = block_for(0, beside)
    summed = lax.optimization_barrier(add(own, far))
    hidden = activate_packed(summed, near, rows, width)

    total = None
    for d in range(n_gx - 1):
        block = swap(hidden, "gx", n_gx, d) if d else hidden
        total = down(block, starts_of(d), total, down_weight, rows, width, None)
    block = swap(hidden, "gx", n_gx, n_gx - 1)
    token_me = lax.axis_index(TOKEN_AXES)
    slots = jnp.stack([token_me ^ r for r in range(n_token)]).astype(jnp.int32)
    terms = down(block, starts_of(n_gx - 1), total, down_weight, rows, width, slots)
    terms = lax.all_to_all(terms, TOKEN_AXES, 0, 0, tiled=True)
    result = terms[0].astype(jnp.float32)
    for r in range(1, n_token):
        result = result + terms[r].astype(jnp.float32)
    return result.astype(jnp.bfloat16)


def offloaded(tokens, gate_weight, up_weight, down_weight):
    features = lax.all_gather(tokens, TOKEN_AXES, axis=0, tiled=True)
    hidden_width = gate_weight.shape[1]
    gate_part = jnp.dot(features, gate_weight, preferred_element_type=jnp.float32)
    up_part = jnp.dot(features, up_weight, preferred_element_type=jnp.float32)
    summed = lax.psum(
        jnp.concatenate([gate_part, up_part], axis=1).astype(jnp.bfloat16), "gx"
    ).astype(jnp.float32)
    hidden = activate(summed[:, :hidden_width], summed[:, hidden_width:])
    partial_value = jnp.dot(hidden, down_weight, preferred_element_type=jnp.float32)
    return lax.psum_scatter(
        partial_value.astype(jnp.bfloat16), TOKEN_AXES, scatter_dimension=0, tiled=True
    )


def shards(tokens, gate_weight, up_weight, down_weight):
    n_gx = lax.axis_size("gx")
    n_token = lax.axis_size(TOKEN_AXES)
    rows = tokens.shape[0] * n_token
    tokens_fit = n_token > 1 and n_token & (n_token - 1) == 0 and rows % 4 == 0
    weights_fit = gate_weight.shape[1] % (128 * 4) == 0 and gate_weight.shape[0] % STEP == 0
    if n_gx == 4 and tokens_fit and weights_fit:
        return direct(tokens, gate_weight, up_weight, down_weight)
    return offloaded(tokens, gate_weight, up_weight, down_weight)


def solution(mesh):
    return jax.shard_map(
        shards,
        mesh=mesh,
        in_specs=(
            P(("grp", "gy", "gz"), "gx"),
            P("gx", ("gy", "gz")),
            P("gx", ("gy", "gz")),
            P(("gy", "gz"), "gx"),
        ),
        out_specs=P(("grp", "gy", "gz"), "gx"),
        check_vma=False,
    )
```

```python
import functools

import jax
import jax.numpy as jnp
from jax import lax
from jax.experimental import pallas as pl
from jax.experimental.pallas import tpu as pltpu
from jax.sharding import PartitionSpec as P

MIB = 1 << 20
STEP = 256
TOKEN_AXES = ("gy", "gz")
IN_HBM = pl.BlockSpec(memory_space=pltpu.HBM)
ANY = pl.BlockSpec(memory_space=pl.ANY)
WHOLE = pl.BlockSpec(memory_space=pltpu.VMEM)
SCALARS = pl.BlockSpec(memory_space=pltpu.SMEM)


def activate(gate, up):
    return (jax.nn.silu(gate) * up).astype(jnp.bfloat16)


def pieces_of(total, step):
    return [(start, min(step, total - start)) for start in range(0, total, step)]


def in_hbm(value):
    return pltpu.with_memory_space_constraint(value, pltpu.HBM)


def in_vmem(value):
    return pltpu.with_memory_space_constraint(value, pltpu.VMEM)


SMALL = pl.CostEstimate(flops=0, bytes_accessed=MIB, transcendentals=0)


def params(mib):
    return pltpu.CompilerParams(vmem_limit_bytes=mib * MIB)


def packed_pair_width(rows, width):
    return (rows // 8) * 2 * width + (width if rows % 8 else 0)


def pack_pair(out, gate, up):
    rows, width = gate.shape
    for g in range(rows // 8):
        for w, value in enumerate((gate, up)):
            at = (2 * g + w) * width
            out[:, at : at + width] = value[8 * g : 8 * g + 8].astype(out.dtype)
    if rows % 8:
        at = (rows // 8) * 2 * width
        tail = jnp.concatenate([gate[rows - 4 :], up[rows - 4 :]], axis=0)
        out[:, at : at + width] = tail.astype(out.dtype)


def start_copies(width, start_ref, gate_ref, up_ref, held, sems):
    columns = pl.ds(pl.multiple_of(start_ref[0], 128), width)
    copies = []
    for k, (row, rows) in enumerate(pieces_of(held.shape[1], STEP)):
        for w, weight in enumerate((gate_ref, up_ref)):
            copy = pltpu.make_async_copy(
                weight.at[pl.ds(row, rows), columns], held.at[w, pl.ds(row, rows)], sems.at[w, k]
            )
            copy.start()
            copies.append((w, row, rows, copy))
    return copies


def fetch_kernel(width, start_ref, gate_ref, up_ref, held, sems):
    for _, _, _, copy in start_copies(width, start_ref, gate_ref, up_ref, held, sems):
        copy.wait()


def fetch(gate_weight, up_weight, start, width):
    depth = gate_weight.shape[0]
    return pl.pallas_call(
        functools.partial(fetch_kernel, width),
        out_shape=pltpu.VMEM((2, depth, width), jnp.bfloat16),
        in_specs=[SCALARS, IN_HBM, IN_HBM],
        out_specs=WHOLE,
        scratch_shapes=[pltpu.SemaphoreType.DMA((2, len(pieces_of(depth, STEP))))],
        compiler_params=params(4),
        cost_estimate=SMALL,
    )(start, in_hbm(gate_weight), in_hbm(up_weight))


def multiply(x_ref, held, total, steps):
    for w, row, rows, copy in steps:
        if copy is not None:
            copy.wait()
        term = jnp.dot(
            x_ref[:, row : row + rows], held[w, row : row + rows, :], preferred_element_type=jnp.float32
        )
        if row == 0:
            total[w] = term
        else:
            total[w] += term


def held_kernel(x_ref, held, out, total):
    parts = pieces_of(x_ref.shape[1], STEP)
    multiply(x_ref, held, total, [(w, row, rows, None) for w in range(2) for row, rows in parts])
    pack_pair(out, total[0], total[1])


def gate_up_held(features, held):
    rows, width = features.shape[0], held.shape[2]
    return pl.pallas_call(
        held_kernel,
        out_shape=jax.ShapeDtypeStruct((8, packed_pair_width(rows, width)), jnp.bfloat16),
        in_specs=[WHOLE, WHOLE],
        out_specs=WHOLE,
        scratch_shapes=[pltpu.VMEM((2, rows, width), jnp.float32)],
        compiler_params=params(8),
        cost_estimate=SMALL,
    )(features, in_vmem(held))


def stream_kernel(width, start_ref, x_ref, gate_ref, up_ref, _, out, held, total, sems):
    copies = start_copies(width, start_ref, gate_ref, up_ref, held, sems)
    multiply(x_ref, held, total, copies)
    pack_pair(out, total[0], total[1])


def gate_up_stream(features, gate_weight, up_weight, start, width, after):
    rows, depth = features.shape
    return pl.pallas_call(
        functools.partial(stream_kernel, width),
        out_shape=jax.ShapeDtypeStruct((8, packed_pair_width(rows, width)), jnp.bfloat16),
        in_specs=[SCALARS, WHOLE, IN_HBM, IN_HBM, ANY],
        out_specs=WHOLE,
        scratch_shapes=[
            pltpu.VMEM((2, depth, width), jnp.bfloat16),
            pltpu.VMEM((2, rows, width), jnp.float32),
            pltpu.SemaphoreType.DMA((2, len(pieces_of(depth, STEP)))),
        ],
        compiler_params=params(18),
        cost_estimate=SMALL,
    )(start, features, in_hbm(gate_weight), in_hbm(up_weight), after)


def hidden_tail(rows, width):
    half = pl.cdiv(width // 2, 128) * 128
    return half if rows % 8 else 0


def activate_kernel(rows, width, summed, near, out):
    def pair(at):
        return summed[:, at : at + width] + near[:, at : at + width].astype(jnp.float32)

    for g in range(rows // 8):
        value = activate(pair(2 * g * width), pair((2 * g + 1) * width))
        out[:, g * width : (g + 1) * width] = value
    if rows % 8:
        last = pair((rows // 8) * 2 * width)
        value = activate(last[:4], last[4:]).astype(jnp.float32)
        half = hidden_tail(rows, width)
        right = jnp.concatenate([value[:, half:], jnp.zeros((4, 2 * half - width), jnp.float32)], axis=1)
        at = (rows // 8) * width
        out[:, at : at + half] = jnp.concatenate([value[:, :half], right], axis=0).astype(out.dtype)


def activate_packed(summed, near, rows, width):
    return pl.pallas_call(
        functools.partial(activate_kernel, rows, width),
        out_shape=jax.ShapeDtypeStruct(
            (8, (rows // 8) * width + hidden_tail(rows, width)), jnp.bfloat16
        ),
        in_specs=[WHOLE] * 2,
        out_specs=WHOLE,
        compiler_params=params(8),
        cost_estimate=SMALL,
    )(summed, near)


def pack_rows(out, value):
    rows, width = value.shape
    for g in range(rows // 8):
        out[:, g * width : (g + 1) * width] = value[8 * g : 8 * g + 8].astype(out.dtype)
    piece = width // 8
    for r in range(rows // 8 * 8, rows):
        at = (rows // 8) * width + (r % 8) * piece
        row = jnp.concatenate(
            [value[r : r + 1, i * piece : (i + 1) * piece] for i in range(8)], axis=0
        )
        out[:, at : at + piece] = row.astype(out.dtype)


def unpack_rows(out, packed):
    rows, width = out.shape
    for g in range(rows // 8):
        out[8 * g : 8 * g + 8, :] = packed[:, g * width : (g + 1) * width]
    piece = width // 8
    for r in range(rows // 8 * 8, rows):
        at = (rows // 8) * width + (r % 8) * piece
        for i in range(8):
            out[r : r + 1, i * piece : (i + 1) * piece] = packed[i : i + 1, at : at + piece]


def down_kernel(first, rows, width, starts, *refs):
    blocks = starts.shape[0]
    hidden, refs = refs[:blocks], refs[blocks:]
    if not first:
        before, refs = refs[0], refs[1:]
    held, outs, (plain, total) = refs[0], refs[1:-2], refs[-2:]
    if first:
        total = outs[0]
    for b in range(blocks):
        for g in range(rows // 8):
            plain[8 * g : 8 * g + 8, :] = hidden[b][:, g * width : (g + 1) * width].astype(jnp.float32)
        if rows % 8:
            at, half = (rows // 8) * width, hidden_tail(rows, width)
            tail = hidden[b][:, at : at + half].astype(jnp.float32)
            plain[rows - 4 :, :half] = tail[:4]
            plain[rows - 4 :, half:] = tail[4:, : width - half]
        for row, tall in pieces_of(width, STEP):
            term = jnp.dot(
                plain[:, row : row + tall].astype(jnp.bfloat16),
                held[pl.ds(pl.multiple_of(starts[b] + row, 128), tall), :],
                preferred_element_type=jnp.float32,
            )
            if b == 0 and row == 0:
                total[...] = term if first else before[...] + term
            else:
                total[...] += term
    if not first:
        tall = rows // len(outs)
        for r, out in enumerate(outs):
            pack_rows(out, total[r * tall : (r + 1) * tall, :])


def down(hidden, starts, before, weight, rows, width, outs):
    columns = weight.shape[1]
    if before is None:
        shapes = [jax.ShapeDtypeStruct((rows, columns), jnp.float32)]
    else:
        packed = (8, rows // outs * columns // 8)
        shapes = [jax.ShapeDtypeStruct(packed, jnp.bfloat16 if r else jnp.float32) for r in range(outs)]
    carried = [] if before is None else [before]
    return pl.pallas_call(
        functools.partial(down_kernel, before is None, rows, width),
        out_shape=shapes,
        in_specs=[SCALARS] + [WHOLE] * (len(hidden) + len(carried) + 1),
        out_specs=[WHOLE] * len(shapes),
        scratch_shapes=[
            pltpu.VMEM((rows, width), jnp.float32),
            pltpu.VMEM((rows, columns), jnp.float32),
        ],
        compiler_params=params(8),
        cost_estimate=SMALL,
    )(starts, *hidden, *carried, in_vmem(weight))


def finish_kernel(*refs):
    terms, out, plain = refs[:-2], refs[-2], refs[-1]
    packed = terms[0][...]
    for term in terms[1:]:
        packed = packed + term[...].astype(jnp.float32)
    unpack_rows(plain, packed)
    out[...] = plain[...].astype(out.dtype)


def finish(terms, shape):
    return pl.pallas_call(
        finish_kernel,
        out_shape=jax.ShapeDtypeStruct(shape, jnp.bfloat16),
        in_specs=[WHOLE] * len(terms),
        out_specs=WHOLE,
        scratch_shapes=[pltpu.VMEM(shape, jnp.float32)],
        compiler_params=params(4),
        cost_estimate=SMALL,
    )(*terms)


def swap(value, axes, size, distance):
    return lax.ppermute(value, axes, [(i, i ^ distance) for i in range(size)])


def add(a, b):
    return a.astype(jnp.float32) + b.astype(jnp.float32)


def direct(tokens, gate_weight, up_weight, down_weight):
    n_gx = lax.axis_size("gx")
    n_token = lax.axis_size(TOKEN_AXES)
    me = lax.axis_index("gx")
    width = gate_weight.shape[1] // n_gx

    def starts_of(*distances):
        return jnp.stack([(me ^ d) * width for d in distances]).astype(jnp.int32)

    held = fetch(gate_weight, up_weight, starts_of(3), width)
    features = jnp.concatenate(
        [tokens] + [swap(tokens, TOKEN_AXES, n_token, r) for r in range(1, n_token)], axis=0
    )
    rows = features.shape[0]

    def block_for(d, after):
        return gate_up_stream(features, gate_weight, up_weight, starts_of(d), width, after)

    relayed = gate_up_held(features, held)
    arrived = swap(relayed, "gx", n_gx, 1)
    across = block_for(2, relayed)
    across = lax.optimization_barrier(add(across, arrived).astype(jnp.bfloat16))
    far = swap(across, "gx", n_gx, 2)
    beside = block_for(1, across)
    near = swap(beside, "gx", n_gx, 1)
    own = block_for(0, beside)
    summed = lax.optimization_barrier(add(own, far))
    hidden = activate_packed(summed, near, rows, width)

    opposite = swap(hidden, "gx", n_gx, 2)
    first = [hidden, swap(hidden, "gx", n_gx, 1), opposite]
    second = [swap(opposite, "gx", n_gx, 1)]
    (partial_sum,) = down(first, starts_of(0, 1, 2), None, down_weight, rows, width, 1)
    outs = down(second, starts_of(3), partial_sum, down_weight, rows, width, n_token)
    terms = [outs[0]] + [swap(outs[r], TOKEN_AXES, n_token, r) for r in range(1, n_token)]
    return finish(terms, tokens.shape)


def offloaded(tokens, gate_weight, up_weight, down_weight):
    features = lax.all_gather(tokens, TOKEN_AXES, axis=0, tiled=True)
    hidden_width = gate_weight.shape[1]
    gate_part = jnp.dot(features, gate_weight, preferred_element_type=jnp.float32)
    up_part = jnp.dot(features, up_weight, preferred_element_type=jnp.float32)
    summed = lax.psum(
        jnp.concatenate([gate_part, up_part], axis=1).astype(jnp.bfloat16), "gx"
    ).astype(jnp.float32)
    hidden = activate(summed[:, :hidden_width], summed[:, hidden_width:])
    partial_value = jnp.dot(hidden, down_weight, preferred_element_type=jnp.float32)
    return lax.psum_scatter(
        partial_value.astype(jnp.bfloat16), TOKEN_AXES, scatter_dimension=0, tiled=True
    )


def shards(tokens, gate_weight, up_weight, down_weight):
    n_gx = lax.axis_size("gx")
    n_token = lax.axis_size(TOKEN_AXES)
    rows = tokens.shape[0] * n_token
    tokens_fit = n_token > 1 and n_token & (n_token - 1) == 0 and rows % 4 == 0
    weights_fit = gate_weight.shape[1] % (128 * 4) == 0 and gate_weight.shape[0] % STEP == 0
    columns_fit = down_weight.shape[1] % (128 * 8) == 0
    if n_gx == 4 and tokens_fit and weights_fit and columns_fit:
        return direct(tokens, gate_weight, up_weight, down_weight)
    return offloaded(tokens, gate_weight, up_weight, down_weight)


def solution(mesh):
    return jax.shard_map(
        shards,
        mesh=mesh,
        in_specs=(
            P(("grp", "gy", "gz"), "gx"),
            P("gx", ("gy", "gz")),
            P("gx", ("gy", "gz")),
            P(("gy", "gz"), "gx"),
        ),
        out_specs=P(("grp", "gy", "gz"), "gx"),
        check_vma=False,
    )
```

```python
import functools

import jax
import jax.numpy as jnp
from jax import lax
from jax.experimental import pallas as pl
from jax.experimental.pallas import tpu as pltpu
from jax.sharding import PartitionSpec as P

MIB = 1 << 20
STEP = 256
TOKEN_AXES = ("gy", "gz")
IN_HBM = pl.BlockSpec(memory_space=pltpu.HBM)
ANY = pl.BlockSpec(memory_space=pl.ANY)
WHOLE = pl.BlockSpec(memory_space=pltpu.VMEM)
SCALARS = pl.BlockSpec(memory_space=pltpu.SMEM)


def activate(gate, up):
    return (jax.nn.silu(gate) * up).astype(jnp.bfloat16)


def pieces_of(total, step):
    return [(start, min(step, total - start)) for start in range(0, total, step)]


def in_hbm(value):
    return pltpu.with_memory_space_constraint(value, pltpu.HBM)


def in_vmem(value):
    return pltpu.with_memory_space_constraint(value, pltpu.VMEM)


SMALL = pl.CostEstimate(flops=0, bytes_accessed=MIB, transcendentals=0)


def params(mib):
    return pltpu.CompilerParams(vmem_limit_bytes=mib * MIB)


def packed_pair_width(rows, width):
    return (rows // 8) * 2 * width + (width if rows % 8 else 0)


def pack_one(out, value, w):
    rows, width = value.shape
    for g in range(rows // 8):
        at = (2 * g + w) * width
        out[:, at : at + width] = value[8 * g : 8 * g + 8].astype(out.dtype)


def pack_last(out, gate, up):
    rows, width = gate.shape
    if rows % 8:
        at = (rows // 8) * 2 * width
        tail = jnp.concatenate([gate[rows - 4 :], up[rows - 4 :]], axis=0)
        out[:, at : at + width] = tail.astype(out.dtype)


def start_copies(width, start, first, weights, held, sems):
    columns = pl.ds(pl.multiple_of(start, 128), width)
    copies = []
    for w, weight in enumerate(weights):
        for k, (row, rows) in enumerate(pieces_of(held.shape[1], STEP)):
            copy = pltpu.make_async_copy(
                weight.at[pl.ds(first + row, rows), columns],
                held.at[w, pl.ds(row, rows)],
                sems.at[w, k],
            )
            copy.start()
            copies.append((w, row, rows, copy))
    return copies


def fetch_kernel(width, start_ref, gate_ref, up_ref, held, sems):
    for _, _, _, copy in start_copies(width, start_ref[0], 0, (gate_ref, up_ref), held, sems):
        copy.wait()


def fetch(weights, start, depth, width):
    return pl.pallas_call(
        functools.partial(fetch_kernel, width),
        out_shape=pltpu.VMEM((2, depth, width), jnp.bfloat16),
        in_specs=[SCALARS, IN_HBM, IN_HBM],
        out_specs=WHOLE,
        scratch_shapes=[pltpu.SemaphoreType.DMA((2, len(pieces_of(depth, STEP))))],
        compiler_params=params(4),
        cost_estimate=SMALL,
    )(start, *[in_hbm(w) for w in weights])


def block_kernel(width, ahead, has_held, has_partial, starts, x_ref, *refs):
    refs = list(refs)
    held = refs.pop(0) if has_held else None
    partial = refs.pop(0) if has_partial else None
    weights = refs[:2]
    refs = refs[3:]
    out = refs.pop(0)
    next_total = refs.pop(0) if ahead else None
    stream, total, sems = refs[:3]
    first = x_ref.shape[1] - stream.shape[1]
    copies = start_copies(width, starts[0], first, weights, stream, sems)
    if ahead:
        next_stream, next_sems = refs[3:]
        next_copies = start_copies(width, starts[1], 0, weights, next_stream, next_sems)

    def product(row, rows, weight):
        return jnp.dot(x_ref[:, row : row + rows], weight, preferred_element_type=jnp.float32)

    for w in range(2):
        if has_held:
            for row, rows in pieces_of(first, STEP):
                term = product(row, rows, held[w, row : row + rows, :])
                total[w] = total[w] + term if row else term
        if has_partial:
            total[w] = partial[w]
    for w, row, rows, copy in copies:
        copy.wait()
        term = product(first + row, rows, stream[w, row : row + rows, :])
        total[w] = total[w] + term if first + row else term
        if row + rows == stream.shape[1]:
            pack_one(out, total[w], w)
    pack_last(out, total[0], total[1])
    if ahead:
        for w, row, rows, copy in next_copies:
            copy.wait()
            term = product(row, rows, next_stream[w, row : row + rows, :])
            next_total[w] = next_total[w] + term if row else term


def gate_up(features, weights, starts, width, after, held=None, partial=None, summed=0, ahead=0):
    rows, depth = features.shape
    below = depth - (held.shape[1] if held is not None else summed)
    out_shape = [jax.ShapeDtypeStruct((8, packed_pair_width(rows, width)), jnp.bfloat16)]
    scratch = [
        pltpu.VMEM((2, below, width), jnp.bfloat16),
        pltpu.VMEM((2, rows, width), jnp.float32),
        pltpu.SemaphoreType.DMA((2, len(pieces_of(below, STEP)))),
    ]
    if ahead:
        out_shape.append(jax.ShapeDtypeStruct((2, rows, width), jnp.float32))
        scratch += [
            pltpu.VMEM((2, ahead, width), jnp.bfloat16),
            pltpu.SemaphoreType.DMA((2, len(pieces_of(ahead, STEP)))),
        ]
    before = [] if held is None else [in_vmem(held)]
    before += [] if partial is None else [partial]
    mib = 4 + -(-(below + ahead) * width * 4 // MIB)
    return pl.pallas_call(
        functools.partial(block_kernel, width, ahead, held is not None, partial is not None),
        out_shape=out_shape,
        in_specs=[SCALARS, WHOLE] + [WHOLE] * len(before) + [IN_HBM, IN_HBM, ANY],
        out_specs=[WHOLE] * len(out_shape),
        scratch_shapes=scratch,
        compiler_params=params(mib),
        cost_estimate=SMALL,
    )(starts, features, *before, *[in_hbm(w) for w in weights], after)


def hidden_tail(rows, width):
    half = pl.cdiv(width // 2, 128) * 128
    return half if rows % 8 else 0


def packed_hidden_shape(rows, width):
    return (8, (rows // 8) * width + hidden_tail(rows, width))


def pack_hidden_last(out, value, rows):
    width = value.shape[1]
    half = hidden_tail(rows, width)
    right = value[:, half:]
    if 2 * half > width:
        right = jnp.concatenate([right, jnp.zeros((4, 2 * half - width), jnp.float32)], axis=1)
    at = (rows // 8) * width
    out[:, at : at + half] = jnp.concatenate([value[:, :half], right], axis=0).astype(out.dtype)


def unpack_hidden(plain, hidden, column, width):
    rows = plain.shape[0]
    for g in range(rows // 8):
        value = hidden[:, g * width : (g + 1) * width].astype(jnp.float32)
        plain[8 * g : 8 * g + 8, column : column + width] = value
    if rows % 8:
        at, half = (rows // 8) * width, hidden_tail(rows, width)
        tail = hidden[:, at : at + half].astype(jnp.float32)
        plain[rows - 4 :, column : column + half] = tail[:4]
        plain[rows - 4 :, column + half : column + width] = tail[4:, : width - half]


def activate_kernel(rows, cuts, summed, near, *outs):
    width = cuts[-1]
    parts = [(0, width)] + list(zip(cuts[:-1], cuts[1:]))

    def pair(at):
        return summed[:, at : at + width] + near[:, at : at + width].astype(jnp.float32)

    for g in range(rows // 8):
        value = activate(pair(2 * g * width), pair((2 * g + 1) * width))
        for out, (left, right) in zip(outs, parts):
            wide = right - left
            out[:, g * wide : (g + 1) * wide] = value[:, left:right]
    if rows % 8:
        last = pair((rows // 8) * 2 * width)
        value = activate(last[:4], last[4:]).astype(jnp.float32)
        for out, (left, right) in zip(outs, parts):
            pack_hidden_last(out, value[:, left:right], rows)


def activate_packed(summed, near, rows, cuts):
    widths = [cuts[-1]] + [right - left for left, right in zip(cuts[:-1], cuts[1:])]
    return pl.pallas_call(
        functools.partial(activate_kernel, rows, cuts),
        out_shape=[jax.ShapeDtypeStruct(packed_hidden_shape(rows, w), jnp.bfloat16) for w in widths],
        in_specs=[WHOLE] * 2,
        out_specs=[WHOLE] * len(widths),
        compiler_params=params(8),
        cost_estimate=SMALL,
    )(summed, near)


def pack_rows(out, value):
    rows, width = value.shape
    for g in range(rows // 8):
        out[:, g * width : (g + 1) * width] = value[8 * g : 8 * g + 8].astype(out.dtype)
    piece = width // 8
    for r in range(rows // 8 * 8, rows):
        at = (rows // 8) * width + (r % 8) * piece
        row = jnp.concatenate(
            [value[r : r + 1, i * piece : (i + 1) * piece] for i in range(8)], axis=0
        )
        out[:, at : at + piece] = row.astype(out.dtype)


def unpack_rows(out, packed):
    rows, width = out.shape
    for g in range(rows // 8):
        out[8 * g : 8 * g + 8, :] = packed[:, g * width : (g + 1) * width]
    piece = width // 8
    for r in range(rows // 8 * 8, rows):
        at = (rows // 8) * width + (r % 8) * piece
        for i in range(8):
            out[r : r + 1, i * piece : (i + 1) * piece] = packed[i : i + 1, at : at + piece]


def down_kernel(layout, first, last, starts, *refs):
    refs = list(refs)
    hidden = [[refs.pop(0) for _ in widths] for widths in layout]
    before = None if first else refs.pop(0)
    held, outs, (plain, total) = refs[0], refs[1:-2], refs[-2:]
    if not last:
        total = outs[0]
    width = plain.shape[1]
    for b, widths in enumerate(layout):
        column = 0
        for part, wide in zip(hidden[b], widths):
            unpack_hidden(plain, part, column, wide)
            column += wide
        for row, tall in pieces_of(width, STEP):
            term = jnp.dot(
                plain[:, row : row + tall].astype(jnp.bfloat16),
                held[pl.ds(pl.multiple_of(starts[b] + row, 128), tall), :],
                preferred_element_type=jnp.float32,
            )
            if b == 0 and row == 0:
                total[...] = term if first else before[...] + term
            else:
                total[...] += term
    if last:
        tall = plain.shape[0] // len(outs)
        for r, out in enumerate(outs):
            pack_rows(out, total[r * tall : (r + 1) * tall, :])


def down(hidden, layout, starts, before, weight, rows, outs):
    columns = weight.shape[1]
    if outs == 1:
        shapes = [jax.ShapeDtypeStruct((rows, columns), jnp.float32)]
    else:
        packed = (8, rows // outs * columns // 8)
        shapes = [jax.ShapeDtypeStruct(packed, jnp.bfloat16 if r else jnp.float32) for r in range(outs)]
    arrays = [part for parts in hidden for part in parts]
    arrays += [] if before is None else [before]
    return pl.pallas_call(
        functools.partial(down_kernel, layout, before is None, outs > 1),
        out_shape=shapes,
        in_specs=[SCALARS] + [WHOLE] * (len(arrays) + 1),
        out_specs=[WHOLE] * len(shapes),
        scratch_shapes=[
            pltpu.VMEM((rows, sum(layout[0])), jnp.float32),
            pltpu.VMEM((rows, columns), jnp.float32),
        ],
        compiler_params=params(8),
        cost_estimate=SMALL,
    )(starts, *arrays, in_vmem(weight))


def finish_kernel(*refs):
    terms, out, plain = refs[:-2], refs[-2], refs[-1]
    packed = terms[0][...]
    for term in terms[1:]:
        packed = packed + term[...].astype(jnp.float32)
    unpack_rows(plain, packed)
    out[...] = plain[...].astype(out.dtype)


def finish(terms, shape):
    return pl.pallas_call(
        finish_kernel,
        out_shape=jax.ShapeDtypeStruct(shape, jnp.bfloat16),
        in_specs=[WHOLE] * len(terms),
        out_specs=WHOLE,
        scratch_shapes=[pltpu.VMEM(shape, jnp.float32)],
        compiler_params=params(4),
        cost_estimate=SMALL,
    )(*terms)


def swap(value, axes, size, distance):
    return lax.ppermute(value, axes, [(i, i ^ distance) for i in range(size)])


def add(a, b):
    return a.astype(jnp.float32) + b.astype(jnp.float32)


def direct(tokens, gate_weight, up_weight, down_weight):
    n_gx = lax.axis_size("gx")
    n_token = lax.axis_size(TOKEN_AXES)
    me = lax.axis_index("gx")
    width = gate_weight.shape[1] // n_gx

    def starts_of(*distances):
        return jnp.stack([(me ^ d) * width for d in distances]).astype(jnp.int32)

    weights = (gate_weight, up_weight)
    early = gate_weight.shape[0] // STEP * 3 // 4 * STEP
    ahead = gate_weight.shape[0] // STEP // 4 * STEP
    held = fetch(weights, starts_of(3), early, width)
    features = jnp.concatenate(
        [tokens] + [swap(tokens, TOKEN_AXES, n_token, r) for r in range(1, n_token)], axis=0
    )
    rows = features.shape[0]

    (relayed,) = gate_up(features, weights, starts_of(3), width, features, held=held)
    arrived = swap(relayed, "gx", n_gx, 1)
    across, partial = gate_up(features, weights, starts_of(2, 1), width, relayed, ahead=ahead)
    across = lax.optimization_barrier(add(across, arrived).astype(jnp.bfloat16))
    far = swap(across, "gx", n_gx, 2)
    (beside,) = gate_up(
        features, weights, starts_of(1), width, across, partial=partial, summed=ahead
    )
    near = swap(beside, "gx", n_gx, 1)
    (own,) = gate_up(features, weights, starts_of(0), width, beside)
    summed = lax.optimization_barrier(add(own, far))

    middle = (width // 128 + 1) // 2 * 128
    whole, halves = (width,), (middle, width - middle)
    hidden, *parts = activate_packed(summed, near, rows, (0, middle, width))
    opposite = [swap(part, "gx", n_gx, 2) for part in parts]
    beside = swap(hidden, "gx", n_gx, 1)
    (total,) = down(
        [[hidden], [beside]], [whole, whole], starts_of(0, 1), None, down_weight, rows, 1
    )
    diagonal = []
    for i, part in enumerate(opposite):
        opposite[i], total = lax.optimization_barrier((part, total))
        diagonal.append(swap(opposite[i], "gx", n_gx, 1))
    (total,) = down([opposite], [halves], starts_of(2), total, down_weight, rows, 1)
    outs = down([diagonal], [halves], starts_of(3), total, down_weight, rows, n_token)
    terms = [outs[0]] + [swap(outs[r], TOKEN_AXES, n_token, r) for r in range(1, n_token)]
    return finish(terms, tokens.shape)


def offloaded(tokens, gate_weight, up_weight, down_weight):
    features = lax.all_gather(tokens, TOKEN_AXES, axis=0, tiled=True)
    hidden_width = gate_weight.shape[1]
    gate_part = jnp.dot(features, gate_weight, preferred_element_type=jnp.float32)
    up_part = jnp.dot(features, up_weight, preferred_element_type=jnp.float32)
    summed = lax.psum(
        jnp.concatenate([gate_part, up_part], axis=1).astype(jnp.bfloat16), "gx"
    ).astype(jnp.float32)
    hidden = activate(summed[:, :hidden_width], summed[:, hidden_width:])
    partial_value = jnp.dot(hidden, down_weight, preferred_element_type=jnp.float32)
    return lax.psum_scatter(
        partial_value.astype(jnp.bfloat16), TOKEN_AXES, scatter_dimension=0, tiled=True
    )


def shards(tokens, gate_weight, up_weight, down_weight):
    n_gx = lax.axis_size("gx")
    n_token = lax.axis_size(TOKEN_AXES)
    rows = tokens.shape[0] * n_token
    tokens_fit = n_token > 1 and n_token & (n_token - 1) == 0 and rows % 4 == 0
    weights_fit = gate_weight.shape[1] % (128 * 4) == 0 and gate_weight.shape[0] % (4 * STEP) == 0
    columns_fit = down_weight.shape[1] % (128 * 8) == 0
    if n_gx == 4 and tokens_fit and weights_fit and columns_fit:
        return direct(tokens, gate_weight, up_weight, down_weight)
    return offloaded(tokens, gate_weight, up_weight, down_weight)


def solution(mesh):
    return jax.shard_map(
        shards,
        mesh=mesh,
        in_specs=(
            P(("grp", "gy", "gz"), "gx"),
            P("gx", ("gy", "gz")),
            P("gx", ("gy", "gz")),
            P(("gy", "gz"), "gx"),
        ),
        out_specs=P(("grp", "gy", "gz"), "gx"),
        check_vma=False,
    )
```

```python
import functools

import jax
import jax.numpy as jnp
from jax import lax
from jax.experimental import pallas as pl
from jax.experimental.pallas import tpu as pltpu
from jax.sharding import PartitionSpec as P

MIB = 1 << 20
STEP = 256
IN_FLIGHT = 5
TOKEN_AXES = ("gy", "gz")
IN_HBM = pl.BlockSpec(memory_space=pltpu.HBM)
ANY = pl.BlockSpec(memory_space=pl.ANY)
WHOLE = pl.BlockSpec(memory_space=pltpu.VMEM)
SCALARS = pl.BlockSpec(memory_space=pltpu.SMEM)


def activate(gate, up):
    return (jax.nn.silu(gate) * up).astype(jnp.bfloat16)


def pieces_of(total, step):
    return [(start, min(step, total - start)) for start in range(0, total, step)]


def in_hbm(value):
    return pltpu.with_memory_space_constraint(value, pltpu.HBM)


def in_vmem(value):
    return pltpu.with_memory_space_constraint(value, pltpu.VMEM)


SMALL = pl.CostEstimate(flops=0, bytes_accessed=MIB, transcendentals=0)


def params(mib):
    return pltpu.CompilerParams(vmem_limit_bytes=mib * MIB)


def packed_pair_width(rows, width):
    return (rows // 8) * 2 * width + (width if rows % 8 else 0)


def pack_pair(out, gate, up):
    rows, width = gate.shape
    for g in range(rows // 8):
        for w, value in enumerate((gate, up)):
            at = (2 * g + w) * width
            out[:, at : at + width] = value[8 * g : 8 * g + 8].astype(out.dtype)
    if rows % 8:
        at = (rows // 8) * 2 * width
        tail = jnp.concatenate([gate[rows - 4 :], up[rows - 4 :]], axis=0)
        out[:, at : at + width] = tail.astype(out.dtype)


def block_copies(width, first, start_ref, gate_ref, up_ref, held, sems):
    columns = pl.ds(pl.multiple_of(start_ref[0], 128), width)
    copies = []
    for k, (row, rows) in enumerate(pieces_of(held.shape[1], STEP)):
        for w, weight in enumerate((gate_ref, up_ref)):
            copy = pltpu.make_async_copy(
                weight.at[pl.ds(first + row, rows), columns],
                held.at[w, pl.ds(row, rows)],
                sems.at[w, k],
            )
            copies.append((w, row, rows, copy))
    return copies


def fetch_kernel(width, start_ref, gate_ref, up_ref, held, sems):
    copies = block_copies(width, 0, start_ref, gate_ref, up_ref, held, sems)
    for _, _, _, copy in copies:
        copy.start()
    for _, _, _, copy in copies:
        copy.wait()


def fetch(gate_weight, up_weight, start, depth, width):
    return pl.pallas_call(
        functools.partial(fetch_kernel, width),
        out_shape=pltpu.VMEM((2, depth, width), jnp.bfloat16),
        in_specs=[SCALARS, IN_HBM, IN_HBM],
        out_specs=WHOLE,
        scratch_shapes=[pltpu.SemaphoreType.DMA((2, len(pieces_of(depth, STEP))))],
        compiler_params=params(4),
        cost_estimate=SMALL,
    )(start, in_hbm(gate_weight), in_hbm(up_weight))


def block_kernel(width, has_held, start_ref, x_ref, *refs):
    refs = list(refs)
    held = refs.pop(0) if has_held else None
    gate_ref, up_ref, _, out, stream, total, sems = refs
    first = x_ref.shape[1] - stream.shape[1]
    copies = block_copies(width, first, start_ref, gate_ref, up_ref, stream, sems)
    for _, _, _, copy in copies[:IN_FLIGHT]:
        copy.start()

    def accumulate(w, row, rows, weight):
        term = jnp.dot(x_ref[:, row : row + rows], weight, preferred_element_type=jnp.float32)
        if row == 0:
            total[w] = term
        else:
            total[w] += term

    if has_held:
        for row, rows in pieces_of(first, STEP):
            for w in range(2):
                accumulate(w, row, rows, held[w, row : row + rows, :])
    for i, (w, row, rows, copy) in enumerate(copies):
        copy.wait()
        if i + IN_FLIGHT < len(copies):
            copies[i + IN_FLIGHT][-1].start()
        accumulate(w, first + row, rows, stream[w, row : row + rows, :])
    pack_pair(out, total[0], total[1])


def gate_up(features, gate_weight, up_weight, start, width, after, held=None):
    rows, depth = features.shape
    below = depth if held is None else depth - held.shape[1]
    before = [] if held is None else [in_vmem(held)]
    return pl.pallas_call(
        functools.partial(block_kernel, width, held is not None),
        out_shape=jax.ShapeDtypeStruct((8, packed_pair_width(rows, width)), jnp.bfloat16),
        in_specs=[SCALARS, WHOLE] + [WHOLE] * len(before) + [IN_HBM, IN_HBM, ANY],
        out_specs=WHOLE,
        scratch_shapes=[
            pltpu.VMEM((2, below, width), jnp.bfloat16),
            pltpu.VMEM((2, rows, width), jnp.float32),
            pltpu.SemaphoreType.DMA((2, len(pieces_of(below, STEP)))),
        ],
        compiler_params=params(5 + -(-below * width * 4 // MIB)),
        cost_estimate=SMALL,
    )(start, features, *before, in_hbm(gate_weight), in_hbm(up_weight), after)


def hidden_tail(rows, width):
    half = pl.cdiv(width // 2, 128) * 128
    return half if rows % 8 else 0


def activate_kernel(rows, width, summed, near, out):
    def pair(at):
        return summed[:, at : at + width] + near[:, at : at + width].astype(jnp.float32)

    for g in range(rows // 8):
        value = activate(pair(2 * g * width), pair((2 * g + 1) * width))
        out[:, g * width : (g + 1) * width] = value
    if rows % 8:
        last = pair((rows // 8) * 2 * width)
        value = activate(last[:4], last[4:]).astype(jnp.float32)
        half = hidden_tail(rows, width)
        right = jnp.concatenate([value[:, half:], jnp.zeros((4, 2 * half - width), jnp.float32)], axis=1)
        at = (rows // 8) * width
        out[:, at : at + half] = jnp.concatenate([value[:, :half], right], axis=0).astype(out.dtype)


def activate_packed(summed, near, rows, width):
    return pl.pallas_call(
        functools.partial(activate_kernel, rows, width),
        out_shape=jax.ShapeDtypeStruct(
            (8, (rows // 8) * width + hidden_tail(rows, width)), jnp.bfloat16
        ),
        in_specs=[WHOLE] * 2,
        out_specs=WHOLE,
        compiler_params=params(8),
        cost_estimate=SMALL,
    )(summed, near)


def pack_rows(out, value):
    rows, width = value.shape
    for g in range(rows // 8):
        out[:, g * width : (g + 1) * width] = value[8 * g : 8 * g + 8].astype(out.dtype)
    piece = width // 8
    for r in range(rows // 8 * 8, rows):
        at = (rows // 8) * width + (r % 8) * piece
        row = jnp.concatenate(
            [value[r : r + 1, i * piece : (i + 1) * piece] for i in range(8)], axis=0
        )
        out[:, at : at + piece] = row.astype(out.dtype)


def unpack_rows(out, packed):
    rows, width = out.shape
    for g in range(rows // 8):
        out[8 * g : 8 * g + 8, :] = packed[:, g * width : (g + 1) * width]
    piece = width // 8
    for r in range(rows // 8 * 8, rows):
        at = (rows // 8) * width + (r % 8) * piece
        for i in range(8):
            out[r : r + 1, i * piece : (i + 1) * piece] = packed[i : i + 1, at : at + piece]


def down_kernel(first, rows, width, starts, *refs):
    blocks = starts.shape[0]
    hidden, refs = refs[:blocks], refs[blocks:]
    if not first:
        before, refs = refs[0], refs[1:]
    held, outs, (plain, total) = refs[0], refs[1:-2], refs[-2:]
    if first:
        total = outs[0]
    for b in range(blocks):
        for g in range(rows // 8):
            plain[8 * g : 8 * g + 8, :] = hidden[b][:, g * width : (g + 1) * width].astype(jnp.float32)
        if rows % 8:
            at, half = (rows // 8) * width, hidden_tail(rows, width)
            tail = hidden[b][:, at : at + half].astype(jnp.float32)
            plain[rows - 4 :, :half] = tail[:4]
            plain[rows - 4 :, half:] = tail[4:, : width - half]
        for row, tall in pieces_of(width, STEP):
            term = jnp.dot(
                plain[:, row : row + tall].astype(jnp.bfloat16),
                held[pl.ds(pl.multiple_of(starts[b] + row, 128), tall), :],
                preferred_element_type=jnp.float32,
            )
            if b == 0 and row == 0:
                total[...] = term if first else before[...] + term
            else:
                total[...] += term
    if not first:
        tall = rows // len(outs)
        for r, out in enumerate(outs):
            pack_rows(out, total[r * tall : (r + 1) * tall, :])


def down(hidden, starts, before, weight, rows, width, outs):
    columns = weight.shape[1]
    if before is None:
        shapes = [jax.ShapeDtypeStruct((rows, columns), jnp.float32)]
    else:
        packed = (8, rows // outs * columns // 8)
        shapes = [jax.ShapeDtypeStruct(packed, jnp.bfloat16 if r else jnp.float32) for r in range(outs)]
    carried = [] if before is None else [before]
    return pl.pallas_call(
        functools.partial(down_kernel, before is None, rows, width),
        out_shape=shapes,
        in_specs=[SCALARS] + [WHOLE] * (len(hidden) + len(carried) + 1),
        out_specs=[WHOLE] * len(shapes),
        scratch_shapes=[
            pltpu.VMEM((rows, width), jnp.float32),
            pltpu.VMEM((rows, columns), jnp.float32),
        ],
        compiler_params=params(8),
        cost_estimate=SMALL,
    )(starts, *hidden, *carried, in_vmem(weight))


def finish_kernel(*refs):
    terms, out, plain = refs[:-2], refs[-2], refs[-1]
    packed = terms[0][...]
    for term in terms[1:]:
        packed = packed + term[...].astype(jnp.float32)
    unpack_rows(plain, packed)
    out[...] = plain[...].astype(out.dtype)


def finish(terms, shape):
    return pl.pallas_call(
        finish_kernel,
        out_shape=jax.ShapeDtypeStruct(shape, jnp.bfloat16),
        in_specs=[WHOLE] * len(terms),
        out_specs=WHOLE,
        scratch_shapes=[pltpu.VMEM(shape, jnp.float32)],
        compiler_params=params(4),
        cost_estimate=SMALL,
    )(*terms)


def swap(value, axes, size, distance):
    return lax.ppermute(value, axes, [(i, i ^ distance) for i in range(size)])


def add(a, b):
    return a.astype(jnp.float32) + b.astype(jnp.float32)


def direct(tokens, gate_weight, up_weight, down_weight):
    n_gx = lax.axis_size("gx")
    n_token = lax.axis_size(TOKEN_AXES)
    me = lax.axis_index("gx")
    width = gate_weight.shape[1] // n_gx

    def starts_of(*distances):
        return jnp.stack([(me ^ d) * width for d in distances]).astype(jnp.int32)

    early = gate_weight.shape[0] - STEP
    held = fetch(gate_weight, up_weight, starts_of(3), early, width)
    features = jnp.concatenate(
        [tokens] + [swap(tokens, TOKEN_AXES, n_token, r) for r in range(1, n_token)], axis=0
    )
    rows = features.shape[0]

    def block_for(d, after, held=None):
        return gate_up(features, gate_weight, up_weight, starts_of(d), width, after, held)

    relayed = block_for(3, features, held)
    arrived = swap(relayed, "gx", n_gx, 1)
    across = block_for(2, relayed)
    across = lax.optimization_barrier(add(across, arrived).astype(jnp.bfloat16))
    far = swap(across, "gx", n_gx, 2)
    beside = block_for(1, across)
    near = swap(beside, "gx", n_gx, 1)
    own = block_for(0, beside)
    summed = lax.optimization_barrier(add(own, far))
    hidden = activate_packed(summed, near, rows, width)

    opposite = swap(hidden, "gx", n_gx, 2)
    first = [hidden, swap(hidden, "gx", n_gx, 1), opposite]
    second = [swap(opposite, "gx", n_gx, 1)]
    (partial_sum,) = down(first, starts_of(0, 1, 2), None, down_weight, rows, width, 1)
    outs = down(second, starts_of(3), partial_sum, down_weight, rows, width, n_token)
    terms = [outs[0]] + [swap(outs[r], TOKEN_AXES, n_token, r) for r in range(1, n_token)]
    return finish(terms, tokens.shape)


def offloaded(tokens, gate_weight, up_weight, down_weight):
    features = lax.all_gather(tokens, TOKEN_AXES, axis=0, tiled=True)
    hidden_width = gate_weight.shape[1]
    gate_part = jnp.dot(features, gate_weight, preferred_element_type=jnp.float32)
    up_part = jnp.dot(features, up_weight, preferred_element_type=jnp.float32)
    summed = lax.psum(
        jnp.concatenate([gate_part, up_part], axis=1).astype(jnp.bfloat16), "gx"
    ).astype(jnp.float32)
    hidden = activate(summed[:, :hidden_width], summed[:, hidden_width:])
    partial_value = jnp.dot(hidden, down_weight, preferred_element_type=jnp.float32)
    return lax.psum_scatter(
        partial_value.astype(jnp.bfloat16), TOKEN_AXES, scatter_dimension=0, tiled=True
    )


def shards(tokens, gate_weight, up_weight, down_weight):
    n_gx = lax.axis_size("gx")
    n_token = lax.axis_size(TOKEN_AXES)
    rows = tokens.shape[0] * n_token
    tokens_fit = n_token > 1 and n_token & (n_token - 1) == 0 and rows % 4 == 0
    weights_fit = gate_weight.shape[1] % (128 * 4) == 0 and gate_weight.shape[0] % STEP == 0 and gate_weight.shape[0] > STEP
    columns_fit = down_weight.shape[1] % (128 * 8) == 0
    if n_gx == 4 and tokens_fit and weights_fit and columns_fit:
        return direct(tokens, gate_weight, up_weight, down_weight)
    return offloaded(tokens, gate_weight, up_weight, down_weight)


def solution(mesh):
    return jax.shard_map(
        shards,
        mesh=mesh,
        in_specs=(
            P(("grp", "gy", "gz"), "gx"),
            P("gx", ("gy", "gz")),
            P("gx", ("gy", "gz")),
            P(("gy", "gz"), "gx"),
        ),
        out_specs=P(("grp", "gy", "gz"), "gx"),
        check_vma=False,
    )
```

```python
import functools

import jax
import jax.numpy as jnp
from jax import lax
from jax.experimental import pallas as pl
from jax.experimental.pallas import tpu as pltpu
from jax.sharding import PartitionSpec as P

MIB = 1 << 20
STEP = 256
TOKEN_AXES = ("gy", "gz")
IN_HBM = pl.BlockSpec(memory_space=pltpu.HBM)
ANY = pl.BlockSpec(memory_space=pl.ANY)
WHOLE = pl.BlockSpec(memory_space=pltpu.VMEM)
SCALARS = pl.BlockSpec(memory_space=pltpu.SMEM)


def activate(gate, up):
    return (jax.nn.silu(gate) * up).astype(jnp.bfloat16)


def pieces_of(total, step):
    return [(start, min(step, total - start)) for start in range(0, total, step)]


def in_hbm(value):
    return pltpu.with_memory_space_constraint(value, pltpu.HBM)


def in_vmem(value):
    return pltpu.with_memory_space_constraint(value, pltpu.VMEM)


SMALL = pl.CostEstimate(flops=0, bytes_accessed=MIB, transcendentals=0)


def params(mib):
    return pltpu.CompilerParams(vmem_limit_bytes=mib * MIB)


def packed_pair_width(rows, width):
    return (rows // 8) * 2 * width + (width if rows % 8 else 0)


def pack_pair(out, gate, up):
    rows, width = gate.shape
    for g in range(rows // 8):
        for w, value in enumerate((gate, up)):
            at = (2 * g + w) * width
            out[:, at : at + width] = value[8 * g : 8 * g + 8].astype(out.dtype)
    if rows % 8:
        at = (rows // 8) * 2 * width
        tail = jnp.concatenate([gate[rows - 4 :], up[rows - 4 :]], axis=0)
        out[:, at : at + width] = tail.astype(out.dtype)


def piece_copy(width, start_ref, weight, held, sems, w, k):
    return pltpu.make_async_copy(
        weight.at[pl.ds(k * STEP, STEP), pl.ds(pl.multiple_of(start_ref[0], 128), width)],
        held.at[w, pl.ds(k * STEP, STEP)],
        sems.at[w, k],
    )


def start_copies(width, start_ref, weights, held, sems):
    @pl.loop(0, held.shape[1] // STEP)
    def _(k):
        for w, weight in enumerate(weights):
            piece_copy(width, start_ref, weight, held, sems, w, k).start()


def fetch_kernel(width, start_ref, gate_ref, up_ref, held, sems):
    weights = (gate_ref, up_ref)
    start_copies(width, start_ref, weights, held, sems)

    @pl.loop(0, held.shape[1] // STEP)
    def _(k):
        for w, weight in enumerate(weights):
            piece_copy(width, start_ref, weight, held, sems, w, k).wait()


def fetch(gate_weight, up_weight, start, width):
    depth = gate_weight.shape[0]
    return pl.pallas_call(
        functools.partial(fetch_kernel, width),
        out_shape=pltpu.VMEM((2, depth, width), jnp.bfloat16),
        in_specs=[SCALARS, IN_HBM, IN_HBM],
        out_specs=WHOLE,
        scratch_shapes=[pltpu.SemaphoreType.DMA((2, depth // STEP))],
        compiler_params=params(4),
        cost_estimate=SMALL,
    )(start, in_hbm(gate_weight), in_hbm(up_weight))


def accumulate(x_ref, held, total, w, k):
    rows = pl.ds(pl.multiple_of(k * STEP, STEP), STEP)
    total[w] += jnp.dot(x_ref[:, rows], held[w, rows, :], preferred_element_type=jnp.float32)


def held_kernel(x_ref, held, out, total):
    total[...] = jnp.zeros_like(total)

    @pl.loop(0, held.shape[1] // STEP)
    def _(k):
        for w in range(2):
            accumulate(x_ref, held, total, w, k)

    pack_pair(out, total[0], total[1])


def gate_up_held(features, held):
    rows, width = features.shape[0], held.shape[2]
    return pl.pallas_call(
        held_kernel,
        out_shape=jax.ShapeDtypeStruct((8, packed_pair_width(rows, width)), jnp.bfloat16),
        in_specs=[WHOLE, WHOLE],
        out_specs=WHOLE,
        scratch_shapes=[pltpu.VMEM((2, rows, width), jnp.float32)],
        compiler_params=params(8),
        cost_estimate=SMALL,
    )(features, in_vmem(held))


def stream_kernel(width, start_ref, x_ref, gate_ref, up_ref, _, out, held, total, sems):
    weights = (gate_ref, up_ref)
    start_copies(width, start_ref, weights, held, sems)
    total[...] = jnp.zeros_like(total)

    @pl.loop(0, held.shape[1] // STEP)
    def _(k):
        for w, weight in enumerate(weights):
            piece_copy(width, start_ref, weight, held, sems, w, k).wait()
            accumulate(x_ref, held, total, w, k)

    pack_pair(out, total[0], total[1])


def gate_up_stream(features, gate_weight, up_weight, start, width, after):
    rows, depth = features.shape
    return pl.pallas_call(
        functools.partial(stream_kernel, width),
        out_shape=jax.ShapeDtypeStruct((8, packed_pair_width(rows, width)), jnp.bfloat16),
        in_specs=[SCALARS, WHOLE, IN_HBM, IN_HBM, ANY],
        out_specs=WHOLE,
        scratch_shapes=[
            pltpu.VMEM((2, depth, width), jnp.bfloat16),
            pltpu.VMEM((2, rows, width), jnp.float32),
            pltpu.SemaphoreType.DMA((2, depth // STEP)),
        ],
        compiler_params=params(18),
        cost_estimate=SMALL,
    )(start, features, in_hbm(gate_weight), in_hbm(up_weight), after)


def hidden_tail(rows, width):
    half = pl.cdiv(width // 2, 128) * 128
    return half if rows % 8 else 0


def activate_kernel(rows, width, summed, near, out):
    def pair(at):
        return summed[:, at : at + width] + near[:, at : at + width].astype(jnp.float32)

    for g in range(rows // 8):
        value = activate(pair(2 * g * width), pair((2 * g + 1) * width))
        out[:, g * width : (g + 1) * width] = value
    if rows % 8:
        last = pair((rows // 8) * 2 * width)
        value = activate(last[:4], last[4:]).astype(jnp.float32)
        half = hidden_tail(rows, width)
        right = jnp.concatenate([value[:, half:], jnp.zeros((4, 2 * half - width), jnp.float32)], axis=1)
        at = (rows // 8) * width
        out[:, at : at + half] = jnp.concatenate([value[:, :half], right], axis=0).astype(out.dtype)


def activate_packed(summed, near, rows, width):
    return pl.pallas_call(
        functools.partial(activate_kernel, rows, width),
        out_shape=jax.ShapeDtypeStruct(
            (8, (rows // 8) * width + hidden_tail(rows, width)), jnp.bfloat16
        ),
        in_specs=[WHOLE] * 2,
        out_specs=WHOLE,
        compiler_params=params(8),
        cost_estimate=SMALL,
    )(summed, near)


def pack_rows(out, value):
    rows, width = value.shape
    for g in range(rows // 8):
        out[:, g * width : (g + 1) * width] = value[8 * g : 8 * g + 8].astype(out.dtype)
    piece = width // 8
    for r in range(rows // 8 * 8, rows):
        at = (rows // 8) * width + (r % 8) * piece
        row = jnp.concatenate(
            [value[r : r + 1, i * piece : (i + 1) * piece] for i in range(8)], axis=0
        )
        out[:, at : at + piece] = row.astype(out.dtype)


def unpack_rows(out, packed):
    rows, width = out.shape
    for g in range(rows // 8):
        out[8 * g : 8 * g + 8, :] = packed[:, g * width : (g + 1) * width]
    piece = width // 8
    for r in range(rows // 8 * 8, rows):
        at = (rows // 8) * width + (r % 8) * piece
        for i in range(8):
            out[r : r + 1, i * piece : (i + 1) * piece] = packed[i : i + 1, at : at + piece]


def down_kernel(first, rows, width, starts, *refs):
    blocks = starts.shape[0]
    hidden, refs = refs[:blocks], refs[blocks:]
    if not first:
        before, refs = refs[0], refs[1:]
    held, outs, (plain, total) = refs[0], refs[1:-2], refs[-2:]
    if first:
        total = outs[0]
        total[...] = jnp.zeros_like(total)
    else:
        total[...] = before[...]
    for b in range(blocks):
        for g in range(rows // 8):
            plain[8 * g : 8 * g + 8, :] = hidden[b][:, g * width : (g + 1) * width].astype(jnp.float32)
        if rows % 8:
            at, half = (rows // 8) * width, hidden_tail(rows, width)
            tail = hidden[b][:, at : at + half].astype(jnp.float32)
            plain[rows - 4 :, :half] = tail[:4]
            plain[rows - 4 :, half:] = tail[4:, : width - half]

        def accumulate_down(row, tall):
            total[...] += jnp.dot(
                plain[:, pl.ds(row, tall)].astype(jnp.bfloat16),
                held[pl.ds(pl.multiple_of(starts[b] + row, 128), tall), :],
                preferred_element_type=jnp.float32,
            )

        @pl.loop(0, width // STEP)
        def _(k):
            accumulate_down(pl.multiple_of(k * STEP, STEP), STEP)

        if width % STEP:
            accumulate_down(width // STEP * STEP, width % STEP)
    if not first:
        tall = rows // len(outs)
        for r, out in enumerate(outs):
            pack_rows(out, total[r * tall : (r + 1) * tall, :])


def down(hidden, starts, before, weight, rows, width, outs):
    columns = weight.shape[1]
    if before is None:
        shapes = [jax.ShapeDtypeStruct((rows, columns), jnp.float32)]
    else:
        packed = (8, rows // outs * columns // 8)
        shapes = [jax.ShapeDtypeStruct(packed, jnp.bfloat16 if r else jnp.float32) for r in range(outs)]
    carried = [] if before is None else [before]
    return pl.pallas_call(
        functools.partial(down_kernel, before is None, rows, width),
        out_shape=shapes,
        in_specs=[SCALARS] + [WHOLE] * (len(hidden) + len(carried) + 1),
        out_specs=[WHOLE] * len(shapes),
        scratch_shapes=[
            pltpu.VMEM((rows, width), jnp.float32),
            pltpu.VMEM((rows, columns), jnp.float32),
        ],
        compiler_params=params(8),
        cost_estimate=SMALL,
    )(starts, *hidden, *carried, in_vmem(weight))


def finish_kernel(*refs):
    terms, out, plain = refs[:-2], refs[-2], refs[-1]
    packed = terms[0][...]
    for term in terms[1:]:
        packed = packed + term[...].astype(jnp.float32)
    unpack_rows(plain, packed)
    out[...] = plain[...].astype(out.dtype)


def finish(terms, shape):
    return pl.pallas_call(
        finish_kernel,
        out_shape=jax.ShapeDtypeStruct(shape, jnp.bfloat16),
        in_specs=[WHOLE] * len(terms),
        out_specs=WHOLE,
        scratch_shapes=[pltpu.VMEM(shape, jnp.float32)],
        compiler_params=params(4),
        cost_estimate=SMALL,
    )(*terms)


def swap(value, axes, size, distance):
    return lax.ppermute(value, axes, [(i, i ^ distance) for i in range(size)])


def add(a, b):
    return a.astype(jnp.float32) + b.astype(jnp.float32)


def direct(tokens, gate_weight, up_weight, down_weight):
    n_gx = lax.axis_size("gx")
    n_token = lax.axis_size(TOKEN_AXES)
    me = lax.axis_index("gx")
    width = gate_weight.shape[1] // n_gx

    def starts_of(*distances):
        return jnp.stack([(me ^ d) * width for d in distances]).astype(jnp.int32)

    held = fetch(gate_weight, up_weight, starts_of(3), width)
    features = jnp.concatenate(
        [tokens] + [swap(tokens, TOKEN_AXES, n_token, r) for r in range(1, n_token)], axis=0
    )
    rows = features.shape[0]

    def block_for(d, after):
        return gate_up_stream(features, gate_weight, up_weight, starts_of(d), width, after)

    relayed = gate_up_held(features, held)
    arrived = swap(relayed, "gx", n_gx, 1)
    across = block_for(2, relayed)
    across = lax.optimization_barrier(add(across, arrived).astype(jnp.bfloat16))
    far = swap(across, "gx", n_gx, 2)
    beside = block_for(1, across)
    near = swap(beside, "gx", n_gx, 1)
    own = block_for(0, beside)
    summed = lax.optimization_barrier(add(own, far))
    hidden = activate_packed(summed, near, rows, width)

    opposite = swap(hidden, "gx", n_gx, 2)
    first = [hidden, swap(hidden, "gx", n_gx, 1), opposite]
    second = [swap(opposite, "gx", n_gx, 1)]
    (partial_sum,) = down(first, starts_of(0, 1, 2), None, down_weight, rows, width, 1)
    outs = down(second, starts_of(3), partial_sum, down_weight, rows, width, n_token)
    terms = [outs[0]] + [swap(outs[r], TOKEN_AXES, n_token, r) for r in range(1, n_token)]
    return finish(terms, tokens.shape)


def offloaded(tokens, gate_weight, up_weight, down_weight):
    features = lax.all_gather(tokens, TOKEN_AXES, axis=0, tiled=True)
    hidden_width = gate_weight.shape[1]
    gate_part = jnp.dot(features, gate_weight, preferred_element_type=jnp.float32)
    up_part = jnp.dot(features, up_weight, preferred_element_type=jnp.float32)
    summed = lax.psum(
        jnp.concatenate([gate_part, up_part], axis=1).astype(jnp.bfloat16), "gx"
    ).astype(jnp.float32)
    hidden = activate(summed[:, :hidden_width], summed[:, hidden_width:])
    partial_value = jnp.dot(hidden, down_weight, preferred_element_type=jnp.float32)
    return lax.psum_scatter(
        partial_value.astype(jnp.bfloat16), TOKEN_AXES, scatter_dimension=0, tiled=True
    )


def shards(tokens, gate_weight, up_weight, down_weight):
    n_gx = lax.axis_size("gx")
    n_token = lax.axis_size(TOKEN_AXES)
    rows = tokens.shape[0] * n_token
    tokens_fit = n_token > 1 and n_token & (n_token - 1) == 0 and rows % 4 == 0
    weights_fit = gate_weight.shape[1] % (128 * 4) == 0 and gate_weight.shape[0] % STEP == 0
    columns_fit = down_weight.shape[1] % (128 * 8) == 0
    if n_gx == 4 and tokens_fit and weights_fit and columns_fit:
        return direct(tokens, gate_weight, up_weight, down_weight)
    return offloaded(tokens, gate_weight, up_weight, down_weight)


def solution(mesh):
    return jax.shard_map(
        shards,
        mesh=mesh,
        in_specs=(
            P(("grp", "gy", "gz"), "gx"),
            P("gx", ("gy", "gz")),
            P("gx", ("gy", "gz")),
            P(("gy", "gz"), "gx"),
        ),
        out_specs=P(("grp", "gy", "gz"), "gx"),
        check_vma=False,
    )
```

```python
import functools

import jax
import jax.numpy as jnp
from jax import lax
from jax.experimental import pallas as pl
from jax.experimental.pallas import tpu as pltpu
from jax.sharding import PartitionSpec as P

MIB = 1 << 20
STEP = 256
TOKEN_AXES = ("gy", "gz")
IN_HBM = pl.BlockSpec(memory_space=pltpu.HBM)
ANY = pl.BlockSpec(memory_space=pl.ANY)
WHOLE = pl.BlockSpec(memory_space=pltpu.VMEM)
SCALARS = pl.BlockSpec(memory_space=pltpu.SMEM)


def activate(gate, up):
    return (jax.nn.silu(gate) * up).astype(jnp.bfloat16)


def pieces_of(total, step):
    return [(start, min(step, total - start)) for start in range(0, total, step)]


def in_hbm(value):
    return pltpu.with_memory_space_constraint(value, pltpu.HBM)


def in_vmem(value):
    return pltpu.with_memory_space_constraint(value, pltpu.VMEM)


SMALL = pl.CostEstimate(flops=0, bytes_accessed=MIB, transcendentals=0)


def params(mib):
    return pltpu.CompilerParams(vmem_limit_bytes=mib * MIB)


def packed_pair_width(rows, width):
    return (rows // 8) * 2 * width + (width if rows % 8 else 0)


def pack_pair(out, gate, up):
    rows, width = gate.shape
    for g in range(rows // 8):
        for w, value in enumerate((gate, up)):
            at = (2 * g + w) * width
            out[:, at : at + width] = value[8 * g : 8 * g + 8].astype(out.dtype)
    if rows % 8:
        at = (rows // 8) * 2 * width
        tail = jnp.concatenate([gate[rows - 4 :], up[rows - 4 :]], axis=0)
        out[:, at : at + width] = tail.astype(out.dtype)


def start_copies(width, starts, b, gate_ref, up_ref, held, sems):
    columns = pl.ds(pl.multiple_of(starts[b], 128), width)
    copies = []
    for k, (row, rows) in enumerate(pieces_of(held.shape[1], STEP)):
        for w, weight in enumerate((gate_ref, up_ref)):
            copy = pltpu.make_async_copy(
                weight.at[pl.ds(row, rows), columns], held.at[w, pl.ds(row, rows)], sems.at[w, k]
            )
            copy.start()
            copies.append((w, row, rows, copy))
    return copies


def fetch_kernel(width, start_ref, gate_ref, up_ref, held, sems):
    for _, _, _, copy in start_copies(width, start_ref, 0, gate_ref, up_ref, held, sems):
        copy.wait()


def fetch(gate_weight, up_weight, start, width):
    depth = gate_weight.shape[0]
    return pl.pallas_call(
        functools.partial(fetch_kernel, width),
        out_shape=pltpu.VMEM((2, depth, width), jnp.bfloat16),
        in_specs=[SCALARS, IN_HBM, IN_HBM],
        out_specs=WHOLE,
        scratch_shapes=[pltpu.SemaphoreType.DMA((2, len(pieces_of(depth, STEP))))],
        compiler_params=params(4),
        cost_estimate=SMALL,
    )(start, in_hbm(gate_weight), in_hbm(up_weight))


def multiply(x_ref, held, total, steps):
    for w, row, rows, copy in steps:
        if copy is not None:
            copy.wait()
        term = jnp.dot(
            x_ref[:, row : row + rows], held[w, row : row + rows, :], preferred_element_type=jnp.float32
        )
        if row == 0:
            total[w] = term
        else:
            total[w] += term


def held_kernel(x_ref, held, out, total):
    parts = pieces_of(x_ref.shape[1], STEP)
    multiply(x_ref, held, total, [(w, row, rows, None) for w in range(2) for row, rows in parts])
    pack_pair(out, total[0], total[1])


def gate_up_held(features, held):
    rows, width = features.shape[0], held.shape[2]
    return pl.pallas_call(
        held_kernel,
        out_shape=jax.ShapeDtypeStruct((8, packed_pair_width(rows, width)), jnp.bfloat16),
        in_specs=[WHOLE, WHOLE],
        out_specs=WHOLE,
        scratch_shapes=[pltpu.VMEM((2, rows, width), jnp.float32)],
        compiler_params=params(8),
        cost_estimate=SMALL,
    )(features, in_vmem(held))


def stream_kernel(widths, starts, x_ref, gate_ref, up_ref, _, *refs):
    outs, refs = refs[: len(widths)], refs[len(widths) :]
    blocks = []
    for b, width in enumerate(widths):
        held, total, sems = refs[3 * b : 3 * b + 3]
        copies = start_copies(width, starts, b, gate_ref, up_ref, held, sems)
        blocks.append((outs[b], held, total, copies))
    for out, held, total, copies in blocks:
        multiply(x_ref, held, total, copies)
        pack_pair(out, total[0], total[1])


def gate_up_stream(features, gate_weight, up_weight, starts, widths, after):
    rows, depth = features.shape
    scratch = []
    for width in widths:
        scratch += [
            pltpu.VMEM((2, depth, width), jnp.bfloat16),
            pltpu.VMEM((2, rows, width), jnp.float32),
            pltpu.SemaphoreType.DMA((2, len(pieces_of(depth, STEP)))),
        ]
    return pl.pallas_call(
        functools.partial(stream_kernel, widths),
        out_shape=[
            jax.ShapeDtypeStruct((8, packed_pair_width(rows, w)), jnp.bfloat16) for w in widths
        ],
        in_specs=[SCALARS, WHOLE, IN_HBM, IN_HBM, ANY],
        out_specs=[WHOLE] * len(widths),
        scratch_shapes=scratch,
        compiler_params=params(5 + -(-depth * sum(widths) * 4 // MIB)),
        cost_estimate=SMALL,
    )(starts, features, in_hbm(gate_weight), in_hbm(up_weight), after)


def hidden_tail(rows, width):
    half = pl.cdiv(width // 2, 128) * 128
    return half if rows % 8 else 0


def activate_kernel(rows, widths, summed, *refs):
    near, out = refs[:-1], refs[-1]
    width = sum(widths)

    def pair(w, g):
        column = (2 * g + w) * width
        parts = []
        for part, wide in zip(near, widths):
            at = (2 * g + w) * wide
            parts.append(
                summed[:, column : column + wide] + part[:, at : at + wide].astype(jnp.float32)
            )
            column += wide
        return jnp.concatenate(parts, axis=1)

    for g in range(rows // 8):
        out[:, g * width : (g + 1) * width] = activate(pair(0, g), pair(1, g))
    if rows % 8:
        last = pair(0, rows // 8)
        value = activate(last[:4], last[4:]).astype(jnp.float32)
        half = hidden_tail(rows, width)
        right = jnp.concatenate([value[:, half:], jnp.zeros((4, 2 * half - width), jnp.float32)], axis=1)
        at = (rows // 8) * width
        out[:, at : at + half] = jnp.concatenate([value[:, :half], right], axis=0).astype(out.dtype)


def activate_packed(summed, near, rows, widths):
    width = sum(widths)
    return pl.pallas_call(
        functools.partial(activate_kernel, rows, widths),
        out_shape=jax.ShapeDtypeStruct(
            (8, (rows // 8) * width + hidden_tail(rows, width)), jnp.bfloat16
        ),
        in_specs=[WHOLE] * (1 + len(near)),
        out_specs=WHOLE,
        compiler_params=params(8),
        cost_estimate=SMALL,
    )(summed, *near)


def pack_rows(out, value):
    rows, width = value.shape
    for g in range(rows // 8):
        out[:, g * width : (g + 1) * width] = value[8 * g : 8 * g + 8].astype(out.dtype)
    piece = width // 8
    for r in range(rows // 8 * 8, rows):
        at = (rows // 8) * width + (r % 8) * piece
        row = jnp.concatenate(
            [value[r : r + 1, i * piece : (i + 1) * piece] for i in range(8)], axis=0
        )
        out[:, at : at + piece] = row.astype(out.dtype)


def unpack_rows(out, packed):
    rows, width = out.shape
    for g in range(rows // 8):
        out[8 * g : 8 * g + 8, :] = packed[:, g * width : (g + 1) * width]
    piece = width // 8
    for r in range(rows // 8 * 8, rows):
        at = (rows // 8) * width + (r % 8) * piece
        for i in range(8):
            out[r : r + 1, i * piece : (i + 1) * piece] = packed[i : i + 1, at : at + piece]


def down_kernel(first, rows, width, starts, *refs):
    blocks = starts.shape[0]
    hidden, refs = refs[:blocks], refs[blocks:]
    if not first:
        before, refs = refs[0], refs[1:]
    held, outs, (plain, total) = refs[0], refs[1:-2], refs[-2:]
    if first:
        total = outs[0]
    for b in range(blocks):
        for g in range(rows // 8):
            plain[8 * g : 8 * g + 8, :] = hidden[b][:, g * width : (g + 1) * width].astype(jnp.float32)
        if rows % 8:
            at, half = (rows // 8) * width, hidden_tail(rows, width)
            tail = hidden[b][:, at : at + half].astype(jnp.float32)
            plain[rows - 4 :, :half] = tail[:4]
            plain[rows - 4 :, half:] = tail[4:, : width - half]
        for row, tall in pieces_of(width, STEP):
            term = jnp.dot(
                plain[:, row : row + tall].astype(jnp.bfloat16),
                held[pl.ds(pl.multiple_of(starts[b] + row, 128), tall), :],
                preferred_element_type=jnp.float32,
            )
            if b == 0 and row == 0:
                total[...] = term if first else before[...] + term
            else:
                total[...] += term
    if not first:
        tall = rows // len(outs)
        for r, out in enumerate(outs):
            pack_rows(out, total[r * tall : (r + 1) * tall, :])


def down(hidden, starts, before, weight, rows, width, outs):
    columns = weight.shape[1]
    if before is None:
        shapes = [jax.ShapeDtypeStruct((rows, columns), jnp.float32)]
    else:
        packed = (8, rows // outs * columns // 8)
        shapes = [jax.ShapeDtypeStruct(packed, jnp.bfloat16 if r else jnp.float32) for r in range(outs)]
    carried = [] if before is None else [before]
    return pl.pallas_call(
        functools.partial(down_kernel, before is None, rows, width),
        out_shape=shapes,
        in_specs=[SCALARS] + [WHOLE] * (len(hidden) + len(carried) + 1),
        out_specs=[WHOLE] * len(shapes),
        scratch_shapes=[
            pltpu.VMEM((rows, width), jnp.float32),
            pltpu.VMEM((rows, columns), jnp.float32),
        ],
        compiler_params=params(8),
        cost_estimate=SMALL,
    )(starts, *hidden, *carried, in_vmem(weight))


def finish_kernel(*refs):
    terms, out, plain = refs[:-2], refs[-2], refs[-1]
    packed = terms[0][...]
    for term in terms[1:]:
        packed = packed + term[...].astype(jnp.float32)
    unpack_rows(plain, packed)
    out[...] = plain[...].astype(out.dtype)


def finish(terms, shape):
    return pl.pallas_call(
        finish_kernel,
        out_shape=jax.ShapeDtypeStruct(shape, jnp.bfloat16),
        in_specs=[WHOLE] * len(terms),
        out_specs=WHOLE,
        scratch_shapes=[pltpu.VMEM(shape, jnp.float32)],
        compiler_params=params(4),
        cost_estimate=SMALL,
    )(*terms)


def swap(value, axes, size, distance):
    return lax.ppermute(value, axes, [(i, i ^ distance) for i in range(size)])


def add(a, b):
    return a.astype(jnp.float32) + b.astype(jnp.float32)


def direct(tokens, gate_weight, up_weight, down_weight):
    n_gx = lax.axis_size("gx")
    n_token = lax.axis_size(TOKEN_AXES)
    me = lax.axis_index("gx")
    width = gate_weight.shape[1] // n_gx

    def starts_of(*distances):
        return jnp.stack([(me ^ d) * width for d in distances]).astype(jnp.int32)

    held = fetch(gate_weight, up_weight, starts_of(3), width)
    features = jnp.concatenate(
        [tokens] + [swap(tokens, TOKEN_AXES, n_token, r) for r in range(1, n_token)], axis=0
    )
    rows = features.shape[0]

    def blocks_for(starts, widths, after):
        return gate_up_stream(features, gate_weight, up_weight, starts, widths, after)

    ahead = width // 128 * 2 // 5 * 128
    relayed = gate_up_held(features, held)
    arrived = swap(relayed, "gx", n_gx, 1)
    across, beside = blocks_for(starts_of(2, 1), (width, ahead), relayed)
    across = lax.optimization_barrier(add(across, arrived).astype(jnp.bfloat16))
    far = swap(across, "gx", n_gx, 2)
    near = [swap(beside, "gx", n_gx, 1)]
    (beside,) = blocks_for(starts_of(1) + ahead, (width - ahead,), across)
    near.append(swap(beside, "gx", n_gx, 1))
    (own,) = blocks_for(starts_of(0), (width,), beside)
    summed = lax.optimization_barrier(add(own, far))
    hidden = activate_packed(summed, near, rows, (ahead, width - ahead))

    opposite = swap(hidden, "gx", n_gx, 2)
    first = [hidden, swap(hidden, "gx", n_gx, 1), opposite]
    second = [swap(opposite, "gx", n_gx, 1)]
    (partial_sum,) = down(first, starts_of(0, 1, 2), None, down_weight, rows, width, 1)
    outs = down(second, starts_of(3), partial_sum, down_weight, rows, width, n_token)
    terms = [outs[0]] + [swap(outs[r], TOKEN_AXES, n_token, r) for r in range(1, n_token)]
    return finish(terms, tokens.shape)


def offloaded(tokens, gate_weight, up_weight, down_weight):
    features = lax.all_gather(tokens, TOKEN_AXES, axis=0, tiled=True)
    hidden_width = gate_weight.shape[1]
    gate_part = jnp.dot(features, gate_weight, preferred_element_type=jnp.float32)
    up_part = jnp.dot(features, up_weight, preferred_element_type=jnp.float32)
    summed = lax.psum(
        jnp.concatenate([gate_part, up_part], axis=1).astype(jnp.bfloat16), "gx"
    ).astype(jnp.float32)
    hidden = activate(summed[:, :hidden_width], summed[:, hidden_width:])
    partial_value = jnp.dot(hidden, down_weight, preferred_element_type=jnp.float32)
    return lax.psum_scatter(
        partial_value.astype(jnp.bfloat16), TOKEN_AXES, scatter_dimension=0, tiled=True
    )


def shards(tokens, gate_weight, up_weight, down_weight):
    n_gx = lax.axis_size("gx")
    n_token = lax.axis_size(TOKEN_AXES)
    rows = tokens.shape[0] * n_token
    tokens_fit = n_token > 1 and n_token & (n_token - 1) == 0 and rows % 4 == 0
    weights_fit = gate_weight.shape[1] % (128 * 4) == 0 and gate_weight.shape[0] % STEP == 0
    columns_fit = down_weight.shape[1] % (128 * 8) == 0
    if n_gx == 4 and tokens_fit and weights_fit and columns_fit:
        return direct(tokens, gate_weight, up_weight, down_weight)
    return offloaded(tokens, gate_weight, up_weight, down_weight)


def solution(mesh):
    return jax.shard_map(
        shards,
        mesh=mesh,
        in_specs=(
            P(("grp", "gy", "gz"), "gx"),
            P("gx", ("gy", "gz")),
            P("gx", ("gy", "gz")),
            P(("gy", "gz"), "gx"),
        ),
        out_specs=P(("grp", "gy", "gz"), "gx"),
        check_vma=False,
    )
```

```python
import functools

import jax
import jax.numpy as jnp
from jax import lax
from jax.experimental import pallas as pl
from jax.experimental.pallas import tpu as pltpu
from jax.sharding import PartitionSpec as P

MIB = 1 << 20
STEP = 256
IN_FLIGHT = 8
TOKEN_AXES = ("gy", "gz")
IN_HBM = pl.BlockSpec(memory_space=pltpu.HBM)
ANY = pl.BlockSpec(memory_space=pl.ANY)
WHOLE = pl.BlockSpec(memory_space=pltpu.VMEM)
SCALARS = pl.BlockSpec(memory_space=pltpu.SMEM)


def activate(gate, up):
    return (jax.nn.silu(gate) * up).astype(jnp.bfloat16)


def pieces_of(total, step):
    return [(start, min(step, total - start)) for start in range(0, total, step)]


def in_hbm(value):
    return pltpu.with_memory_space_constraint(value, pltpu.HBM)


def in_vmem(value):
    return pltpu.with_memory_space_constraint(value, pltpu.VMEM)


SMALL = pl.CostEstimate(flops=0, bytes_accessed=MIB, transcendentals=0)


def params(mib):
    return pltpu.CompilerParams(vmem_limit_bytes=mib * MIB)


def packed_pair_width(rows, width):
    return (rows // 8) * 2 * width + (width if rows % 8 else 0)


def pack_pair(out, gate, up):
    rows, width = gate.shape
    for g in range(rows // 8):
        for w, value in enumerate((gate, up)):
            at = (2 * g + w) * width
            out[:, at : at + width] = value[8 * g : 8 * g + 8].astype(out.dtype)
    if rows % 8:
        at = (rows // 8) * 2 * width
        tail = jnp.concatenate([gate[rows - 4 :], up[rows - 4 :]], axis=0)
        out[:, at : at + width] = tail.astype(out.dtype)


def block_copies(width, starts, b, gate_ref, up_ref, held, sems):
    columns = pl.ds(pl.multiple_of(starts[b], 128), width)
    copies = []
    for k, (row, rows) in enumerate(pieces_of(held.shape[1], STEP)):
        for w, weight in enumerate((gate_ref, up_ref)):
            copy = pltpu.make_async_copy(
                weight.at[pl.ds(row, rows), columns], held.at[w, pl.ds(row, rows)], sems.at[w, k]
            )
            copies.append((w, row, rows, copy))
    return copies


def fetch_kernel(width, start_ref, gate_ref, up_ref, held, sems):
    copies = block_copies(width, start_ref, 0, gate_ref, up_ref, held, sems)
    for _, _, _, copy in copies:
        copy.start()
    for _, _, _, copy in copies:
        copy.wait()


def fetch(gate_weight, up_weight, start, width):
    depth = gate_weight.shape[0]
    return pl.pallas_call(
        functools.partial(fetch_kernel, width),
        out_shape=pltpu.VMEM((2, depth, width), jnp.bfloat16),
        in_specs=[SCALARS, IN_HBM, IN_HBM],
        out_specs=WHOLE,
        scratch_shapes=[pltpu.SemaphoreType.DMA((2, len(pieces_of(depth, STEP))))],
        compiler_params=params(4),
        cost_estimate=SMALL,
    )(start, in_hbm(gate_weight), in_hbm(up_weight))


def multiply(x_ref, held, total, steps, waiting=()):
    for w, row, rows, copy in steps:
        if copy is not None:
            copy.wait()
        if waiting:
            waiting.pop(0).start()
        term = jnp.dot(
            x_ref[:, row : row + rows], held[w, row : row + rows, :], preferred_element_type=jnp.float32
        )
        if row == 0:
            total[w] = term
        else:
            total[w] += term


def held_kernel(x_ref, held, out, total):
    parts = pieces_of(x_ref.shape[1], STEP)
    multiply(x_ref, held, total, [(w, row, rows, None) for w in range(2) for row, rows in parts])
    pack_pair(out, total[0], total[1])


def gate_up_held(features, held):
    rows, width = features.shape[0], held.shape[2]
    return pl.pallas_call(
        held_kernel,
        out_shape=jax.ShapeDtypeStruct((8, packed_pair_width(rows, width)), jnp.bfloat16),
        in_specs=[WHOLE, WHOLE],
        out_specs=WHOLE,
        scratch_shapes=[pltpu.VMEM((2, rows, width), jnp.float32)],
        compiler_params=params(8),
        cost_estimate=SMALL,
    )(features, in_vmem(held))


def stream_kernel(widths, starts, x_ref, gate_ref, up_ref, _, *refs):
    outs, refs = refs[: len(widths)], refs[len(widths) :]
    blocks = []
    for b, width in enumerate(widths):
        held, total, sems = refs[3 * b : 3 * b + 3]
        copies = block_copies(width, starts, b, gate_ref, up_ref, held, sems)
        blocks.append((outs[b], held, total, copies))
    waiting = [step[-1] for block in blocks for step in block[-1]]
    in_flight = IN_FLIGHT if len(widths) > 1 else len(waiting)
    for copy in waiting[:in_flight]:
        copy.start()
    waiting = waiting[in_flight:]
    for out, held, total, copies in blocks:
        multiply(x_ref, held, total, copies, waiting)
        pack_pair(out, total[0], total[1])


def gate_up_stream(features, gate_weight, up_weight, starts, widths, after):
    rows, depth = features.shape
    scratch = []
    for width in widths:
        scratch += [
            pltpu.VMEM((2, depth, width), jnp.bfloat16),
            pltpu.VMEM((2, rows, width), jnp.float32),
            pltpu.SemaphoreType.DMA((2, len(pieces_of(depth, STEP)))),
        ]
    return pl.pallas_call(
        functools.partial(stream_kernel, widths),
        out_shape=[
            jax.ShapeDtypeStruct((8, packed_pair_width(rows, w)), jnp.bfloat16) for w in widths
        ],
        in_specs=[SCALARS, WHOLE, IN_HBM, IN_HBM, ANY],
        out_specs=[WHOLE] * len(widths),
        scratch_shapes=scratch,
        compiler_params=params(5 + -(-depth * sum(widths) * 4 // MIB)),
        cost_estimate=SMALL,
    )(starts, features, in_hbm(gate_weight), in_hbm(up_weight), after)


def hidden_tail(rows, width):
    half = pl.cdiv(width // 2, 128) * 128
    return half if rows % 8 else 0


def activate_kernel(rows, widths, summed, *refs):
    near, out = refs[:-1], refs[-1]
    width = sum(widths)

    def pair(w, g):
        column = (2 * g + w) * width
        parts = []
        for part, wide in zip(near, widths):
            at = (2 * g + w) * wide
            parts.append(
                summed[:, column : column + wide] + part[:, at : at + wide].astype(jnp.float32)
            )
            column += wide
        return jnp.concatenate(parts, axis=1)

    for g in range(rows // 8):
        out[:, g * width : (g + 1) * width] = activate(pair(0, g), pair(1, g))
    if rows % 8:
        last = pair(0, rows // 8)
        value = activate(last[:4], last[4:]).astype(jnp.float32)
        half = hidden_tail(rows, width)
        right = jnp.concatenate([value[:, half:], jnp.zeros((4, 2 * half - width), jnp.float32)], axis=1)
        at = (rows // 8) * width
        out[:, at : at + half] = jnp.concatenate([value[:, :half], right], axis=0).astype(out.dtype)


def activate_packed(summed, near, rows, widths):
    width = sum(widths)
    return pl.pallas_call(
        functools.partial(activate_kernel, rows, widths),
        out_shape=jax.ShapeDtypeStruct(
            (8, (rows // 8) * width + hidden_tail(rows, width)), jnp.bfloat16
        ),
        in_specs=[WHOLE] * (1 + len(near)),
        out_specs=WHOLE,
        compiler_params=params(8),
        cost_estimate=SMALL,
    )(summed, *near)


def pack_rows(out, value):
    rows, width = value.shape
    for g in range(rows // 8):
        out[:, g * width : (g + 1) * width] = value[8 * g : 8 * g + 8].astype(out.dtype)
    piece = width // 8
    for r in range(rows // 8 * 8, rows):
        at = (rows // 8) * width + (r % 8) * piece
        row = jnp.concatenate(
            [value[r : r + 1, i * piece : (i + 1) * piece] for i in range(8)], axis=0
        )
        out[:, at : at + piece] = row.astype(out.dtype)


def unpack_rows(out, packed):
    rows, width = out.shape
    for g in range(rows // 8):
        out[8 * g : 8 * g + 8, :] = packed[:, g * width : (g + 1) * width]
    piece = width // 8
    for r in range(rows // 8 * 8, rows):
        at = (rows // 8) * width + (r % 8) * piece
        for i in range(8):
            out[r : r + 1, i * piece : (i + 1) * piece] = packed[i : i + 1, at : at + piece]


def down_kernel(first, rows, width, starts, *refs):
    blocks = starts.shape[0]
    hidden, refs = refs[:blocks], refs[blocks:]
    if not first:
        before, refs = refs[0], refs[1:]
    held, outs, (plain, total) = refs[0], refs[1:-2], refs[-2:]
    if first:
        total = outs[0]
    for b in range(blocks):
        for g in range(rows // 8):
            plain[8 * g : 8 * g + 8, :] = hidden[b][:, g * width : (g + 1) * width].astype(jnp.float32)
        if rows % 8:
            at, half = (rows // 8) * width, hidden_tail(rows, width)
            tail = hidden[b][:, at : at + half].astype(jnp.float32)
            plain[rows - 4 :, :half] = tail[:4]
            plain[rows - 4 :, half:] = tail[4:, : width - half]
        for row, tall in pieces_of(width, STEP):
            term = jnp.dot(
                plain[:, row : row + tall].astype(jnp.bfloat16),
                held[pl.ds(pl.multiple_of(starts[b] + row, 128), tall), :],
                preferred_element_type=jnp.float32,
            )
            if b == 0 and row == 0:
                total[...] = term if first else before[...] + term
            else:
                total[...] += term
    if not first:
        tall = rows // len(outs)
        for r, out in enumerate(outs):
            pack_rows(out, total[r * tall : (r + 1) * tall, :])


def down(hidden, starts, before, weight, rows, width, outs):
    columns = weight.shape[1]
    if before is None:
        shapes = [jax.ShapeDtypeStruct((rows, columns), jnp.float32)]
    else:
        packed = (8, rows // outs * columns // 8)
        shapes = [jax.ShapeDtypeStruct(packed, jnp.bfloat16 if r else jnp.float32) for r in range(outs)]
    carried = [] if before is None else [before]
    return pl.pallas_call(
        functools.partial(down_kernel, before is None, rows, width),
        out_shape=shapes,
        in_specs=[SCALARS] + [WHOLE] * (len(hidden) + len(carried) + 1),
        out_specs=[WHOLE] * len(shapes),
        scratch_shapes=[
            pltpu.VMEM((rows, width), jnp.float32),
            pltpu.VMEM((rows, columns), jnp.float32),
        ],
        compiler_params=params(8),
        cost_estimate=SMALL,
    )(starts, *hidden, *carried, in_vmem(weight))


def finish_kernel(*refs):
    terms, out, plain = refs[:-2], refs[-2], refs[-1]
    packed = terms[0][...]
    for term in terms[1:]:
        packed = packed + term[...].astype(jnp.float32)
    unpack_rows(plain, packed)
    out[...] = plain[...].astype(out.dtype)


def finish(terms, shape):
    return pl.pallas_call(
        finish_kernel,
        out_shape=jax.ShapeDtypeStruct(shape, jnp.bfloat16),
        in_specs=[WHOLE] * len(terms),
        out_specs=WHOLE,
        scratch_shapes=[pltpu.VMEM(shape, jnp.float32)],
        compiler_params=params(4),
        cost_estimate=SMALL,
    )(*terms)


def swap(value, axes, size, distance):
    return lax.ppermute(value, axes, [(i, i ^ distance) for i in range(size)])


def add(a, b):
    return a.astype(jnp.float32) + b.astype(jnp.float32)


def direct(tokens, gate_weight, up_weight, down_weight):
    n_gx = lax.axis_size("gx")
    n_token = lax.axis_size(TOKEN_AXES)
    me = lax.axis_index("gx")
    width = gate_weight.shape[1] // n_gx

    def starts_of(*distances):
        return jnp.stack([(me ^ d) * width for d in distances]).astype(jnp.int32)

    held = fetch(gate_weight, up_weight, starts_of(3), width)
    features = jnp.concatenate(
        [tokens] + [swap(tokens, TOKEN_AXES, n_token, r) for r in range(1, n_token)], axis=0
    )
    rows = features.shape[0]

    def blocks_for(starts, widths, after):
        return gate_up_stream(features, gate_weight, up_weight, starts, widths, after)

    ahead = width // 128 * 2 // 5 * 128
    relayed = gate_up_held(features, held)
    arrived = swap(relayed, "gx", n_gx, 1)
    across, beside = blocks_for(starts_of(2, 1), (width, ahead), relayed)
    across = lax.optimization_barrier(add(across, arrived).astype(jnp.bfloat16))
    far = swap(across, "gx", n_gx, 2)
    near = [swap(beside, "gx", n_gx, 1)]
    (beside,) = blocks_for(starts_of(1) + ahead, (width - ahead,), across)
    near.append(swap(beside, "gx", n_gx, 1))
    (own,) = blocks_for(starts_of(0), (width,), beside)
    summed = lax.optimization_barrier(add(own, far))
    hidden = activate_packed(summed, near, rows, (ahead, width - ahead))

    opposite = swap(hidden, "gx", n_gx, 2)
    first = [hidden, swap(hidden, "gx", n_gx, 1), opposite]
    second = [swap(opposite, "gx", n_gx, 1)]
    (partial_sum,) = down(first, starts_of(0, 1, 2), None, down_weight, rows, width, 1)
    outs = down(second, starts_of(3), partial_sum, down_weight, rows, width, n_token)
    terms = [outs[0]] + [swap(outs[r], TOKEN_AXES, n_token, r) for r in range(1, n_token)]
    return finish(terms, tokens.shape)


def offloaded(tokens, gate_weight, up_weight, down_weight):
    features = lax.all_gather(tokens, TOKEN_AXES, axis=0, tiled=True)
    hidden_width = gate_weight.shape[1]
    gate_part = jnp.dot(features, gate_weight, preferred_element_type=jnp.float32)
    up_part = jnp.dot(features, up_weight, preferred_element_type=jnp.float32)
    summed = lax.psum(
        jnp.concatenate([gate_part, up_part], axis=1).astype(jnp.bfloat16), "gx"
    ).astype(jnp.float32)
    hidden = activate(summed[:, :hidden_width], summed[:, hidden_width:])
    partial_value = jnp.dot(hidden, down_weight, preferred_element_type=jnp.float32)
    return lax.psum_scatter(
        partial_value.astype(jnp.bfloat16), TOKEN_AXES, scatter_dimension=0, tiled=True
    )


def shards(tokens, gate_weight, up_weight, down_weight):
    n_gx = lax.axis_size("gx")
    n_token = lax.axis_size(TOKEN_AXES)
    rows = tokens.shape[0] * n_token
    tokens_fit = n_token > 1 and n_token & (n_token - 1) == 0 and rows % 4 == 0
    weights_fit = gate_weight.shape[1] % (128 * 4) == 0 and gate_weight.shape[0] % STEP == 0
    columns_fit = down_weight.shape[1] % (128 * 8) == 0
    if n_gx == 4 and tokens_fit and weights_fit and columns_fit:
        return direct(tokens, gate_weight, up_weight, down_weight)
    return offloaded(tokens, gate_weight, up_weight, down_weight)


def solution(mesh):
    return jax.shard_map(
        shards,
        mesh=mesh,
        in_specs=(
            P(("grp", "gy", "gz"), "gx"),
            P("gx", ("gy", "gz")),
            P("gx", ("gy", "gz")),
            P(("gy", "gz"), "gx"),
        ),
        out_specs=P(("grp", "gy", "gz"), "gx"),
        check_vma=False,
    )
```

```python
import functools

import jax
import jax.numpy as jnp
from jax import lax
from jax.experimental import pallas as pl
from jax.experimental.pallas import tpu as pltpu
from jax.sharding import PartitionSpec as P

MIB = 1 << 20
STEP = 256
IN_FLIGHT = 8
TOKEN_AXES = ("gy", "gz")
IN_HBM = pl.BlockSpec(memory_space=pltpu.HBM)
ANY = pl.BlockSpec(memory_space=pl.ANY)
WHOLE = pl.BlockSpec(memory_space=pltpu.VMEM)
SCALARS = pl.BlockSpec(memory_space=pltpu.SMEM)


def activate(gate, up):
    return (jax.nn.silu(gate) * up).astype(jnp.bfloat16)


def pieces_of(total, step):
    return [(start, min(step, total - start)) for start in range(0, total, step)]


def in_hbm(value):
    return pltpu.with_memory_space_constraint(value, pltpu.HBM)


def in_vmem(value):
    return pltpu.with_memory_space_constraint(value, pltpu.VMEM)


SMALL = pl.CostEstimate(flops=0, bytes_accessed=MIB, transcendentals=0)


def params(mib):
    return pltpu.CompilerParams(vmem_limit_bytes=mib * MIB)


def packed_pair_width(rows, width):
    return (rows // 8) * 2 * width + (width if rows % 8 else 0)


def pack_pair(out, gate, up):
    rows, width = gate.shape
    for g in range(rows // 8):
        for w, value in enumerate((gate, up)):
            at = (2 * g + w) * width
            out[:, at : at + width] = value[8 * g : 8 * g + 8].astype(out.dtype)
    if rows % 8:
        at = (rows // 8) * 2 * width
        tail = jnp.concatenate([gate[rows - 4 :], up[rows - 4 :]], axis=0)
        out[:, at : at + width] = tail.astype(out.dtype)


def block_copies(width, start, weights, held, sems):
    columns = pl.ds(pl.multiple_of(start, 128), width)
    copies = []
    for k, (row, rows) in enumerate(pieces_of(held.shape[1], STEP)):
        for w, weight in enumerate(weights):
            copy = pltpu.make_async_copy(
                weight.at[pl.ds(row, rows), columns], held.at[w, pl.ds(row, rows)], sems.at[w, k]
            )
            copies.append((w, row, rows, copy))
    return copies


def fetch_kernel(width, start_ref, gate_ref, up_ref, held, sems):
    copies = block_copies(width, start_ref[0], (gate_ref, up_ref), held, sems)
    for _, _, _, copy in copies:
        copy.start()
    for _, _, _, copy in copies:
        copy.wait()


def fetch(gate_weight, up_weight, start, width):
    depth = gate_weight.shape[0]
    return pl.pallas_call(
        functools.partial(fetch_kernel, width),
        out_shape=pltpu.VMEM((2, depth, width), jnp.bfloat16),
        in_specs=[SCALARS, IN_HBM, IN_HBM],
        out_specs=WHOLE,
        scratch_shapes=[pltpu.SemaphoreType.DMA((2, len(pieces_of(depth, STEP))))],
        compiler_params=params(4),
        cost_estimate=SMALL,
    )(start, in_hbm(gate_weight), in_hbm(up_weight))


def multiply(x_ref, held, total, steps, waiting=()):
    for w, row, rows, copy in steps:
        if copy is not None:
            copy.wait()
        if waiting:
            waiting.pop(0).start()
        term = jnp.dot(
            x_ref[:, row : row + rows], held[w, row : row + rows, :], preferred_element_type=jnp.float32
        )
        if row == 0:
            total[w] = term
        else:
            total[w] += term


def held_kernel(x_ref, held, out, total):
    parts = pieces_of(x_ref.shape[1], STEP)
    multiply(x_ref, held, total, [(w, row, rows, None) for w in range(2) for row, rows in parts])
    pack_pair(out, total[0], total[1])


def gate_up_held(features, held):
    rows, width = features.shape[0], held.shape[2]
    return pl.pallas_call(
        held_kernel,
        out_shape=jax.ShapeDtypeStruct((8, packed_pair_width(rows, width)), jnp.bfloat16),
        in_specs=[WHOLE, WHOLE],
        out_specs=WHOLE,
        scratch_shapes=[pltpu.VMEM((2, rows, width), jnp.float32)],
        compiler_params=params(8),
        cost_estimate=SMALL,
    )(features, in_vmem(held))


def stream_kernel(width, blocks, starts, x_ref, gate_ref, up_ref, _, *refs):
    outs, refs = refs[: len(blocks)], refs[len(blocks) :]
    work = []
    for b, which in enumerate(blocks):
        held, total, sems = refs[3 * b : 3 * b + 3]
        weights = [(gate_ref, up_ref)[w] for w in which]
        copies = block_copies(width, starts[b], weights, held, sems)
        work.append((outs[b], held, total, copies))
    waiting = [step[-1] for block in work for step in block[-1]]
    in_flight = IN_FLIGHT if len(blocks) > 1 else len(waiting)
    for copy in waiting[:in_flight]:
        copy.start()
    waiting = waiting[in_flight:]
    for (out, held, total, copies), which in zip(work, blocks):
        multiply(x_ref, held, total, copies, waiting)
        if len(which) == 2:
            pack_pair(out, total[0], total[1])
        else:
            pack_single(out, total[0])


def gate_up_stream(features, gate_weight, up_weight, starts, blocks, width, after):
    rows, depth = features.shape
    scratch, shapes = [], []
    for which in blocks:
        packed = packed_pair_width(rows, width) if len(which) == 2 else packed_width(rows, width)
        shapes.append(jax.ShapeDtypeStruct((8, packed), jnp.bfloat16))
        scratch += [
            pltpu.VMEM((len(which), depth, width), jnp.bfloat16),
            pltpu.VMEM((len(which), rows, width), jnp.float32),
            pltpu.SemaphoreType.DMA((len(which), len(pieces_of(depth, STEP)))),
        ]
    held_mib = -(-depth * width * 2 * sum(len(which) for which in blocks) // MIB)
    return pl.pallas_call(
        functools.partial(stream_kernel, width, blocks),
        out_shape=shapes,
        in_specs=[SCALARS, WHOLE, IN_HBM, IN_HBM, ANY],
        out_specs=[WHOLE] * len(blocks),
        scratch_shapes=scratch,
        compiler_params=params(5 + held_mib),
        cost_estimate=SMALL,
    )(starts, features, in_hbm(gate_weight), in_hbm(up_weight), after)


def hidden_tail(rows, width):
    half = pl.cdiv(width // 2, 128) * 128
    return half if rows % 8 else 0


def packed_width(rows, width):
    return (rows // 8) * width + hidden_tail(rows, width)


def pack_single(out, value):
    rows, width = value.shape
    for g in range(rows // 8):
        out[:, g * width : (g + 1) * width] = value[8 * g : 8 * g + 8].astype(out.dtype)
    if rows % 8:
        at, half = (rows // 8) * width, hidden_tail(rows, width)
        left, right = value[rows - 4 :, :half], value[rows - 4 :, half:]
        if 2 * half > width:
            right = jnp.concatenate([right, jnp.zeros((4, 2 * half - width), jnp.float32)], axis=1)
        out[:, at : at + half] = jnp.concatenate([left, right], axis=0).astype(out.dtype)


def last_rows(packed, rows, width):
    at, half = (rows // 8) * width, hidden_tail(rows, width)
    tail = packed[:, at : at + half].astype(jnp.float32)
    return jnp.concatenate([tail[:4], tail[4:, : width - half]], axis=1)


def activate_kernel(rows, width, summed, gate_near, up_near, out):
    for g in range(rows // 8):
        near = slice(g * width, (g + 1) * width)
        gate, up = ((2 * g + w) * width for w in range(2))
        out[:, near] = activate(
            summed[:, gate : gate + width] + gate_near[:, near].astype(jnp.float32),
            summed[:, up : up + width] + up_near[:, near].astype(jnp.float32),
        )
    if rows % 8:
        at, half = (rows // 8) * 2 * width, hidden_tail(rows, width)
        value = activate(
            summed[:4, at : at + width] + last_rows(gate_near, rows, width),
            summed[4:, at : at + width] + last_rows(up_near, rows, width),
        ).astype(jnp.float32)
        right = jnp.concatenate([value[:, half:], jnp.zeros((4, 2 * half - width), jnp.float32)], axis=1)
        at = (rows // 8) * width
        out[:, at : at + half] = jnp.concatenate([value[:, :half], right], axis=0).astype(out.dtype)


def activate_packed(summed, near, rows, width):
    return pl.pallas_call(
        functools.partial(activate_kernel, rows, width),
        out_shape=jax.ShapeDtypeStruct((8, packed_width(rows, width)), jnp.bfloat16),
        in_specs=[WHOLE] * 3,
        out_specs=WHOLE,
        compiler_params=params(8),
        cost_estimate=SMALL,
    )(summed, *near)


def pack_rows(out, value):
    rows, width = value.shape
    for g in range(rows // 8):
        out[:, g * width : (g + 1) * width] = value[8 * g : 8 * g + 8].astype(out.dtype)
    piece = width // 8
    for r in range(rows // 8 * 8, rows):
        at = (rows // 8) * width + (r % 8) * piece
        row = jnp.concatenate(
            [value[r : r + 1, i * piece : (i + 1) * piece] for i in range(8)], axis=0
        )
        out[:, at : at + piece] = row.astype(out.dtype)


def unpack_rows(out, packed):
    rows, width = out.shape
    for g in range(rows // 8):
        out[8 * g : 8 * g + 8, :] = packed[:, g * width : (g + 1) * width]
    piece = width // 8
    for r in range(rows // 8 * 8, rows):
        at = (rows // 8) * width + (r % 8) * piece
        for i in range(8):
            out[r : r + 1, i * piece : (i + 1) * piece] = packed[i : i + 1, at : at + piece]


def down_kernel(first, rows, width, starts, *refs):
    blocks = starts.shape[0]
    hidden, refs = refs[:blocks], refs[blocks:]
    if not first:
        before, refs = refs[0], refs[1:]
    held, outs, (plain, total) = refs[0], refs[1:-2], refs[-2:]
    if first:
        total = outs[0]
    for b in range(blocks):
        for g in range(rows // 8):
            plain[8 * g : 8 * g + 8, :] = hidden[b][:, g * width : (g + 1) * width].astype(jnp.float32)
        if rows % 8:
            at, half = (rows // 8) * width, hidden_tail(rows, width)
            tail = hidden[b][:, at : at + half].astype(jnp.float32)
            plain[rows - 4 :, :half] = tail[:4]
            plain[rows - 4 :, half:] = tail[4:, : width - half]
        for row, tall in pieces_of(width, STEP):
            term = jnp.dot(
                plain[:, row : row + tall].astype(jnp.bfloat16),
                held[pl.ds(pl.multiple_of(starts[b] + row, 128), tall), :],
                preferred_element_type=jnp.float32,
            )
            if b == 0 and row == 0:
                total[...] = term if first else before[...] + term
            else:
                total[...] += term
    if not first:
        tall = rows // len(outs)
        for r, out in enumerate(outs):
            pack_rows(out, total[r * tall : (r + 1) * tall, :])


def down(hidden, starts, before, weight, rows, width, outs):
    columns = weight.shape[1]
    if before is None:
        shapes = [jax.ShapeDtypeStruct((rows, columns), jnp.float32)]
    else:
        packed = (8, rows // outs * columns // 8)
        shapes = [jax.ShapeDtypeStruct(packed, jnp.bfloat16 if r else jnp.float32) for r in range(outs)]
    carried = [] if before is None else [before]
    return pl.pallas_call(
        functools.partial(down_kernel, before is None, rows, width),
        out_shape=shapes,
        in_specs=[SCALARS] + [WHOLE] * (len(hidden) + len(carried) + 1),
        out_specs=[WHOLE] * len(shapes),
        scratch_shapes=[
            pltpu.VMEM((rows, width), jnp.float32),
            pltpu.VMEM((rows, columns), jnp.float32),
        ],
        compiler_params=params(8),
        cost_estimate=SMALL,
    )(starts, *hidden, *carried, in_vmem(weight))


def finish_kernel(*refs):
    terms, out, plain = refs[:-2], refs[-2], refs[-1]
    packed = terms[0][...]
    for term in terms[1:]:
        packed = packed + term[...].astype(jnp.float32)
    unpack_rows(plain, packed)
    out[...] = plain[...].astype(out.dtype)


def finish(terms, shape):
    return pl.pallas_call(
        finish_kernel,
        out_shape=jax.ShapeDtypeStruct(shape, jnp.bfloat16),
        in_specs=[WHOLE] * len(terms),
        out_specs=WHOLE,
        scratch_shapes=[pltpu.VMEM(shape, jnp.float32)],
        compiler_params=params(4),
        cost_estimate=SMALL,
    )(*terms)


def swap(value, axes, size, distance):
    return lax.ppermute(value, axes, [(i, i ^ distance) for i in range(size)])


def add(a, b):
    return a.astype(jnp.float32) + b.astype(jnp.float32)


def direct(tokens, gate_weight, up_weight, down_weight):
    n_gx = lax.axis_size("gx")
    n_token = lax.axis_size(TOKEN_AXES)
    me = lax.axis_index("gx")
    width = gate_weight.shape[1] // n_gx

    def starts_of(*distances):
        return jnp.stack([(me ^ d) * width for d in distances]).astype(jnp.int32)

    held = fetch(gate_weight, up_weight, starts_of(3), width)
    features = jnp.concatenate(
        [tokens] + [swap(tokens, TOKEN_AXES, n_token, r) for r in range(1, n_token)], axis=0
    )
    rows = features.shape[0]

    def blocks_for(starts, blocks, after):
        return gate_up_stream(features, gate_weight, up_weight, starts, blocks, width, after)

    relayed = gate_up_held(features, held)
    arrived = swap(relayed, "gx", n_gx, 1)
    across, beside = blocks_for(starts_of(2, 1), ((0, 1), (0,)), relayed)
    across = lax.optimization_barrier(add(across, arrived).astype(jnp.bfloat16))
    far = swap(across, "gx", n_gx, 2)
    near = [swap(beside, "gx", n_gx, 1)]
    (beside,) = blocks_for(starts_of(1), ((1,),), across)
    near.append(swap(beside, "gx", n_gx, 1))
    (own,) = blocks_for(starts_of(0), ((0, 1),), beside)
    summed = lax.optimization_barrier(add(own, far))
    hidden = activate_packed(summed, near, rows, width)

    opposite = swap(hidden, "gx", n_gx, 2)
    first = [hidden, swap(hidden, "gx", n_gx, 1), opposite]
    second = [swap(opposite, "gx", n_gx, 1)]
    (partial_sum,) = down(first, starts_of(0, 1, 2), None, down_weight, rows, width, 1)
    outs = down(second, starts_of(3), partial_sum, down_weight, rows, width, n_token)
    terms = [outs[0]] + [swap(outs[r], TOKEN_AXES, n_token, r) for r in range(1, n_token)]
    return finish(terms, tokens.shape)


def offloaded(tokens, gate_weight, up_weight, down_weight):
    features = lax.all_gather(tokens, TOKEN_AXES, axis=0, tiled=True)
    hidden_width = gate_weight.shape[1]
    gate_part = jnp.dot(features, gate_weight, preferred_element_type=jnp.float32)
    up_part = jnp.dot(features, up_weight, preferred_element_type=jnp.float32)
    summed = lax.psum(
        jnp.concatenate([gate_part, up_part], axis=1).astype(jnp.bfloat16), "gx"
    ).astype(jnp.float32)
    hidden = activate(summed[:, :hidden_width], summed[:, hidden_width:])
    partial_value = jnp.dot(hidden, down_weight, preferred_element_type=jnp.float32)
    return lax.psum_scatter(
        partial_value.astype(jnp.bfloat16), TOKEN_AXES, scatter_dimension=0, tiled=True
    )


def shards(tokens, gate_weight, up_weight, down_weight):
    n_gx = lax.axis_size("gx")
    n_token = lax.axis_size(TOKEN_AXES)
    rows = tokens.shape[0] * n_token
    tokens_fit = n_token > 1 and n_token & (n_token - 1) == 0 and rows % 4 == 0
    weights_fit = gate_weight.shape[1] % (128 * 4) == 0 and gate_weight.shape[0] % STEP == 0
    columns_fit = down_weight.shape[1] % (128 * 8) == 0
    if n_gx == 4 and tokens_fit and weights_fit and columns_fit:
        return direct(tokens, gate_weight, up_weight, down_weight)
    return offloaded(tokens, gate_weight, up_weight, down_weight)


def solution(mesh):
    return jax.shard_map(
        shards,
        mesh=mesh,
        in_specs=(
            P(("grp", "gy", "gz"), "gx"),
            P("gx", ("gy", "gz")),
            P("gx", ("gy", "gz")),
            P(("gy", "gz"), "gx"),
        ),
        out_specs=P(("grp", "gy", "gz"), "gx"),
        check_vma=False,
    )
```

```python
import functools

import jax
import jax.numpy as jnp
from jax import lax
from jax.experimental import pallas as pl
from jax.experimental.pallas import tpu as pltpu
from jax.sharding import PartitionSpec as P

MIB = 1 << 20
STEP = 256
COPY_STEP = 512
IN_FLIGHT = 6
TOKEN_AXES = ("gy", "gz")
IN_HBM = pl.BlockSpec(memory_space=pltpu.HBM)
ANY = pl.BlockSpec(memory_space=pl.ANY)
WHOLE = pl.BlockSpec(memory_space=pltpu.VMEM)
SCALARS = pl.BlockSpec(memory_space=pltpu.SMEM)


def activate(gate, up):
    return (jax.nn.silu(gate) * up).astype(jnp.bfloat16)


def pieces_of(total, step):
    return [(start, min(step, total - start)) for start in range(0, total, step)]


def in_hbm(value):
    return pltpu.with_memory_space_constraint(value, pltpu.HBM)


def in_vmem(value):
    return pltpu.with_memory_space_constraint(value, pltpu.VMEM)


SMALL = pl.CostEstimate(flops=0, bytes_accessed=MIB, transcendentals=0)


def params(mib):
    return pltpu.CompilerParams(vmem_limit_bytes=mib * MIB)


def packed_pair_width(rows, width):
    return (rows // 8) * 2 * width + (width if rows % 8 else 0)


def pack_pair(out, gate, up):
    rows, width = gate.shape
    for g in range(rows // 8):
        for w, value in enumerate((gate, up)):
            at = (2 * g + w) * width
            out[:, at : at + width] = value[8 * g : 8 * g + 8].astype(out.dtype)
    if rows % 8:
        at = (rows // 8) * 2 * width
        tail = jnp.concatenate([gate[rows - 4 :], up[rows - 4 :]], axis=0)
        out[:, at : at + width] = tail.astype(out.dtype)


def block_copies(width, start, weights, held, sems):
    columns = pl.ds(pl.multiple_of(start, 128), width)
    copies = []
    for k, (row, rows) in enumerate(pieces_of(held.shape[1], COPY_STEP)):
        for w, weight in enumerate(weights):
            copy = pltpu.make_async_copy(
                weight.at[pl.ds(row, rows), columns], held.at[w, pl.ds(row, rows)], sems.at[w, k]
            )
            copies.append((w, row, rows, copy))
    return copies


def fetch_kernel(width, start_ref, gate_ref, up_ref, held, sems):
    copies = block_copies(width, start_ref[0], (gate_ref, up_ref), held, sems)
    for _, _, _, copy in copies:
        copy.start()
    for _, _, _, copy in copies:
        copy.wait()


def fetch(gate_weight, up_weight, start, width):
    depth = gate_weight.shape[0]
    return pl.pallas_call(
        functools.partial(fetch_kernel, width),
        out_shape=pltpu.VMEM((2, depth, width), jnp.bfloat16),
        in_specs=[SCALARS, IN_HBM, IN_HBM],
        out_specs=WHOLE,
        scratch_shapes=[pltpu.SemaphoreType.DMA((2, len(pieces_of(depth, COPY_STEP))))],
        compiler_params=params(4),
        cost_estimate=SMALL,
    )(start, in_hbm(gate_weight), in_hbm(up_weight))


def multiply(x_ref, held, total, steps, waiting=()):
    for w, first, tall, copy in steps:
        if copy is not None:
            copy.wait()
        if waiting:
            waiting.pop(0).start()
        for row, rows in pieces_of(tall, STEP):
            rows = slice(first + row, first + row + rows)
            term = jnp.dot(x_ref[:, rows], held[w, rows, :], preferred_element_type=jnp.float32)
            if rows.start == 0:
                total[w] = term
            else:
                total[w] += term


def held_kernel(x_ref, held, out, total):
    parts = pieces_of(x_ref.shape[1], STEP)
    multiply(x_ref, held, total, [(w, row, rows, None) for w in range(2) for row, rows in parts])
    pack_pair(out, total[0], total[1])


def gate_up_held(features, held):
    rows, width = features.shape[0], held.shape[2]
    return pl.pallas_call(
        held_kernel,
        out_shape=jax.ShapeDtypeStruct((8, packed_pair_width(rows, width)), jnp.bfloat16),
        in_specs=[WHOLE, WHOLE],
        out_specs=WHOLE,
        scratch_shapes=[pltpu.VMEM((2, rows, width), jnp.float32)],
        compiler_params=params(8),
        cost_estimate=SMALL,
    )(features, in_vmem(held))


def stream_kernel(width, blocks, starts, x_ref, gate_ref, up_ref, _, *refs):
    outs, refs = refs[: len(blocks)], refs[len(blocks) :]
    work = []
    for b, which in enumerate(blocks):
        held, total, sems = refs[3 * b : 3 * b + 3]
        weights = [(gate_ref, up_ref)[w] for w in which]
        copies = block_copies(width, starts[b], weights, held, sems)
        work.append((outs[b], held, total, copies))
    waiting = [step[-1] for block in work for step in block[-1]]
    in_flight = IN_FLIGHT if len(blocks) > 1 else len(waiting)
    for copy in waiting[:in_flight]:
        copy.start()
    waiting = waiting[in_flight:]
    for (out, held, total, copies), which in zip(work, blocks):
        multiply(x_ref, held, total, copies, waiting)
        if len(which) == 2:
            pack_pair(out, total[0], total[1])
        else:
            pack_single(out, total[0])


def gate_up_stream(features, gate_weight, up_weight, starts, blocks, width, after):
    rows, depth = features.shape
    scratch, shapes = [], []
    for which in blocks:
        packed = packed_pair_width(rows, width) if len(which) == 2 else packed_width(rows, width)
        shapes.append(jax.ShapeDtypeStruct((8, packed), jnp.bfloat16))
        scratch += [
            pltpu.VMEM((len(which), depth, width), jnp.bfloat16),
            pltpu.VMEM((len(which), rows, width), jnp.float32),
            pltpu.SemaphoreType.DMA((len(which), len(pieces_of(depth, COPY_STEP)))),
        ]
    held_mib = -(-depth * width * 2 * sum(len(which) for which in blocks) // MIB)
    return pl.pallas_call(
        functools.partial(stream_kernel, width, blocks),
        out_shape=shapes,
        in_specs=[SCALARS, WHOLE, IN_HBM, IN_HBM, ANY],
        out_specs=[WHOLE] * len(blocks),
        scratch_shapes=scratch,
        compiler_params=params(5 + held_mib),
        cost_estimate=SMALL,
    )(starts, features, in_hbm(gate_weight), in_hbm(up_weight), after)


def hidden_tail(rows, width):
    half = pl.cdiv(width // 2, 128) * 128
    return half if rows % 8 else 0


def packed_width(rows, width):
    return (rows // 8) * width + hidden_tail(rows, width)


def pack_single(out, value):
    rows, width = value.shape
    for g in range(rows // 8):
        out[:, g * width : (g + 1) * width] = value[8 * g : 8 * g + 8].astype(out.dtype)
    if rows % 8:
        at, half = (rows // 8) * width, hidden_tail(rows, width)
        left, right = value[rows - 4 :, :half], value[rows - 4 :, half:]
        if 2 * half > width:
            right = jnp.concatenate([right, jnp.zeros((4, 2 * half - width), jnp.float32)], axis=1)
        out[:, at : at + half] = jnp.concatenate([left, right], axis=0).astype(out.dtype)


def last_rows(packed, rows, width):
    at, half = (rows // 8) * width, hidden_tail(rows, width)
    tail = packed[:, at : at + half].astype(jnp.float32)
    return jnp.concatenate([tail[:4], tail[4:, : width - half]], axis=1)


def activate_kernel(rows, width, summed, gate_near, up_near, out):
    for g in range(rows // 8):
        near = slice(g * width, (g + 1) * width)
        gate, up = ((2 * g + w) * width for w in range(2))
        out[:, near] = activate(
            summed[:, gate : gate + width] + gate_near[:, near].astype(jnp.float32),
            summed[:, up : up + width] + up_near[:, near].astype(jnp.float32),
        )
    if rows % 8:
        at, half = (rows // 8) * 2 * width, hidden_tail(rows, width)
        value = activate(
            summed[:4, at : at + width] + last_rows(gate_near, rows, width),
            summed[4:, at : at + width] + last_rows(up_near, rows, width),
        ).astype(jnp.float32)
        right = jnp.concatenate([value[:, half:], jnp.zeros((4, 2 * half - width), jnp.float32)], axis=1)
        at = (rows // 8) * width
        out[:, at : at + half] = jnp.concatenate([value[:, :half], right], axis=0).astype(out.dtype)


def activate_packed(summed, near, rows, width):
    return pl.pallas_call(
        functools.partial(activate_kernel, rows, width),
        out_shape=jax.ShapeDtypeStruct((8, packed_width(rows, width)), jnp.bfloat16),
        in_specs=[WHOLE] * 3,
        out_specs=WHOLE,
        compiler_params=params(8),
        cost_estimate=SMALL,
    )(summed, *near)


def pack_rows(out, value):
    rows, width = value.shape
    for g in range(rows // 8):
        out[:, g * width : (g + 1) * width] = value[8 * g : 8 * g + 8].astype(out.dtype)
    piece = width // 8
    for r in range(rows // 8 * 8, rows):
        at = (rows // 8) * width + (r % 8) * piece
        row = jnp.concatenate(
            [value[r : r + 1, i * piece : (i + 1) * piece] for i in range(8)], axis=0
        )
        out[:, at : at + piece] = row.astype(out.dtype)


def unpack_rows(out, packed):
    rows, width = out.shape
    for g in range(rows // 8):
        out[8 * g : 8 * g + 8, :] = packed[:, g * width : (g + 1) * width]
    piece = width // 8
    for r in range(rows // 8 * 8, rows):
        at = (rows // 8) * width + (r % 8) * piece
        for i in range(8):
            out[r : r + 1, i * piece : (i + 1) * piece] = packed[i : i + 1, at : at + piece]


def down_kernel(first, rows, width, starts, *refs):
    blocks = starts.shape[0]
    hidden, refs = refs[:blocks], refs[blocks:]
    if not first:
        before, refs = refs[0], refs[1:]
    held, outs, (plain, total) = refs[0], refs[1:-2], refs[-2:]
    if first:
        total = outs[0]
    for b in range(blocks):
        for g in range(rows // 8):
            plain[8 * g : 8 * g + 8, :] = hidden[b][:, g * width : (g + 1) * width].astype(jnp.float32)
        if rows % 8:
            at, half = (rows // 8) * width, hidden_tail(rows, width)
            tail = hidden[b][:, at : at + half].astype(jnp.float32)
            plain[rows - 4 :, :half] = tail[:4]
            plain[rows - 4 :, half:] = tail[4:, : width - half]
        for row, tall in pieces_of(width, STEP):
            term = jnp.dot(
                plain[:, row : row + tall].astype(jnp.bfloat16),
                held[pl.ds(pl.multiple_of(starts[b] + row, 128), tall), :],
                preferred_element_type=jnp.float32,
            )
            if b == 0 and row == 0:
                total[...] = term if first else before[...] + term
            else:
                total[...] += term
    if not first:
        tall = rows // len(outs)
        for r, out in enumerate(outs):
            pack_rows(out, total[r * tall : (r + 1) * tall, :])


def down(hidden, starts, before, weight, rows, width, outs):
    columns = weight.shape[1]
    if before is None:
        shapes = [jax.ShapeDtypeStruct((rows, columns), jnp.float32)]
    else:
        packed = (8, rows // outs * columns // 8)
        shapes = [jax.ShapeDtypeStruct(packed, jnp.bfloat16 if r else jnp.float32) for r in range(outs)]
    carried = [] if before is None else [before]
    return pl.pallas_call(
        functools.partial(down_kernel, before is None, rows, width),
        out_shape=shapes,
        in_specs=[SCALARS] + [WHOLE] * (len(hidden) + len(carried) + 1),
        out_specs=[WHOLE] * len(shapes),
        scratch_shapes=[
            pltpu.VMEM((rows, width), jnp.float32),
            pltpu.VMEM((rows, columns), jnp.float32),
        ],
        compiler_params=params(8),
        cost_estimate=SMALL,
    )(starts, *hidden, *carried, in_vmem(weight))


def finish_kernel(*refs):
    terms, out, plain = refs[:-2], refs[-2], refs[-1]
    packed = terms[0][...]
    for term in terms[1:]:
        packed = packed + term[...].astype(jnp.float32)
    unpack_rows(plain, packed)
    out[...] = plain[...].astype(out.dtype)


def finish(terms, shape):
    return pl.pallas_call(
        finish_kernel,
        out_shape=jax.ShapeDtypeStruct(shape, jnp.bfloat16),
        in_specs=[WHOLE] * len(terms),
        out_specs=WHOLE,
        scratch_shapes=[pltpu.VMEM(shape, jnp.float32)],
        compiler_params=params(4),
        cost_estimate=SMALL,
    )(*terms)


def swap(value, axes, size, distance):
    return lax.ppermute(value, axes, [(i, i ^ distance) for i in range(size)])


def add(a, b):
    return a.astype(jnp.float32) + b.astype(jnp.float32)


def direct(tokens, gate_weight, up_weight, down_weight):
    n_gx = lax.axis_size("gx")
    n_token = lax.axis_size(TOKEN_AXES)
    me = lax.axis_index("gx")
    width = gate_weight.shape[1] // n_gx

    def starts_of(*distances):
        return jnp.stack([(me ^ d) * width for d in distances]).astype(jnp.int32)

    held = fetch(gate_weight, up_weight, starts_of(3), width)
    features = jnp.concatenate(
        [tokens] + [swap(tokens, TOKEN_AXES, n_token, r) for r in range(1, n_token)], axis=0
    )
    rows = features.shape[0]

    def blocks_for(starts, blocks, after):
        return gate_up_stream(features, gate_weight, up_weight, starts, blocks, width, after)

    relayed = gate_up_held(features, held)
    arrived = swap(relayed, "gx", n_gx, 1)
    across, beside = blocks_for(starts_of(2, 1), ((0, 1), (0,)), relayed)
    across = lax.optimization_barrier(add(across, arrived).astype(jnp.bfloat16))
    far = swap(across, "gx", n_gx, 2)
    near = [swap(beside, "gx", n_gx, 1)]
    (beside,) = blocks_for(starts_of(1), ((1,),), across)
    near.append(swap(beside, "gx", n_gx, 1))
    (own,) = blocks_for(starts_of(0), ((0, 1),), beside)
    summed = lax.optimization_barrier(add(own, far))
    hidden = activate_packed(summed, near, rows, width)

    opposite = swap(hidden, "gx", n_gx, 2)
    first = [hidden, swap(hidden, "gx", n_gx, 1), opposite]
    second = [swap(opposite, "gx", n_gx, 1)]
    (partial_sum,) = down(first, starts_of(0, 1, 2), None, down_weight, rows, width, 1)
    outs = down(second, starts_of(3), partial_sum, down_weight, rows, width, n_token)
    terms = [outs[0]] + [swap(outs[r], TOKEN_AXES, n_token, r) for r in range(1, n_token)]
    return finish(terms, tokens.shape)


def offloaded(tokens, gate_weight, up_weight, down_weight):
    features = lax.all_gather(tokens, TOKEN_AXES, axis=0, tiled=True)
    hidden_width = gate_weight.shape[1]
    gate_part = jnp.dot(features, gate_weight, preferred_element_type=jnp.float32)
    up_part = jnp.dot(features, up_weight, preferred_element_type=jnp.float32)
    summed = lax.psum(
        jnp.concatenate([gate_part, up_part], axis=1).astype(jnp.bfloat16), "gx"
    ).astype(jnp.float32)
    hidden = activate(summed[:, :hidden_width], summed[:, hidden_width:])
    partial_value = jnp.dot(hidden, down_weight, preferred_element_type=jnp.float32)
    return lax.psum_scatter(
        partial_value.astype(jnp.bfloat16), TOKEN_AXES, scatter_dimension=0, tiled=True
    )


def shards(tokens, gate_weight, up_weight, down_weight):
    n_gx = lax.axis_size("gx")
    n_token = lax.axis_size(TOKEN_AXES)
    rows = tokens.shape[0] * n_token
    tokens_fit = n_token > 1 and n_token & (n_token - 1) == 0 and rows % 4 == 0
    weights_fit = gate_weight.shape[1] % (128 * 4) == 0 and gate_weight.shape[0] % STEP == 0
    columns_fit = down_weight.shape[1] % (128 * 8) == 0
    if n_gx == 4 and tokens_fit and weights_fit and columns_fit:
        return direct(tokens, gate_weight, up_weight, down_weight)
    return offloaded(tokens, gate_weight, up_weight, down_weight)


def solution(mesh):
    return jax.shard_map(
        shards,
        mesh=mesh,
        in_specs=(
            P(("grp", "gy", "gz"), "gx"),
            P("gx", ("gy", "gz")),
            P("gx", ("gy", "gz")),
            P(("gy", "gz"), "gx"),
        ),
        out_specs=P(("grp", "gy", "gz"), "gx"),
        check_vma=False,
    )
```

```python
import functools

import jax
import jax.numpy as jnp
from jax import lax
from jax.experimental import pallas as pl
from jax.experimental.pallas import tpu as pltpu
from jax.sharding import PartitionSpec as P

MIB = 1 << 20
STEP = 256
COPY_STEP = 512
IN_FLIGHT = 6
TOKEN_AXES = ("gy", "gz")
IN_HBM = pl.BlockSpec(memory_space=pltpu.HBM)
ANY = pl.BlockSpec(memory_space=pl.ANY)
WHOLE = pl.BlockSpec(memory_space=pltpu.VMEM)
SCALARS = pl.BlockSpec(memory_space=pltpu.SMEM)


def activate(gate, up):
    return (jax.nn.silu(gate) * up).astype(jnp.bfloat16)


def pieces_of(total, step):
    return [(start, min(step, total - start)) for start in range(0, total, step)]


def in_hbm(value):
    return pltpu.with_memory_space_constraint(value, pltpu.HBM)


def in_vmem(value):
    return pltpu.with_memory_space_constraint(value, pltpu.VMEM)


SMALL = pl.CostEstimate(flops=0, bytes_accessed=MIB, transcendentals=0)


def params(mib):
    return pltpu.CompilerParams(vmem_limit_bytes=mib * MIB)


def packed_pair_width(rows, width):
    return (rows // 8) * 2 * width + (width if rows % 8 else 0)


def pack_pair(out, gate, up):
    rows, width = gate.shape
    for g in range(rows // 8):
        for w, value in enumerate((gate, up)):
            at = (2 * g + w) * width
            out[:, at : at + width] = value[8 * g : 8 * g + 8].astype(out.dtype)
    if rows % 8:
        at = (rows // 8) * 2 * width
        tail = jnp.concatenate([gate[rows - 4 :], up[rows - 4 :]], axis=0)
        out[:, at : at + width] = tail.astype(out.dtype)


def block_copies(width, start, weights, first, held, sems):
    columns = pl.ds(pl.multiple_of(start, 128), width)
    copies = []
    for k, (row, rows) in enumerate(pieces_of(held.shape[1], COPY_STEP)):
        for w, weight in enumerate(weights):
            copy = pltpu.make_async_copy(
                weight.at[pl.ds(first + row, rows), columns],
                held.at[w, pl.ds(row, rows)],
                sems.at[w, k],
            )
            copies.append((w, row, rows, copy))
    return copies


def copy_sems(weights, depth):
    return pltpu.SemaphoreType.DMA((weights, len(pieces_of(depth, COPY_STEP))))


def fetch_kernel(width, start_ref, gate_ref, up_ref, held, sems):
    copies = block_copies(width, start_ref[0], (gate_ref, up_ref), 0, held, sems)
    for _, _, _, copy in copies:
        copy.start()
    for _, _, _, copy in copies:
        copy.wait()


def fetch(gate_weight, up_weight, start, width):
    depth = gate_weight.shape[0]
    return pl.pallas_call(
        functools.partial(fetch_kernel, width),
        out_shape=pltpu.VMEM((2, depth, width), jnp.bfloat16),
        in_specs=[SCALARS, IN_HBM, IN_HBM],
        out_specs=WHOLE,
        scratch_shapes=[copy_sems(2, depth)],
        compiler_params=params(4),
        cost_estimate=SMALL,
    )(start, in_hbm(gate_weight), in_hbm(up_weight))


def multiply(x_ref, first, held, total, steps, waiting=()):
    for w, top, tall, copy in steps:
        if copy is not None:
            copy.wait()
        if waiting:
            waiting.pop(0).start()
        for row, rows in pieces_of(tall, STEP):
            at, rows = first + top + row, slice(top + row, top + row + rows)
            term = jnp.dot(
                x_ref[:, at : at + rows.stop - rows.start],
                held[w, rows, :],
                preferred_element_type=jnp.float32,
            )
            if at == 0:
                total[w] = term
            else:
                total[w] += term


def held_steps(held):
    return [(w, row, rows, None) for row, rows in pieces_of(held.shape[1], STEP) for w in range(2)]


def held_kernel(width, start_ref, x_ref, held, gate_ref, up_ref, out, ahead, total, sems):
    copies = block_copies(width, start_ref[0], (gate_ref, up_ref), 0, ahead, sems)
    for _, _, _, copy in copies:
        copy.start()
    multiply(x_ref, 0, held, total, held_steps(held))
    pack_pair(out, total[0], total[1])
    for _, _, _, copy in copies:
        copy.wait()


def gate_up_held(features, held, gate_weight, up_weight, start, ahead):
    rows, width = features.shape[0], held.shape[2]
    return pl.pallas_call(
        functools.partial(held_kernel, width),
        out_shape=(
            jax.ShapeDtypeStruct((8, packed_pair_width(rows, width)), jnp.bfloat16),
            pltpu.VMEM((2, ahead, width), jnp.bfloat16),
        ),
        in_specs=[SCALARS, WHOLE, WHOLE, IN_HBM, IN_HBM],
        out_specs=(WHOLE, WHOLE),
        scratch_shapes=[pltpu.VMEM((2, rows, width), jnp.float32), copy_sems(2, ahead)],
        compiler_params=params(8),
        cost_estimate=SMALL,
    )(start, features, in_vmem(held), in_hbm(gate_weight), in_hbm(up_weight))


def stream_kernel(width, blocks, has_held, starts, x_ref, *refs):
    refs = list(refs)
    held_top = refs.pop(0) if has_held else None
    gate_ref, up_ref, _ = refs[:3]
    outs, refs = refs[3 : 3 + len(blocks)], refs[3 + len(blocks) :]
    work = []
    for b, which in enumerate(blocks):
        held, total, sems = refs[3 * b : 3 * b + 3]
        weights = [(gate_ref, up_ref)[w] for w in which]
        first = x_ref.shape[1] - held.shape[1]
        copies = block_copies(width, starts[b], weights, first, held, sems)
        work.append((outs[b], first, held, total, copies))
    waiting = [step[-1] for block in work for step in block[-1]]
    in_flight = IN_FLIGHT if len(blocks) > 1 else len(waiting)
    for copy in waiting[:in_flight]:
        copy.start()
    waiting = waiting[in_flight:]
    if has_held:
        multiply(x_ref, 0, held_top, work[0][3], held_steps(held_top))
    for (out, first, held, total, copies), which in zip(work, blocks):
        multiply(x_ref, first, held, total, copies, waiting)
        if len(which) == 2:
            pack_pair(out, total[0], total[1])
        else:
            pack_single(out, total[0])


def gate_up_stream(features, gate_weight, up_weight, starts, blocks, width, after, held=None):
    rows, depth = features.shape
    scratch, shapes, held_bytes = [], [], 0
    for b, which in enumerate(blocks):
        packed = packed_pair_width(rows, width) if len(which) == 2 else packed_width(rows, width)
        shapes.append(jax.ShapeDtypeStruct((8, packed), jnp.bfloat16))
        below = depth - (held.shape[1] if held is not None and b == 0 else 0)
        held_bytes += len(which) * below * width * 2
        scratch += [
            pltpu.VMEM((len(which), below, width), jnp.bfloat16),
            pltpu.VMEM((len(which), rows, width), jnp.float32),
            copy_sems(len(which), below),
        ]
    before = [] if held is None else [in_vmem(held)]
    return pl.pallas_call(
        functools.partial(stream_kernel, width, blocks, held is not None),
        out_shape=shapes,
        in_specs=[SCALARS, WHOLE] + [WHOLE] * len(before) + [IN_HBM, IN_HBM, ANY],
        out_specs=[WHOLE] * len(blocks),
        scratch_shapes=scratch,
        compiler_params=params(5 + -(-held_bytes // MIB)),
        cost_estimate=SMALL,
    )(starts, features, *before, in_hbm(gate_weight), in_hbm(up_weight), after)


def hidden_tail(rows, width):
    half = pl.cdiv(width // 2, 128) * 128
    return half if rows % 8 else 0


def packed_width(rows, width):
    return (rows // 8) * width + hidden_tail(rows, width)


def pack_single(out, value):
    rows, width = value.shape
    for g in range(rows // 8):
        out[:, g * width : (g + 1) * width] = value[8 * g : 8 * g + 8].astype(out.dtype)
    if rows % 8:
        at, half = (rows // 8) * width, hidden_tail(rows, width)
        left, right = value[rows - 4 :, :half], value[rows - 4 :, half:]
        if 2 * half > width:
            right = jnp.concatenate([right, jnp.zeros((4, 2 * half - width), jnp.float32)], axis=1)
        out[:, at : at + half] = jnp.concatenate([left, right], axis=0).astype(out.dtype)


def last_rows(packed, rows, width):
    at, half = (rows // 8) * width, hidden_tail(rows, width)
    tail = packed[:, at : at + half].astype(jnp.float32)
    return jnp.concatenate([tail[:4], tail[4:, : width - half]], axis=1)


def activate_kernel(rows, width, summed, gate_near, up_near, out):
    for g in range(rows // 8):
        near = slice(g * width, (g + 1) * width)
        gate, up = ((2 * g + w) * width for w in range(2))
        out[:, near] = activate(
            summed[:, gate : gate + width] + gate_near[:, near].astype(jnp.float32),
            summed[:, up : up + width] + up_near[:, near].astype(jnp.float32),
        )
    if rows % 8:
        at, half = (rows // 8) * 2 * width, hidden_tail(rows, width)
        value = activate(
            summed[:4, at : at + width] + last_rows(gate_near, rows, width),
            summed[4:, at : at + width] + last_rows(up_near, rows, width),
        ).astype(jnp.float32)
        right = jnp.concatenate([value[:, half:], jnp.zeros((4, 2 * half - width), jnp.float32)], axis=1)
        at = (rows // 8) * width
        out[:, at : at + half] = jnp.concatenate([value[:, :half], right], axis=0).astype(out.dtype)


def activate_packed(summed, near, rows, width):
    return pl.pallas_call(
        functools.partial(activate_kernel, rows, width),
        out_shape=jax.ShapeDtypeStruct((8, packed_width(rows, width)), jnp.bfloat16),
        in_specs=[WHOLE] * 3,
        out_specs=WHOLE,
        compiler_params=params(8),
        cost_estimate=SMALL,
    )(summed, *near)


def pack_rows(out, value):
    rows, width = value.shape
    for g in range(rows // 8):
        out[:, g * width : (g + 1) * width] = value[8 * g : 8 * g + 8].astype(out.dtype)
    piece = width // 8
    for r in range(rows // 8 * 8, rows):
        at = (rows // 8) * width + (r % 8) * piece
        row = jnp.concatenate(
            [value[r : r + 1, i * piece : (i + 1) * piece] for i in range(8)], axis=0
        )
        out[:, at : at + piece] = row.astype(out.dtype)


def unpack_rows(out, packed):
    rows, width = out.shape
    for g in range(rows // 8):
        out[8 * g : 8 * g + 8, :] = packed[:, g * width : (g + 1) * width]
    piece = width // 8
    for r in range(rows // 8 * 8, rows):
        at = (rows // 8) * width + (r % 8) * piece
        for i in range(8):
            out[r : r + 1, i * piece : (i + 1) * piece] = packed[i : i + 1, at : at + piece]


def down_kernel(first, rows, width, starts, *refs):
    blocks = starts.shape[0]
    hidden, refs = refs[:blocks], refs[blocks:]
    if not first:
        before, refs = refs[0], refs[1:]
    held, outs, (plain, total) = refs[0], refs[1:-2], refs[-2:]
    if first:
        total = outs[0]
    for b in range(blocks):
        for g in range(rows // 8):
            plain[8 * g : 8 * g + 8, :] = hidden[b][:, g * width : (g + 1) * width].astype(jnp.float32)
        if rows % 8:
            at, half = (rows // 8) * width, hidden_tail(rows, width)
            tail = hidden[b][:, at : at + half].astype(jnp.float32)
            plain[rows - 4 :, :half] = tail[:4]
            plain[rows - 4 :, half:] = tail[4:, : width - half]
        for row, tall in pieces_of(width, STEP):
            term = jnp.dot(
                plain[:, row : row + tall].astype(jnp.bfloat16),
                held[pl.ds(pl.multiple_of(starts[b] + row, 128), tall), :],
                preferred_element_type=jnp.float32,
            )
            if b == 0 and row == 0:
                total[...] = term if first else before[...] + term
            else:
                total[...] += term
    if not first:
        tall = rows // len(outs)
        for r, out in enumerate(outs):
            pack_rows(out, total[r * tall : (r + 1) * tall, :])


def down(hidden, starts, before, weight, rows, width, outs):
    columns = weight.shape[1]
    if before is None:
        shapes = [jax.ShapeDtypeStruct((rows, columns), jnp.float32)]
    else:
        packed = (8, rows // outs * columns // 8)
        shapes = [jax.ShapeDtypeStruct(packed, jnp.bfloat16 if r else jnp.float32) for r in range(outs)]
    carried = [] if before is None else [before]
    return pl.pallas_call(
        functools.partial(down_kernel, before is None, rows, width),
        out_shape=shapes,
        in_specs=[SCALARS] + [WHOLE] * (len(hidden) + len(carried) + 1),
        out_specs=[WHOLE] * len(shapes),
        scratch_shapes=[
            pltpu.VMEM((rows, width), jnp.float32),
            pltpu.VMEM((rows, columns), jnp.float32),
        ],
        compiler_params=params(8),
        cost_estimate=SMALL,
    )(starts, *hidden, *carried, in_vmem(weight))


def finish_kernel(*refs):
    terms, out, plain = refs[:-2], refs[-2], refs[-1]
    packed = terms[0][...]
    for term in terms[1:]:
        packed = packed + term[...].astype(jnp.float32)
    unpack_rows(plain, packed)
    out[...] = plain[...].astype(out.dtype)


def finish(terms, shape):
    return pl.pallas_call(
        finish_kernel,
        out_shape=jax.ShapeDtypeStruct(shape, jnp.bfloat16),
        in_specs=[WHOLE] * len(terms),
        out_specs=WHOLE,
        scratch_shapes=[pltpu.VMEM(shape, jnp.float32)],
        compiler_params=params(4),
        cost_estimate=SMALL,
    )(*terms)


def swap(value, axes, size, distance):
    return lax.ppermute(value, axes, [(i, i ^ distance) for i in range(size)])


def add(a, b):
    return a.astype(jnp.float32) + b.astype(jnp.float32)


def direct(tokens, gate_weight, up_weight, down_weight):
    n_gx = lax.axis_size("gx")
    n_token = lax.axis_size(TOKEN_AXES)
    me = lax.axis_index("gx")
    width = gate_weight.shape[1] // n_gx

    def starts_of(*distances):
        return jnp.stack([(me ^ d) * width for d in distances]).astype(jnp.int32)

    held = fetch(gate_weight, up_weight, starts_of(3), width)
    features = jnp.concatenate(
        [tokens] + [swap(tokens, TOKEN_AXES, n_token, r) for r in range(1, n_token)], axis=0
    )
    rows = features.shape[0]

    def blocks_for(starts, blocks, after, held=None):
        return gate_up_stream(features, gate_weight, up_weight, starts, blocks, width, after, held)

    ahead = gate_weight.shape[0] // 4 // STEP * STEP
    relayed, held = gate_up_held(features, held, gate_weight, up_weight, starts_of(2), ahead)
    arrived = swap(relayed, "gx", n_gx, 1)
    across, beside = blocks_for(starts_of(2, 1), ((0, 1), (0,)), relayed, held)
    across = lax.optimization_barrier(add(across, arrived).astype(jnp.bfloat16))
    far = swap(across, "gx", n_gx, 2)
    near = [swap(beside, "gx", n_gx, 1)]
    (beside,) = blocks_for(starts_of(1), ((1,),), across)
    near.append(swap(beside, "gx", n_gx, 1))
    (own,) = blocks_for(starts_of(0), ((0, 1),), beside)
    summed = lax.optimization_barrier(add(own, far))
    hidden = activate_packed(summed, near, rows, width)

    opposite = swap(hidden, "gx", n_gx, 2)
    first = [hidden, swap(hidden, "gx", n_gx, 1), opposite]
    second = [swap(opposite, "gx", n_gx, 1)]
    (partial_sum,) = down(first, starts_of(0, 1, 2), None, down_weight, rows, width, 1)
    outs = down(second, starts_of(3), partial_sum, down_weight, rows, width, n_token)
    terms = [outs[0]] + [swap(outs[r], TOKEN_AXES, n_token, r) for r in range(1, n_token)]
    return finish(terms, tokens.shape)


def offloaded(tokens, gate_weight, up_weight, down_weight):
    features = lax.all_gather(tokens, TOKEN_AXES, axis=0, tiled=True)
    hidden_width = gate_weight.shape[1]
    gate_part = jnp.dot(features, gate_weight, preferred_element_type=jnp.float32)
    up_part = jnp.dot(features, up_weight, preferred_element_type=jnp.float32)
    summed = lax.psum(
        jnp.concatenate([gate_part, up_part], axis=1).astype(jnp.bfloat16), "gx"
    ).astype(jnp.float32)
    hidden = activate(summed[:, :hidden_width], summed[:, hidden_width:])
    partial_value = jnp.dot(hidden, down_weight, preferred_element_type=jnp.float32)
    return lax.psum_scatter(
        partial_value.astype(jnp.bfloat16), TOKEN_AXES, scatter_dimension=0, tiled=True
    )


def shards(tokens, gate_weight, up_weight, down_weight):
    n_gx = lax.axis_size("gx")
    n_token = lax.axis_size(TOKEN_AXES)
    rows = tokens.shape[0] * n_token
    tokens_fit = n_token > 1 and n_token & (n_token - 1) == 0 and rows % 4 == 0
    weights_fit = gate_weight.shape[1] % (128 * 4) == 0 and gate_weight.shape[0] % (4 * STEP) == 0
    columns_fit = down_weight.shape[1] % (128 * 8) == 0
    if n_gx == 4 and tokens_fit and weights_fit and columns_fit:
        return direct(tokens, gate_weight, up_weight, down_weight)
    return offloaded(tokens, gate_weight, up_weight, down_weight)


def solution(mesh):
    return jax.shard_map(
        shards,
        mesh=mesh,
        in_specs=(
            P(("grp", "gy", "gz"), "gx"),
            P("gx", ("gy", "gz")),
            P("gx", ("gy", "gz")),
            P(("gy", "gz"), "gx"),
        ),
        out_specs=P(("grp", "gy", "gz"), "gx"),
        check_vma=False,
    )
```

```python
import functools

import jax
import jax.numpy as jnp
from jax import lax
from jax.experimental import pallas as pl
from jax.experimental.pallas import tpu as pltpu
from jax.sharding import PartitionSpec as P

MIB = 1 << 20
STEP = 256
COPY_STEP = 512
IN_FLIGHT = 6
TOKEN_AXES = ("gy", "gz")
IN_HBM = pl.BlockSpec(memory_space=pltpu.HBM)
ANY = pl.BlockSpec(memory_space=pl.ANY)
WHOLE = pl.BlockSpec(memory_space=pltpu.VMEM)


def activate(gate, up):
    return (jax.nn.silu(gate) * up).astype(jnp.bfloat16)


def pieces_of(total, step):
    return [(start, min(step, total - start)) for start in range(0, total, step)]


def in_hbm(value):
    return pltpu.with_memory_space_constraint(value, pltpu.HBM)


def in_vmem(value):
    return pltpu.with_memory_space_constraint(value, pltpu.VMEM)


SMALL = pl.CostEstimate(flops=0, bytes_accessed=MIB, transcendentals=0)


def block_start(distance, width):
    return pl.multiple_of((lax.axis_index("gx") ^ distance) * width, 128)


def params(mib):
    return pltpu.CompilerParams(vmem_limit_bytes=mib * MIB)


def packed_pair_width(rows, width):
    return (rows // 8) * 2 * width + (width if rows % 8 else 0)


def pack_pair(out, gate, up):
    rows, width = gate.shape
    for g in range(rows // 8):
        for w, value in enumerate((gate, up)):
            at = (2 * g + w) * width
            out[:, at : at + width] = value[8 * g : 8 * g + 8].astype(out.dtype)
    if rows % 8:
        at = (rows // 8) * 2 * width
        tail = jnp.concatenate([gate[rows - 4 :], up[rows - 4 :]], axis=0)
        out[:, at : at + width] = tail.astype(out.dtype)


def block_copies(width, distance, weights, held, sems):
    columns = pl.ds(block_start(distance, width), width)
    copies = []
    for k, (row, rows) in enumerate(pieces_of(held.shape[1], COPY_STEP)):
        for w, weight in enumerate(weights):
            copy = pltpu.make_async_copy(
                weight.at[pl.ds(row, rows), columns], held.at[w, pl.ds(row, rows)], sems.at[w, k]
            )
            copies.append((w, row, rows, copy))
    return copies


def fetch_kernel(width, distance, gate_ref, up_ref, held, sems):
    copies = block_copies(width, distance, (gate_ref, up_ref), held, sems)
    for _, _, _, copy in copies:
        copy.start()
    for _, _, _, copy in copies:
        copy.wait()


def fetch(gate_weight, up_weight, distance, width):
    depth = gate_weight.shape[0]
    return pl.pallas_call(
        functools.partial(fetch_kernel, width, distance),
        out_shape=pltpu.VMEM((2, depth, width), jnp.bfloat16),
        in_specs=[IN_HBM, IN_HBM],
        out_specs=WHOLE,
        scratch_shapes=[pltpu.SemaphoreType.DMA((2, len(pieces_of(depth, COPY_STEP))))],
        compiler_params=params(4),
        cost_estimate=SMALL,
    )(in_hbm(gate_weight), in_hbm(up_weight))


def multiply(x_ref, held, total, steps, waiting=()):
    for w, first, tall, copy in steps:
        if copy is not None:
            copy.wait()
        if waiting:
            waiting.pop(0).start()
        for row, rows in pieces_of(tall, STEP):
            rows = slice(first + row, first + row + rows)
            term = jnp.dot(x_ref[:, rows], held[w, rows, :], preferred_element_type=jnp.float32)
            if rows.start == 0:
                total[w] = term
            else:
                total[w] += term


def held_kernel(x_ref, held, out, total):
    parts = pieces_of(x_ref.shape[1], STEP)
    multiply(x_ref, held, total, [(w, row, rows, None) for w in range(2) for row, rows in parts])
    pack_pair(out, total[0], total[1])


def gate_up_held(features, held):
    rows, width = features.shape[0], held.shape[2]
    return pl.pallas_call(
        held_kernel,
        out_shape=jax.ShapeDtypeStruct((8, packed_pair_width(rows, width)), jnp.bfloat16),
        in_specs=[WHOLE, WHOLE],
        out_specs=WHOLE,
        scratch_shapes=[pltpu.VMEM((2, rows, width), jnp.float32)],
        compiler_params=params(8),
        cost_estimate=SMALL,
    )(features, in_vmem(held))


def stream_kernel(width, blocks, distances, x_ref, gate_ref, up_ref, _, *refs):
    outs, refs = refs[: len(blocks)], refs[len(blocks) :]
    work = []
    for b, which in enumerate(blocks):
        held, total, sems = refs[3 * b : 3 * b + 3]
        weights = [(gate_ref, up_ref)[w] for w in which]
        copies = block_copies(width, distances[b], weights, held, sems)
        work.append((outs[b], held, total, copies))
    waiting = [step[-1] for block in work for step in block[-1]]
    in_flight = IN_FLIGHT if len(blocks) > 1 else len(waiting)
    for copy in waiting[:in_flight]:
        copy.start()
    waiting = waiting[in_flight:]
    for (out, held, total, copies), which in zip(work, blocks):
        multiply(x_ref, held, total, copies, waiting)
        if len(which) == 2:
            pack_pair(out, total[0], total[1])
        else:
            pack_single(out, total[0])


def gate_up_stream(features, gate_weight, up_weight, distances, blocks, width, after):
    rows, depth = features.shape
    scratch, shapes = [], []
    for which in blocks:
        packed = packed_pair_width(rows, width) if len(which) == 2 else packed_width(rows, width)
        shapes.append(jax.ShapeDtypeStruct((8, packed), jnp.bfloat16))
        scratch += [
            pltpu.VMEM((len(which), depth, width), jnp.bfloat16),
            pltpu.VMEM((len(which), rows, width), jnp.float32),
            pltpu.SemaphoreType.DMA((len(which), len(pieces_of(depth, COPY_STEP)))),
        ]
    held_mib = -(-depth * width * 2 * sum(len(which) for which in blocks) // MIB)
    return pl.pallas_call(
        functools.partial(stream_kernel, width, blocks, distances),
        out_shape=shapes,
        in_specs=[WHOLE, IN_HBM, IN_HBM, ANY],
        out_specs=[WHOLE] * len(blocks),
        scratch_shapes=scratch,
        compiler_params=params(5 + held_mib),
        cost_estimate=SMALL,
    )(features, in_hbm(gate_weight), in_hbm(up_weight), after)


def hidden_tail(rows, width):
    half = pl.cdiv(width // 2, 128) * 128
    return half if rows % 8 else 0


def packed_width(rows, width):
    return (rows // 8) * width + hidden_tail(rows, width)


def pack_single(out, value):
    rows, width = value.shape
    for g in range(rows // 8):
        out[:, g * width : (g + 1) * width] = value[8 * g : 8 * g + 8].astype(out.dtype)
    if rows % 8:
        at, half = (rows // 8) * width, hidden_tail(rows, width)
        left, right = value[rows - 4 :, :half], value[rows - 4 :, half:]
        if 2 * half > width:
            right = jnp.concatenate([right, jnp.zeros((4, 2 * half - width), jnp.float32)], axis=1)
        out[:, at : at + half] = jnp.concatenate([left, right], axis=0).astype(out.dtype)


def last_rows(packed, rows, width):
    at, half = (rows // 8) * width, hidden_tail(rows, width)
    tail = packed[:, at : at + half].astype(jnp.float32)
    return jnp.concatenate([tail[:4], tail[4:, : width - half]], axis=1)


def activate_kernel(rows, width, own, far, gate_near, up_near, out):
    def pair(at):
        columns = slice(at, at + width)
        return own[:, columns].astype(jnp.float32) + far[:, columns].astype(jnp.float32)

    for g in range(rows // 8):
        near = slice(g * width, (g + 1) * width)
        out[:, near] = activate(
            pair(2 * g * width) + gate_near[:, near].astype(jnp.float32),
            pair((2 * g + 1) * width) + up_near[:, near].astype(jnp.float32),
        )
    if rows % 8:
        half = hidden_tail(rows, width)
        last = pair((rows // 8) * 2 * width)
        value = activate(
            last[:4] + last_rows(gate_near, rows, width),
            last[4:] + last_rows(up_near, rows, width),
        ).astype(jnp.float32)
        right = jnp.concatenate([value[:, half:], jnp.zeros((4, 2 * half - width), jnp.float32)], axis=1)
        at = (rows // 8) * width
        out[:, at : at + half] = jnp.concatenate([value[:, :half], right], axis=0).astype(out.dtype)


def activate_packed(own, far, near, rows, width):
    return pl.pallas_call(
        functools.partial(activate_kernel, rows, width),
        out_shape=jax.ShapeDtypeStruct((8, packed_width(rows, width)), jnp.bfloat16),
        in_specs=[WHOLE] * 4,
        out_specs=WHOLE,
        compiler_params=params(8),
        cost_estimate=SMALL,
    )(own, far, *near)


def pack_rows(out, value):
    rows, width = value.shape
    for g in range(rows // 8):
        out[:, g * width : (g + 1) * width] = value[8 * g : 8 * g + 8].astype(out.dtype)
    piece = width // 8
    for r in range(rows // 8 * 8, rows):
        at = (rows // 8) * width + (r % 8) * piece
        row = jnp.concatenate(
            [value[r : r + 1, i * piece : (i + 1) * piece] for i in range(8)], axis=0
        )
        out[:, at : at + piece] = row.astype(out.dtype)


def unpack_rows(out, packed):
    rows, width = out.shape
    for g in range(rows // 8):
        out[8 * g : 8 * g + 8, :] = packed[:, g * width : (g + 1) * width]
    piece = width // 8
    for r in range(rows // 8 * 8, rows):
        at = (rows // 8) * width + (r % 8) * piece
        for i in range(8):
            out[r : r + 1, i * piece : (i + 1) * piece] = packed[i : i + 1, at : at + piece]


def down_kernel(first, rows, width, distances, *refs):
    blocks = len(distances)
    hidden, refs = refs[:blocks], refs[blocks:]
    if not first:
        before, refs = refs[0], refs[1:]
    held, outs, (plain, total) = refs[0], refs[1:-2], refs[-2:]
    if first:
        total = outs[0]
    for b in range(blocks):
        for g in range(rows // 8):
            plain[8 * g : 8 * g + 8, :] = hidden[b][:, g * width : (g + 1) * width].astype(jnp.float32)
        if rows % 8:
            at, half = (rows // 8) * width, hidden_tail(rows, width)
            tail = hidden[b][:, at : at + half].astype(jnp.float32)
            plain[rows - 4 :, :half] = tail[:4]
            plain[rows - 4 :, half:] = tail[4:, : width - half]
        for row, tall in pieces_of(width, STEP):
            term = jnp.dot(
                plain[:, row : row + tall].astype(jnp.bfloat16),
                held[pl.ds(pl.multiple_of(block_start(distances[b], width) + row, 128), tall), :],
                preferred_element_type=jnp.float32,
            )
            if b == 0 and row == 0:
                total[...] = term if first else before[...] + term
            else:
                total[...] += term
    if not first:
        tall = rows // len(outs)
        for r, out in enumerate(outs):
            pack_rows(out, total[r * tall : (r + 1) * tall, :])


def down(hidden, distances, before, weight, rows, width, outs):
    columns = weight.shape[1]
    if before is None:
        shapes = [jax.ShapeDtypeStruct((rows, columns), jnp.float32)]
    else:
        packed = (8, rows // outs * columns // 8)
        shapes = [jax.ShapeDtypeStruct(packed, jnp.bfloat16 if r else jnp.float32) for r in range(outs)]
    carried = [] if before is None else [before]
    return pl.pallas_call(
        functools.partial(down_kernel, before is None, rows, width, distances),
        out_shape=shapes,
        in_specs=[WHOLE] * (len(hidden) + len(carried) + 1),
        out_specs=[WHOLE] * len(shapes),
        scratch_shapes=[
            pltpu.VMEM((rows, width), jnp.float32),
            pltpu.VMEM((rows, columns), jnp.float32),
        ],
        compiler_params=params(8),
        cost_estimate=SMALL,
    )(*hidden, *carried, in_vmem(weight))


def finish_kernel(*refs):
    terms, out, plain = refs[:-2], refs[-2], refs[-1]
    packed = terms[0][...]
    for term in terms[1:]:
        packed = packed + term[...].astype(jnp.float32)
    unpack_rows(plain, packed)
    out[...] = plain[...].astype(out.dtype)


def finish(terms, shape):
    return pl.pallas_call(
        finish_kernel,
        out_shape=jax.ShapeDtypeStruct(shape, jnp.bfloat16),
        in_specs=[WHOLE] * len(terms),
        out_specs=WHOLE,
        scratch_shapes=[pltpu.VMEM(shape, jnp.float32)],
        compiler_params=params(4),
        cost_estimate=SMALL,
    )(*terms)


def swap(value, axes, size, distance):
    return lax.ppermute(value, axes, [(i, i ^ distance) for i in range(size)])


def add(a, b):
    return a.astype(jnp.float32) + b.astype(jnp.float32)


def direct(tokens, gate_weight, up_weight, down_weight):
    n_gx = lax.axis_size("gx")
    n_token = lax.axis_size(TOKEN_AXES)
    width = gate_weight.shape[1] // n_gx

    held = fetch(gate_weight, up_weight, 3, width)
    features = jnp.concatenate(
        [tokens] + [swap(tokens, TOKEN_AXES, n_token, r) for r in range(1, n_token)], axis=0
    )
    rows = features.shape[0]

    def blocks_for(distances, blocks, after):
        return gate_up_stream(features, gate_weight, up_weight, distances, blocks, width, after)

    relayed = gate_up_held(features, held)
    arrived = swap(relayed, "gx", n_gx, 1)
    across, beside = blocks_for((2, 1), ((0, 1), (0,)), relayed)
    across = lax.optimization_barrier(add(across, arrived).astype(jnp.bfloat16))
    far = swap(across, "gx", n_gx, 2)
    near = [swap(beside, "gx", n_gx, 1)]
    (beside,) = blocks_for((1,), ((1,),), across)
    near.append(swap(beside, "gx", n_gx, 1))
    (own,) = blocks_for((0,), ((0, 1),), beside)
    hidden = activate_packed(own, far, near, rows, width)

    opposite = swap(hidden, "gx", n_gx, 2)
    first = [hidden, swap(hidden, "gx", n_gx, 1), opposite]
    second = [swap(opposite, "gx", n_gx, 1)]
    (partial_sum,) = down(first, (0, 1, 2), None, down_weight, rows, width, 1)
    outs = down(second, (3,), partial_sum, down_weight, rows, width, n_token)
    terms = [outs[0]] + [swap(outs[r], TOKEN_AXES, n_token, r) for r in range(1, n_token)]
    return finish(terms, tokens.shape)


def offloaded(tokens, gate_weight, up_weight, down_weight):
    features = lax.all_gather(tokens, TOKEN_AXES, axis=0, tiled=True)
    hidden_width = gate_weight.shape[1]
    gate_part = jnp.dot(features, gate_weight, preferred_element_type=jnp.float32)
    up_part = jnp.dot(features, up_weight, preferred_element_type=jnp.float32)
    summed = lax.psum(
        jnp.concatenate([gate_part, up_part], axis=1).astype(jnp.bfloat16), "gx"
    ).astype(jnp.float32)
    hidden = activate(summed[:, :hidden_width], summed[:, hidden_width:])
    partial_value = jnp.dot(hidden, down_weight, preferred_element_type=jnp.float32)
    return lax.psum_scatter(
        partial_value.astype(jnp.bfloat16), TOKEN_AXES, scatter_dimension=0, tiled=True
    )


def shards(tokens, gate_weight, up_weight, down_weight):
    n_gx = lax.axis_size("gx")
    n_token = lax.axis_size(TOKEN_AXES)
    rows = tokens.shape[0] * n_token
    tokens_fit = n_token > 1 and n_token & (n_token - 1) == 0 and rows % 4 == 0
    weights_fit = gate_weight.shape[1] % (128 * 4) == 0 and gate_weight.shape[0] % STEP == 0
    columns_fit = down_weight.shape[1] % (128 * 8) == 0
    if n_gx == 4 and tokens_fit and weights_fit and columns_fit:
        return direct(tokens, gate_weight, up_weight, down_weight)
    return offloaded(tokens, gate_weight, up_weight, down_weight)


def solution(mesh):
    return jax.shard_map(
        shards,
        mesh=mesh,
        in_specs=(
            P(("grp", "gy", "gz"), "gx"),
            P("gx", ("gy", "gz")),
            P("gx", ("gy", "gz")),
            P(("gy", "gz"), "gx"),
        ),
        out_specs=P(("grp", "gy", "gz"), "gx"),
        check_vma=False,
    )
```

```python
import functools

import jax
import jax.numpy as jnp
from jax import lax
from jax.experimental import pallas as pl
from jax.experimental.pallas import tpu as pltpu
from jax.sharding import PartitionSpec as P

MIB = 1 << 20
STEP = 256
COPY_STEP = 512
TOKEN_AXES = ("gy", "gz")
IN_HBM = pl.BlockSpec(memory_space=pltpu.HBM)
ANY = pl.BlockSpec(memory_space=pl.ANY)
WHOLE = pl.BlockSpec(memory_space=pltpu.VMEM)


def activate(gate, up):
    return (jax.nn.silu(gate) * up).astype(jnp.bfloat16)


def pieces_of(total, step):
    return [(start, min(step, total - start)) for start in range(0, total, step)]


def graded_pieces(total):
    pieces, row = [], 0
    while total - row > STEP:
        rows = max(STEP, (total - row) // (2 * STEP) * STEP)
        pieces.append((row, rows))
        row += rows
    return pieces + [(row, total - row)]


def in_hbm(value):
    return pltpu.with_memory_space_constraint(value, pltpu.HBM)


def in_vmem(value):
    return pltpu.with_memory_space_constraint(value, pltpu.VMEM)


SMALL = pl.CostEstimate(flops=0, bytes_accessed=MIB, transcendentals=0)


def block_start(distance, width):
    return pl.multiple_of((lax.axis_index("gx") ^ distance) * width, 128)


def params(mib):
    return pltpu.CompilerParams(vmem_limit_bytes=mib * MIB)


def packed_pair_width(rows, width):
    return (rows // 8) * 2 * width + (width if rows % 8 else 0)


def pack_pair(out, gate, up):
    rows, width = gate.shape
    for g in range(rows // 8):
        for w, value in enumerate((gate, up)):
            at = (2 * g + w) * width
            out[:, at : at + width] = value[8 * g : 8 * g + 8].astype(out.dtype)
    if rows % 8:
        at = (rows // 8) * 2 * width
        tail = jnp.concatenate([gate[rows - 4 :], up[rows - 4 :]], axis=0)
        out[:, at : at + width] = tail.astype(out.dtype)


def block_copies(width, distance, weights, pieces, held, sems):
    columns = pl.ds(block_start(distance, width), width)
    copies = []
    for k, (row, rows) in enumerate(pieces):
        for w, weight in enumerate(weights):
            copy = pltpu.make_async_copy(
                weight.at[pl.ds(row, rows), columns], held.at[w, pl.ds(row, rows)], sems.at[w, k]
            )
            copies.append((w, row, rows, copy))
    return copies


def fetch_kernel(width, distance, weight, held, sems):
    pieces = pieces_of(held.shape[1], COPY_STEP)
    copies = block_copies(width, distance, (weight,), pieces, held, sems)
    for _, _, _, copy in copies:
        copy.start()
    for _, _, _, copy in copies:
        copy.wait()


def fetch(weight, distance, width):
    depth = weight.shape[0]
    return pl.pallas_call(
        functools.partial(fetch_kernel, width, distance),
        out_shape=pltpu.VMEM((1, depth, width), jnp.bfloat16),
        in_specs=[IN_HBM],
        out_specs=WHOLE,
        scratch_shapes=[pltpu.SemaphoreType.DMA((1, len(pieces_of(depth, COPY_STEP))))],
        compiler_params=params(4),
        cost_estimate=SMALL,
    )(in_hbm(weight))


def multiply(x_ref, held, total, steps):
    for w, first, tall, copy in steps:
        if copy is not None:
            copy.wait()
        for row, rows in pieces_of(tall, STEP):
            rows = slice(first + row, first + row + rows)
            term = jnp.dot(x_ref[:, rows], held[w, rows, :], preferred_element_type=jnp.float32)
            if rows.start == 0:
                total[w] = term
            else:
                total[w] += term


def held_kernel(width, distance, x_ref, held, up_ref, out, stream, total, sems):
    pieces = graded_pieces(stream.shape[1])
    copies = block_copies(width, distance, (up_ref,), pieces, stream, sems)
    for _, _, _, copy in copies:
        copy.start()
    multiply(x_ref, held, total.at[pl.ds(0, 1)], [(0, 0, held.shape[1], None)])
    multiply(x_ref, stream, total.at[pl.ds(1, 1)], copies)
    pack_pair(out, total[0], total[1])


def gate_up_held(features, held, up_weight, distance):
    rows, depth = features.shape
    width = held.shape[2]
    return pl.pallas_call(
        functools.partial(held_kernel, width, distance),
        out_shape=jax.ShapeDtypeStruct((8, packed_pair_width(rows, width)), jnp.bfloat16),
        in_specs=[WHOLE, WHOLE, IN_HBM],
        out_specs=WHOLE,
        scratch_shapes=[
            pltpu.VMEM((1, depth, width), jnp.bfloat16),
            pltpu.VMEM((2, rows, width), jnp.float32),
            pltpu.SemaphoreType.DMA((1, len(graded_pieces(depth)))),
        ],
        compiler_params=params(5 + -(-depth * width * 2 // MIB)),
        cost_estimate=SMALL,
    )(features, in_vmem(held), in_hbm(up_weight))


def stream_kernel(width, blocks, distances, x_ref, gate_ref, up_ref, _, *refs):
    outs, refs = refs[: len(blocks)], refs[len(blocks) :]
    work = []
    for b, which in enumerate(blocks):
        held, total, sems = refs[3 * b : 3 * b + 3]
        weights = [(gate_ref, up_ref)[w] for w in which]
        pieces = stream_pieces(held.shape[1], blocks)
        copies = block_copies(width, distances[b], weights, pieces, held, sems)
        for _, _, _, copy in copies:
            copy.start()
        work.append((outs[b], held, total, copies))
    for (out, held, total, copies), which in zip(work, blocks):
        multiply(x_ref, held, total, copies)
        if len(which) == 2:
            pack_pair(out, total[0], total[1])
        else:
            pack_single(out, total[0])


def stream_pieces(depth, blocks):
    return pieces_of(depth, COPY_STEP) if len(blocks) > 1 else graded_pieces(depth)


def gate_up_stream(features, gate_weight, up_weight, distances, blocks, width, after):
    rows, depth = features.shape
    scratch, shapes = [], []
    for which in blocks:
        packed = packed_pair_width(rows, width) if len(which) == 2 else packed_width(rows, width)
        shapes.append(jax.ShapeDtypeStruct((8, packed), jnp.bfloat16))
        scratch += [
            pltpu.VMEM((len(which), depth, width), jnp.bfloat16),
            pltpu.VMEM((len(which), rows, width), jnp.float32),
            pltpu.SemaphoreType.DMA((len(which), len(stream_pieces(depth, blocks)))),
        ]
    held_mib = -(-depth * width * 2 * sum(len(which) for which in blocks) // MIB)
    return pl.pallas_call(
        functools.partial(stream_kernel, width, blocks, distances),
        out_shape=shapes,
        in_specs=[WHOLE, IN_HBM, IN_HBM, ANY],
        out_specs=[WHOLE] * len(blocks),
        scratch_shapes=scratch,
        compiler_params=params(5 + held_mib),
        cost_estimate=SMALL,
    )(features, in_hbm(gate_weight), in_hbm(up_weight), after)


def hidden_tail(rows, width):
    half = pl.cdiv(width // 2, 128) * 128
    return half if rows % 8 else 0


def packed_width(rows, width):
    return (rows // 8) * width + hidden_tail(rows, width)


def pack_single(out, value):
    rows, width = value.shape
    for g in range(rows // 8):
        out[:, g * width : (g + 1) * width] = value[8 * g : 8 * g + 8].astype(out.dtype)
    if rows % 8:
        at, half = (rows // 8) * width, hidden_tail(rows, width)
        left, right = value[rows - 4 :, :half], value[rows - 4 :, half:]
        if 2 * half > width:
            right = jnp.concatenate([right, jnp.zeros((4, 2 * half - width), jnp.float32)], axis=1)
        out[:, at : at + half] = jnp.concatenate([left, right], axis=0).astype(out.dtype)


def last_rows(packed, rows, width):
    at, half = (rows // 8) * width, hidden_tail(rows, width)
    tail = packed[:, at : at + half].astype(jnp.float32)
    return jnp.concatenate([tail[:4], tail[4:, : width - half]], axis=1)


def activate_kernel(rows, width, own, far, gate_near, up_near, out):
    def pair(at):
        columns = slice(at, at + width)
        return own[:, columns].astype(jnp.float32) + far[:, columns].astype(jnp.float32)

    for g in range(rows // 8):
        near = slice(g * width, (g + 1) * width)
        out[:, near] = activate(
            pair(2 * g * width) + gate_near[:, near].astype(jnp.float32),
            pair((2 * g + 1) * width) + up_near[:, near].astype(jnp.float32),
        )
    if rows % 8:
        half = hidden_tail(rows, width)
        last = pair((rows // 8) * 2 * width)
        value = activate(
            last[:4] + last_rows(gate_near, rows, width),
            last[4:] + last_rows(up_near, rows, width),
        ).astype(jnp.float32)
        right = jnp.concatenate([value[:, half:], jnp.zeros((4, 2 * half - width), jnp.float32)], axis=1)
        at = (rows // 8) * width
        out[:, at : at + half] = jnp.concatenate([value[:, :half], right], axis=0).astype(out.dtype)


def activate_packed(own, far, near, rows, width):
    return pl.pallas_call(
        functools.partial(activate_kernel, rows, width),
        out_shape=jax.ShapeDtypeStruct((8, packed_width(rows, width)), jnp.bfloat16),
        in_specs=[WHOLE] * 4,
        out_specs=WHOLE,
        compiler_params=params(8),
        cost_estimate=SMALL,
    )(own, far, *near)


def pack_rows(out, value):
    rows, width = value.shape
    for g in range(rows // 8):
        out[:, g * width : (g + 1) * width] = value[8 * g : 8 * g + 8].astype(out.dtype)
    piece = width // 8
    for r in range(rows // 8 * 8, rows):
        at = (rows // 8) * width + (r % 8) * piece
        row = jnp.concatenate(
            [value[r : r + 1, i * piece : (i + 1) * piece] for i in range(8)], axis=0
        )
        out[:, at : at + piece] = row.astype(out.dtype)


def unpack_rows(out, packed):
    rows, width = out.shape
    for g in range(rows // 8):
        out[8 * g : 8 * g + 8, :] = packed[:, g * width : (g + 1) * width]
    piece = width // 8
    for r in range(rows // 8 * 8, rows):
        at = (rows // 8) * width + (r % 8) * piece
        for i in range(8):
            out[r : r + 1, i * piece : (i + 1) * piece] = packed[i : i + 1, at : at + piece]


def down_kernel(first, rows, width, distances, *refs):
    blocks = len(distances)
    hidden, refs = refs[:blocks], refs[blocks:]
    if not first:
        before, refs = refs[0], refs[1:]
    held, outs, (plain, total) = refs[0], refs[1:-2], refs[-2:]
    if first:
        total = outs[0]
    for b in range(blocks):
        for g in range(rows // 8):
            plain[8 * g : 8 * g + 8, :] = hidden[b][:, g * width : (g + 1) * width].astype(jnp.float32)
        if rows % 8:
            at, half = (rows // 8) * width, hidden_tail(rows, width)
            tail = hidden[b][:, at : at + half].astype(jnp.float32)
            plain[rows - 4 :, :half] = tail[:4]
            plain[rows - 4 :, half:] = tail[4:, : width - half]
        for row, tall in pieces_of(width, STEP):
            term = jnp.dot(
                plain[:, row : row + tall].astype(jnp.bfloat16),
                held[pl.ds(pl.multiple_of(block_start(distances[b], width) + row, 128), tall), :],
                preferred_element_type=jnp.float32,
            )
            if b == 0 and row == 0:
                total[...] = term if first else before[...] + term
            else:
                total[...] += term
    if not first:
        tall = rows // len(outs)
        for r, out in enumerate(outs):
            pack_rows(out, total[r * tall : (r + 1) * tall, :])


def down(hidden, distances, before, weight, rows, width, outs):
    columns = weight.shape[1]
    if before is None:
        shapes = [jax.ShapeDtypeStruct((rows, columns), jnp.float32)]
    else:
        packed = (8, rows // outs * columns // 8)
        shapes = [jax.ShapeDtypeStruct(packed, jnp.bfloat16 if r else jnp.float32) for r in range(outs)]
    carried = [] if before is None else [before]
    return pl.pallas_call(
        functools.partial(down_kernel, before is None, rows, width, distances),
        out_shape=shapes,
        in_specs=[WHOLE] * (len(hidden) + len(carried) + 1),
        out_specs=[WHOLE] * len(shapes),
        scratch_shapes=[
            pltpu.VMEM((rows, width), jnp.float32),
            pltpu.VMEM((rows, columns), jnp.float32),
        ],
        compiler_params=params(8),
        cost_estimate=SMALL,
    )(*hidden, *carried, in_vmem(weight))


def finish_kernel(*refs):
    terms, out, plain = refs[:-2], refs[-2], refs[-1]
    packed = terms[0][...]
    for term in terms[1:]:
        packed = packed + term[...].astype(jnp.float32)
    unpack_rows(plain, packed)
    out[...] = plain[...].astype(out.dtype)


def finish(terms, shape):
    return pl.pallas_call(
        finish_kernel,
        out_shape=jax.ShapeDtypeStruct(shape, jnp.bfloat16),
        in_specs=[WHOLE] * len(terms),
        out_specs=WHOLE,
        scratch_shapes=[pltpu.VMEM(shape, jnp.float32)],
        compiler_params=params(4),
        cost_estimate=SMALL,
    )(*terms)


def swap(value, axes, size, distance):
    return lax.ppermute(value, axes, [(i, i ^ distance) for i in range(size)])


def add(a, b):
    return a.astype(jnp.float32) + b.astype(jnp.float32)


def direct(tokens, gate_weight, up_weight, down_weight):
    n_gx = lax.axis_size("gx")
    n_token = lax.axis_size(TOKEN_AXES)
    width = gate_weight.shape[1] // n_gx

    held = fetch(gate_weight, 3, width)
    features = jnp.concatenate(
        [tokens] + [swap(tokens, TOKEN_AXES, n_token, r) for r in range(1, n_token)], axis=0
    )
    rows = features.shape[0]

    def blocks_for(distances, blocks, after):
        return gate_up_stream(features, gate_weight, up_weight, distances, blocks, width, after)

    relayed = gate_up_held(features, held, up_weight, 3)
    arrived = swap(relayed, "gx", n_gx, 1)
    across, beside = blocks_for((2, 1), ((0, 1), (0,)), relayed)
    across = lax.optimization_barrier(add(across, arrived).astype(jnp.bfloat16))
    far = swap(across, "gx", n_gx, 2)
    near = [swap(beside, "gx", n_gx, 1)]
    (beside,) = blocks_for((1,), ((1,),), across)
    near.append(swap(beside, "gx", n_gx, 1))
    (own,) = blocks_for((0,), ((0, 1),), beside)
    hidden = activate_packed(own, far, near, rows, width)

    opposite = swap(hidden, "gx", n_gx, 2)
    first = [hidden, swap(hidden, "gx", n_gx, 1), opposite]
    second = [swap(opposite, "gx", n_gx, 1)]
    (partial_sum,) = down(first, (0, 1, 2), None, down_weight, rows, width, 1)
    outs = down(second, (3,), partial_sum, down_weight, rows, width, n_token)
    terms = [outs[0]] + [swap(outs[r], TOKEN_AXES, n_token, r) for r in range(1, n_token)]
    return finish(terms, tokens.shape)


def offloaded(tokens, gate_weight, up_weight, down_weight):
    features = lax.all_gather(tokens, TOKEN_AXES, axis=0, tiled=True)
    hidden_width = gate_weight.shape[1]
    gate_part = jnp.dot(features, gate_weight, preferred_element_type=jnp.float32)
    up_part = jnp.dot(features, up_weight, preferred_element_type=jnp.float32)
    summed = lax.psum(
        jnp.concatenate([gate_part, up_part], axis=1).astype(jnp.bfloat16), "gx"
    ).astype(jnp.float32)
    hidden = activate(summed[:, :hidden_width], summed[:, hidden_width:])
    partial_value = jnp.dot(hidden, down_weight, preferred_element_type=jnp.float32)
    return lax.psum_scatter(
        partial_value.astype(jnp.bfloat16), TOKEN_AXES, scatter_dimension=0, tiled=True
    )


def shards(tokens, gate_weight, up_weight, down_weight):
    n_gx = lax.axis_size("gx")
    n_token = lax.axis_size(TOKEN_AXES)
    rows = tokens.shape[0] * n_token
    tokens_fit = n_token > 1 and n_token & (n_token - 1) == 0 and rows % 4 == 0
    weights_fit = gate_weight.shape[1] % (128 * 4) == 0 and gate_weight.shape[0] % STEP == 0
    columns_fit = down_weight.shape[1] % (128 * 8) == 0
    if n_gx == 4 and tokens_fit and weights_fit and columns_fit:
        return direct(tokens, gate_weight, up_weight, down_weight)
    return offloaded(tokens, gate_weight, up_weight, down_weight)


def solution(mesh):
    return jax.shard_map(
        shards,
        mesh=mesh,
        in_specs=(
            P(("grp", "gy", "gz"), "gx"),
            P("gx", ("gy", "gz")),
            P("gx", ("gy", "gz")),
            P(("gy", "gz"), "gx"),
        ),
        out_specs=P(("grp", "gy", "gz"), "gx"),
        check_vma=False,
    )
```

```python
import functools

import jax
import jax.numpy as jnp
from jax import lax
from jax.experimental import pallas as pl
from jax.experimental.pallas import tpu as pltpu
from jax.sharding import PartitionSpec as P

MIB = 1 << 20
STEP = 256
COPY_STEP = 512
IN_FLIGHT = 6
HELD_STEP = 512
TOKEN_AXES = ("gy", "gz")
IN_HBM = pl.BlockSpec(memory_space=pltpu.HBM)
ANY = pl.BlockSpec(memory_space=pl.ANY)
WHOLE = pl.BlockSpec(memory_space=pltpu.VMEM)


def activate(gate, up):
    return (jax.nn.silu(gate) * up).astype(jnp.bfloat16)


def pieces_of(total, step):
    return [(start, min(step, total - start)) for start in range(0, total, step)]


def copy_pieces(depth, last):
    if not last:
        return pieces_of(depth, COPY_STEP)
    cut = depth // 4 // STEP * STEP
    small = pieces_of(cut, STEP // 2)
    return pieces_of(depth - cut, STEP) + [(depth - cut + row, rows) for row, rows in small]


def in_hbm(value):
    return pltpu.with_memory_space_constraint(value, pltpu.HBM)


def in_vmem(value):
    return pltpu.with_memory_space_constraint(value, pltpu.VMEM)


SMALL = pl.CostEstimate(flops=0, bytes_accessed=MIB, transcendentals=0)


def block_start(distance, width):
    return pl.multiple_of((lax.axis_index("gx") ^ distance) * width, 128)


def params(mib):
    return pltpu.CompilerParams(vmem_limit_bytes=mib * MIB)


def packed_pair_width(rows, width):
    return (rows // 8) * 2 * width + (width if rows % 8 else 0)


def pack_pair(out, gate, up):
    rows, width = gate.shape
    for g in range(rows // 8):
        for w, value in enumerate((gate, up)):
            at = (2 * g + w) * width
            out[:, at : at + width] = value[8 * g : 8 * g + 8].astype(out.dtype)
    if rows % 8:
        at = (rows // 8) * 2 * width
        tail = jnp.concatenate([gate[rows - 4 :], up[rows - 4 :]], axis=0)
        out[:, at : at + width] = tail.astype(out.dtype)


def block_copies(width, distance, weights, held, sems, last=False):
    columns = pl.ds(block_start(distance, width), width)
    copies = []
    for k, (row, rows) in enumerate(copy_pieces(held.shape[1], last)):
        for w, weight in enumerate(weights):
            copy = pltpu.make_async_copy(
                weight.at[pl.ds(row, rows), columns], held.at[w, pl.ds(row, rows)], sems.at[w, k]
            )
            copies.append((w, row, rows, copy))
    return copies


def fetch_kernel(width, distance, gate_ref, up_ref, held, sems):
    copies = block_copies(width, distance, (gate_ref, up_ref), held, sems)
    for _, _, _, copy in copies:
        copy.start()
    for _, _, _, copy in copies:
        copy.wait()


def fetch(gate_weight, up_weight, distance, width):
    depth = gate_weight.shape[0]
    return pl.pallas_call(
        functools.partial(fetch_kernel, width, distance),
        out_shape=pltpu.VMEM((2, depth, width), jnp.bfloat16),
        in_specs=[IN_HBM, IN_HBM],
        out_specs=WHOLE,
        scratch_shapes=[pltpu.SemaphoreType.DMA((2, len(pieces_of(depth, COPY_STEP))))],
        compiler_params=params(4),
        cost_estimate=SMALL,
    )(in_hbm(gate_weight), in_hbm(up_weight))


def multiply(x_ref, held, total, steps, waiting=(), step=STEP):
    for w, first, tall, copy in steps:
        if copy is not None:
            copy.wait()
        if waiting:
            waiting.pop(0).start()
        for row, rows in pieces_of(tall, step):
            rows = slice(first + row, first + row + rows)
            term = jnp.dot(x_ref[:, rows], held[w, rows, :], preferred_element_type=jnp.float32)
            if rows.start == 0:
                total[w] = term
            else:
                total[w] += term


def held_kernel(x_ref, held, out, total):
    multiply(x_ref, held, total, [(w, 0, held.shape[1], None) for w in range(2)], step=HELD_STEP)
    pack_pair(out, total[0], total[1])


def gate_up_held(features, held):
    rows, width = features.shape[0], held.shape[2]
    return pl.pallas_call(
        held_kernel,
        out_shape=jax.ShapeDtypeStruct((8, packed_pair_width(rows, width)), jnp.bfloat16),
        in_specs=[WHOLE, WHOLE],
        out_specs=WHOLE,
        scratch_shapes=[pltpu.VMEM((2, rows, width), jnp.float32)],
        compiler_params=params(8),
        cost_estimate=SMALL,
    )(features, in_vmem(held))


def stream_kernel(width, blocks, distances, x_ref, gate_ref, up_ref, _, *refs):
    outs, refs = refs[: len(blocks)], refs[len(blocks) :]
    work = []
    for b, which in enumerate(blocks):
        held, total, sems = refs[3 * b : 3 * b + 3]
        weights = [(gate_ref, up_ref)[w] for w in which]
        copies = block_copies(width, distances[b], weights, held, sems, last=b > 0)
        work.append((outs[b], held, total, copies))
    waiting = [step[-1] for block in work for step in block[-1]]
    in_flight = IN_FLIGHT if len(blocks) > 1 else len(waiting)
    for copy in waiting[:in_flight]:
        copy.start()
    waiting = waiting[in_flight:]
    for (out, held, total, copies), which in zip(work, blocks):
        multiply(x_ref, held, total, copies, waiting)
        if len(which) == 2:
            pack_pair(out, total[0], total[1])
        else:
            pack_single(out, total[0])


def gate_up_stream(features, gate_weight, up_weight, distances, blocks, width, after):
    rows, depth = features.shape
    scratch, shapes = [], []
    for b, which in enumerate(blocks):
        packed = packed_pair_width(rows, width) if len(which) == 2 else packed_width(rows, width)
        shapes.append(jax.ShapeDtypeStruct((8, packed), jnp.bfloat16))
        scratch += [
            pltpu.VMEM((len(which), depth, width), jnp.bfloat16),
            pltpu.VMEM((len(which), rows, width), jnp.float32),
            pltpu.SemaphoreType.DMA((len(which), len(copy_pieces(depth, b > 0)))),
        ]
    held_mib = -(-depth * width * 2 * sum(len(which) for which in blocks) // MIB)
    return pl.pallas_call(
        functools.partial(stream_kernel, width, blocks, distances),
        out_shape=shapes,
        in_specs=[WHOLE, IN_HBM, IN_HBM, ANY],
        out_specs=[WHOLE] * len(blocks),
        scratch_shapes=scratch,
        compiler_params=params(5 + held_mib),
        cost_estimate=SMALL,
    )(features, in_hbm(gate_weight), in_hbm(up_weight), after)


def hidden_tail(rows, width):
    half = pl.cdiv(width // 2, 128) * 128
    return half if rows % 8 else 0


def packed_width(rows, width):
    return (rows // 8) * width + hidden_tail(rows, width)


def pack_single(out, value):
    rows, width = value.shape
    for g in range(rows // 8):
        out[:, g * width : (g + 1) * width] = value[8 * g : 8 * g + 8].astype(out.dtype)
    if rows % 8:
        at, half = (rows // 8) * width, hidden_tail(rows, width)
        left, right = value[rows - 4 :, :half], value[rows - 4 :, half:]
        if 2 * half > width:
            right = jnp.concatenate([right, jnp.zeros((4, 2 * half - width), jnp.float32)], axis=1)
        out[:, at : at + half] = jnp.concatenate([left, right], axis=0).astype(out.dtype)


def last_rows(packed, rows, width):
    at, half = (rows // 8) * width, hidden_tail(rows, width)
    tail = packed[:, at : at + half].astype(jnp.float32)
    return jnp.concatenate([tail[:4], tail[4:, : width - half]], axis=1)


def activate_kernel(rows, width, own, far, gate_near, up_near, out):
    def pair(at):
        columns = slice(at, at + width)
        return own[:, columns].astype(jnp.float32) + far[:, columns].astype(jnp.float32)

    for g in range(rows // 8):
        near = slice(g * width, (g + 1) * width)
        out[:, near] = activate(
            pair(2 * g * width) + gate_near[:, near].astype(jnp.float32),
            pair((2 * g + 1) * width) + up_near[:, near].astype(jnp.float32),
        )
    if rows % 8:
        half = hidden_tail(rows, width)
        last = pair((rows // 8) * 2 * width)
        value = activate(
            last[:4] + last_rows(gate_near, rows, width),
            last[4:] + last_rows(up_near, rows, width),
        ).astype(jnp.float32)
        right = jnp.concatenate([value[:, half:], jnp.zeros((4, 2 * half - width), jnp.float32)], axis=1)
        at = (rows // 8) * width
        out[:, at : at + half] = jnp.concatenate([value[:, :half], right], axis=0).astype(out.dtype)


def activate_packed(own, far, near, rows, width):
    return pl.pallas_call(
        functools.partial(activate_kernel, rows, width),
        out_shape=jax.ShapeDtypeStruct((8, packed_width(rows, width)), jnp.bfloat16),
        in_specs=[WHOLE] * 4,
        out_specs=WHOLE,
        compiler_params=params(8),
        cost_estimate=SMALL,
    )(own, far, *near)


def pack_rows(out, value):
    rows, width = value.shape
    for g in range(rows // 8):
        out[:, g * width : (g + 1) * width] = value[8 * g : 8 * g + 8].astype(out.dtype)
    piece = width // 8
    for r in range(rows // 8 * 8, rows):
        at = (rows // 8) * width + (r % 8) * piece
        row = jnp.concatenate(
            [value[r : r + 1, i * piece : (i + 1) * piece] for i in range(8)], axis=0
        )
        out[:, at : at + piece] = row.astype(out.dtype)


def unpack_rows(out, packed):
    rows, width = out.shape
    for g in range(rows // 8):
        out[8 * g : 8 * g + 8, :] = packed[:, g * width : (g + 1) * width]
    piece = width // 8
    for r in range(rows // 8 * 8, rows):
        at = (rows // 8) * width + (r % 8) * piece
        for i in range(8):
            out[r : r + 1, i * piece : (i + 1) * piece] = packed[i : i + 1, at : at + piece]


def down_kernel(first, rows, width, distances, *refs):
    blocks = len(distances)
    hidden, refs = refs[:blocks], refs[blocks:]
    if not first:
        before, refs = refs[0], refs[1:]
    held, outs, (plain, total) = refs[0], refs[1:-2], refs[-2:]
    if first:
        total = outs[0]
    for b in range(blocks):
        for g in range(rows // 8):
            plain[8 * g : 8 * g + 8, :] = hidden[b][:, g * width : (g + 1) * width].astype(jnp.float32)
        if rows % 8:
            at, half = (rows // 8) * width, hidden_tail(rows, width)
            tail = hidden[b][:, at : at + half].astype(jnp.float32)
            plain[rows - 4 :, :half] = tail[:4]
            plain[rows - 4 :, half:] = tail[4:, : width - half]
        for row, tall in pieces_of(width, HELD_STEP):
            term = jnp.dot(
                plain[:, row : row + tall].astype(jnp.bfloat16),
                held[pl.ds(pl.multiple_of(block_start(distances[b], width) + row, 128), tall), :],
                preferred_element_type=jnp.float32,
            )
            if b == 0 and row == 0:
                total[...] = term if first else before[...] + term
            else:
                total[...] += term
    if not first:
        tall = rows // len(outs)
        for r, out in enumerate(outs):
            pack_rows(out, total[r * tall : (r + 1) * tall, :])


def down(hidden, distances, before, weight, rows, width, outs):
    columns = weight.shape[1]
    if before is None:
        shapes = [jax.ShapeDtypeStruct((rows, columns), jnp.float32)]
    else:
        packed = (8, rows // outs * columns // 8)
        shapes = [jax.ShapeDtypeStruct(packed, jnp.bfloat16 if r else jnp.float32) for r in range(outs)]
    carried = [] if before is None else [before]
    return pl.pallas_call(
        functools.partial(down_kernel, before is None, rows, width, distances),
        out_shape=shapes,
        in_specs=[WHOLE] * (len(hidden) + len(carried) + 1),
        out_specs=[WHOLE] * len(shapes),
        scratch_shapes=[
            pltpu.VMEM((rows, width), jnp.float32),
            pltpu.VMEM((rows, columns), jnp.float32),
        ],
        compiler_params=params(8),
        cost_estimate=SMALL,
    )(*hidden, *carried, in_vmem(weight))


def finish_kernel(*refs):
    terms, out, plain = refs[:-2], refs[-2], refs[-1]
    packed = terms[0][...]
    for term in terms[1:]:
        packed = packed + term[...].astype(jnp.float32)
    unpack_rows(plain, packed)
    out[...] = plain[...].astype(out.dtype)


def finish(terms, shape):
    return pl.pallas_call(
        finish_kernel,
        out_shape=jax.ShapeDtypeStruct(shape, jnp.bfloat16),
        in_specs=[WHOLE] * len(terms),
        out_specs=WHOLE,
        scratch_shapes=[pltpu.VMEM(shape, jnp.float32)],
        compiler_params=params(4),
        cost_estimate=SMALL,
    )(*terms)


def swap(value, axes, size, distance):
    return lax.ppermute(value, axes, [(i, i ^ distance) for i in range(size)])


def add(a, b):
    return a.astype(jnp.float32) + b.astype(jnp.float32)


def direct(tokens, gate_weight, up_weight, down_weight):
    n_gx = lax.axis_size("gx")
    n_token = lax.axis_size(TOKEN_AXES)
    width = gate_weight.shape[1] // n_gx

    held = fetch(gate_weight, up_weight, 3, width)
    features = jnp.concatenate(
        [tokens] + [swap(tokens, TOKEN_AXES, n_token, r) for r in range(1, n_token)], axis=0
    )
    rows = features.shape[0]

    def blocks_for(distances, blocks, after):
        return gate_up_stream(features, gate_weight, up_weight, distances, blocks, width, after)

    relayed = gate_up_held(features, held)
    arrived = swap(relayed, "gx", n_gx, 1)
    across, beside = blocks_for((2, 1), ((0, 1), (0,)), relayed)
    across = lax.optimization_barrier(add(across, arrived).astype(jnp.bfloat16))
    far = swap(across, "gx", n_gx, 2)
    near = [swap(beside, "gx", n_gx, 1)]
    (beside,) = blocks_for((1,), ((1,),), across)
    near.append(swap(beside, "gx", n_gx, 1))
    (own,) = blocks_for((0,), ((0, 1),), beside)
    hidden = activate_packed(own, far, near, rows, width)

    opposite = swap(hidden, "gx", n_gx, 2)
    first = [hidden, swap(hidden, "gx", n_gx, 1), opposite]
    second = [swap(opposite, "gx", n_gx, 1)]
    (partial_sum,) = down(first, (0, 1, 2), None, down_weight, rows, width, 1)
    outs = down(second, (3,), partial_sum, down_weight, rows, width, n_token)
    terms = [outs[0]] + [swap(outs[r], TOKEN_AXES, n_token, r) for r in range(1, n_token)]
    return finish(terms, tokens.shape)


def offloaded(tokens, gate_weight, up_weight, down_weight):
    features = lax.all_gather(tokens, TOKEN_AXES, axis=0, tiled=True)
    hidden_width = gate_weight.shape[1]
    gate_part = jnp.dot(features, gate_weight, preferred_element_type=jnp.float32)
    up_part = jnp.dot(features, up_weight, preferred_element_type=jnp.float32)
    summed = lax.psum(
        jnp.concatenate([gate_part, up_part], axis=1).astype(jnp.bfloat16), "gx"
    ).astype(jnp.float32)
    hidden = activate(summed[:, :hidden_width], summed[:, hidden_width:])
    partial_value = jnp.dot(hidden, down_weight, preferred_element_type=jnp.float32)
    return lax.psum_scatter(
        partial_value.astype(jnp.bfloat16), TOKEN_AXES, scatter_dimension=0, tiled=True
    )


def shards(tokens, gate_weight, up_weight, down_weight):
    n_gx = lax.axis_size("gx")
    n_token = lax.axis_size(TOKEN_AXES)
    rows = tokens.shape[0] * n_token
    tokens_fit = n_token > 1 and n_token & (n_token - 1) == 0 and rows % 4 == 0
    weights_fit = gate_weight.shape[1] % (128 * 4) == 0 and gate_weight.shape[0] % STEP == 0
    columns_fit = down_weight.shape[1] % (128 * 8) == 0
    if n_gx == 4 and tokens_fit and weights_fit and columns_fit:
        return direct(tokens, gate_weight, up_weight, down_weight)
    return offloaded(tokens, gate_weight, up_weight, down_weight)


def solution(mesh):
    return jax.shard_map(
        shards,
        mesh=mesh,
        in_specs=(
            P(("grp", "gy", "gz"), "gx"),
            P("gx", ("gy", "gz")),
            P("gx", ("gy", "gz")),
            P(("gy", "gz"), "gx"),
        ),
        out_specs=P(("grp", "gy", "gz"), "gx"),
        check_vma=False,
    )
```

```python
import functools

import jax
import jax.numpy as jnp
from jax import lax
from jax.experimental import pallas as pl
from jax.experimental.pallas import tpu as pltpu
from jax.sharding import PartitionSpec as P

MIB = 1 << 20
STEP = 256
COPY_STEP = 512
LARGE_STEP = 1024
IN_FLIGHT = 4
DOWN_STEP = 512
TOKEN_AXES = ("gy", "gz")
IN_HBM = pl.BlockSpec(memory_space=pltpu.HBM)
ANY = pl.BlockSpec(memory_space=pl.ANY)
WHOLE = pl.BlockSpec(memory_space=pltpu.VMEM)


def activate(gate, up):
    return (jax.nn.silu(gate) * up).astype(jnp.bfloat16)


def pieces_of(total, step):
    return [(start, min(step, total - start)) for start in range(0, total, step)]


def in_hbm(value):
    return pltpu.with_memory_space_constraint(value, pltpu.HBM)


def in_vmem(value):
    return pltpu.with_memory_space_constraint(value, pltpu.VMEM)


SMALL = pl.CostEstimate(flops=0, bytes_accessed=MIB, transcendentals=0)


def block_start(distance, width):
    return pl.multiple_of((lax.axis_index("gx") ^ distance) * width, 128)


def params(mib):
    return pltpu.CompilerParams(vmem_limit_bytes=mib * MIB)


def packed_pair_width(rows, width):
    return (rows // 8) * 2 * width + (width if rows % 8 else 0)


def pack_pair(out, gate, up):
    rows, width = gate.shape
    for g in range(rows // 8):
        for w, value in enumerate((gate, up)):
            at = (2 * g + w) * width
            out[:, at : at + width] = value[8 * g : 8 * g + 8].astype(out.dtype)
    if rows % 8:
        at = (rows // 8) * 2 * width
        tail = jnp.concatenate([gate[rows - 4 :], up[rows - 4 :]], axis=0)
        out[:, at : at + width] = tail.astype(out.dtype)


def block_copies(width, distance, weights, held, sems, step=COPY_STEP):
    columns = pl.ds(block_start(distance, width), width)
    copies = []
    for k, (row, rows) in enumerate(pieces_of(held.shape[1], step)):
        for w, weight in enumerate(weights):
            copy = pltpu.make_async_copy(
                weight.at[pl.ds(row, rows), columns], held.at[w, pl.ds(row, rows)], sems.at[w, k]
            )
            copies.append((w, row, rows, copy))
    return copies


def fetch_kernel(width, distance, gate_ref, up_ref, held, sems):
    copies = block_copies(width, distance, (gate_ref, up_ref), held, sems)
    for _, _, _, copy in copies:
        copy.start()
    for _, _, _, copy in copies:
        copy.wait()


def fetch(gate_weight, up_weight, distance, width):
    depth = gate_weight.shape[0]
    return pl.pallas_call(
        functools.partial(fetch_kernel, width, distance),
        out_shape=pltpu.VMEM((2, depth, width), jnp.bfloat16),
        in_specs=[IN_HBM, IN_HBM],
        out_specs=WHOLE,
        scratch_shapes=[pltpu.SemaphoreType.DMA((2, len(pieces_of(depth, COPY_STEP))))],
        compiler_params=params(4),
        cost_estimate=SMALL,
    )(in_hbm(gate_weight), in_hbm(up_weight))


def multiply(x_ref, held, total, steps, waiting=()):
    for w, first, tall, copy in steps:
        if copy is not None:
            copy.wait()
        if waiting:
            waiting.pop(0).start()
        for row, rows in pieces_of(tall, STEP):
            rows = slice(first + row, first + row + rows)
            term = jnp.dot(x_ref[:, rows], held[w, rows, :], preferred_element_type=jnp.float32)
            if rows.start == 0:
                total[w] = term
            else:
                total[w] += term


def held_kernel(x_ref, held, out, total):
    parts = pieces_of(x_ref.shape[1], STEP)
    multiply(x_ref, held, total, [(w, row, rows, None) for w in range(2) for row, rows in parts])
    pack_pair(out, total[0], total[1])


def gate_up_held(features, held):
    rows, width = features.shape[0], held.shape[2]
    return pl.pallas_call(
        held_kernel,
        out_shape=jax.ShapeDtypeStruct((8, packed_pair_width(rows, width)), jnp.bfloat16),
        in_specs=[WHOLE, WHOLE],
        out_specs=WHOLE,
        scratch_shapes=[pltpu.VMEM((2, rows, width), jnp.float32)],
        compiler_params=params(8),
        cost_estimate=SMALL,
    )(features, in_vmem(held))


def stream_step(blocks):
    return COPY_STEP if len(blocks) == 1 else LARGE_STEP


def stream_kernel(width, blocks, distances, x_ref, gate_ref, up_ref, _, *refs):
    outs, refs = refs[: len(blocks)], refs[len(blocks) :]
    work = []
    for b, which in enumerate(blocks):
        held, total, sems = refs[3 * b : 3 * b + 3]
        weights = [(gate_ref, up_ref)[w] for w in which]
        copies = block_copies(width, distances[b], weights, held, sems, stream_step(blocks))
        work.append((outs[b], held, total, copies))
    waiting = [step[-1] for block in work for step in block[-1]]
    alone = len(blocks) == 1
    in_flight = len(waiting) if alone else IN_FLIGHT
    for copy in waiting[:in_flight]:
        copy.start(priority=int(alone))
    waiting = waiting[in_flight:]
    for (out, held, total, copies), which in zip(work, blocks):
        multiply(x_ref, held, total, copies, waiting)
        if len(which) == 2:
            pack_pair(out, total[0], total[1])
        else:
            pack_single(out, total[0])


def gate_up_stream(features, gate_weight, up_weight, distances, blocks, width, after):
    rows, depth = features.shape
    scratch, shapes = [], []
    for which in blocks:
        packed = packed_pair_width(rows, width) if len(which) == 2 else packed_width(rows, width)
        shapes.append(jax.ShapeDtypeStruct((8, packed), jnp.bfloat16))
        scratch += [
            pltpu.VMEM((len(which), depth, width), jnp.bfloat16),
            pltpu.VMEM((len(which), rows, width), jnp.float32),
            pltpu.SemaphoreType.DMA((len(which), len(pieces_of(depth, stream_step(blocks))))),
        ]
    held_mib = -(-depth * width * 2 * sum(len(which) for which in blocks) // MIB)
    return pl.pallas_call(
        functools.partial(stream_kernel, width, blocks, distances),
        out_shape=shapes,
        in_specs=[WHOLE, IN_HBM, IN_HBM, ANY],
        out_specs=[WHOLE] * len(blocks),
        scratch_shapes=scratch,
        compiler_params=params(5 + held_mib),
        cost_estimate=SMALL,
    )(features, in_hbm(gate_weight), in_hbm(up_weight), after)


def hidden_tail(rows, width):
    half = pl.cdiv(width // 2, 128) * 128
    return half if rows % 8 else 0


def packed_width(rows, width):
    return (rows // 8) * width + hidden_tail(rows, width)


def pack_single(out, value):
    rows, width = value.shape
    for g in range(rows // 8):
        out[:, g * width : (g + 1) * width] = value[8 * g : 8 * g + 8].astype(out.dtype)
    if rows % 8:
        at, half = (rows // 8) * width, hidden_tail(rows, width)
        left, right = value[rows - 4 :, :half], value[rows - 4 :, half:]
        if 2 * half > width:
            right = jnp.concatenate([right, jnp.zeros((4, 2 * half - width), jnp.float32)], axis=1)
        out[:, at : at + half] = jnp.concatenate([left, right], axis=0).astype(out.dtype)


def last_rows(packed, rows, width):
    at, half = (rows // 8) * width, hidden_tail(rows, width)
    tail = packed[:, at : at + half].astype(jnp.float32)
    return jnp.concatenate([tail[:4], tail[4:, : width - half]], axis=1)


def activate_kernel(rows, width, own, far, gate_near, up_near, out):
    def pair(at):
        columns = slice(at, at + width)
        return own[:, columns].astype(jnp.float32) + far[:, columns].astype(jnp.float32)

    for g in range(rows // 8):
        near = slice(g * width, (g + 1) * width)
        out[:, near] = activate(
            pair(2 * g * width) + gate_near[:, near].astype(jnp.float32),
            pair((2 * g + 1) * width) + up_near[:, near].astype(jnp.float32),
        )
    if rows % 8:
        half = hidden_tail(rows, width)
        last = pair((rows // 8) * 2 * width)
        value = activate(
            last[:4] + last_rows(gate_near, rows, width),
            last[4:] + last_rows(up_near, rows, width),
        ).astype(jnp.float32)
        right = jnp.concatenate([value[:, half:], jnp.zeros((4, 2 * half - width), jnp.float32)], axis=1)
        at = (rows // 8) * width
        out[:, at : at + half] = jnp.concatenate([value[:, :half], right], axis=0).astype(out.dtype)


def activate_packed(own, far, near, rows, width):
    return pl.pallas_call(
        functools.partial(activate_kernel, rows, width),
        out_shape=jax.ShapeDtypeStruct((8, packed_width(rows, width)), jnp.bfloat16),
        in_specs=[WHOLE] * 4,
        out_specs=WHOLE,
        compiler_params=params(8),
        cost_estimate=SMALL,
    )(own, far, *near)


def pack_rows(out, value):
    rows, width = value.shape
    for g in range(rows // 8):
        out[:, g * width : (g + 1) * width] = value[8 * g : 8 * g + 8].astype(out.dtype)
    piece = width // 8
    for r in range(rows // 8 * 8, rows):
        at = (rows // 8) * width + (r % 8) * piece
        row = jnp.concatenate(
            [value[r : r + 1, i * piece : (i + 1) * piece] for i in range(8)], axis=0
        )
        out[:, at : at + piece] = row.astype(out.dtype)


def unpack_rows(out, packed):
    rows, width = out.shape
    for g in range(rows // 8):
        out[8 * g : 8 * g + 8, :] = packed[:, g * width : (g + 1) * width]
    piece = width // 8
    for r in range(rows // 8 * 8, rows):
        at = (rows // 8) * width + (r % 8) * piece
        for i in range(8):
            out[r : r + 1, i * piece : (i + 1) * piece] = packed[i : i + 1, at : at + piece]


def down_kernel(first, rows, width, distances, *refs):
    blocks = len(distances)
    hidden, refs = refs[:blocks], refs[blocks:]
    if not first:
        before, refs = refs[0], refs[1:]
    held, outs, (plain, total) = refs[0], refs[1:-2], refs[-2:]
    if first:
        total = outs[0]
    for b in range(blocks):
        for g in range(rows // 8):
            plain[8 * g : 8 * g + 8, :] = hidden[b][:, g * width : (g + 1) * width].astype(jnp.float32)
        if rows % 8:
            at, half = (rows // 8) * width, hidden_tail(rows, width)
            tail = hidden[b][:, at : at + half].astype(jnp.float32)
            plain[rows - 4 :, :half] = tail[:4]
            plain[rows - 4 :, half:] = tail[4:, : width - half]
        for row, tall in pieces_of(width, DOWN_STEP):
            term = jnp.dot(
                plain[:, row : row + tall].astype(jnp.bfloat16),
                held[pl.ds(pl.multiple_of(block_start(distances[b], width) + row, 128), tall), :],
                preferred_element_type=jnp.float32,
            )
            if b == 0 and row == 0:
                total[...] = term if first else before[...] + term
            else:
                total[...] += term
    if not first:
        tall = rows // len(outs)
        for r, out in enumerate(outs):
            pack_rows(out, total[r * tall : (r + 1) * tall, :])


def down(hidden, distances, before, weight, rows, width, outs):
    columns = weight.shape[1]
    if before is None:
        shapes = [jax.ShapeDtypeStruct((rows, columns), jnp.float32)]
    else:
        packed = (8, rows // outs * columns // 8)
        shapes = [jax.ShapeDtypeStruct(packed, jnp.bfloat16 if r else jnp.float32) for r in range(outs)]
    carried = [] if before is None else [before]
    return pl.pallas_call(
        functools.partial(down_kernel, before is None, rows, width, distances),
        out_shape=shapes,
        in_specs=[WHOLE] * (len(hidden) + len(carried) + 1),
        out_specs=[WHOLE] * len(shapes),
        scratch_shapes=[
            pltpu.VMEM((rows, width), jnp.float32),
            pltpu.VMEM((rows, columns), jnp.float32),
        ],
        compiler_params=params(8),
        cost_estimate=SMALL,
    )(*hidden, *carried, in_vmem(weight))


def finish_kernel(*refs):
    terms, out, plain = refs[:-2], refs[-2], refs[-1]
    packed = terms[0][...]
    for term in terms[1:]:
        packed = packed + term[...].astype(jnp.float32)
    unpack_rows(plain, packed)
    out[...] = plain[...].astype(out.dtype)


def finish(terms, shape):
    return pl.pallas_call(
        finish_kernel,
        out_shape=jax.ShapeDtypeStruct(shape, jnp.bfloat16),
        in_specs=[WHOLE] * len(terms),
        out_specs=WHOLE,
        scratch_shapes=[pltpu.VMEM(shape, jnp.float32)],
        compiler_params=params(4),
        cost_estimate=SMALL,
    )(*terms)


def swap(value, axes, size, distance):
    return lax.ppermute(value, axes, [(i, i ^ distance) for i in range(size)])


def add(a, b):
    return a.astype(jnp.float32) + b.astype(jnp.float32)


def direct(tokens, gate_weight, up_weight, down_weight):
    n_gx = lax.axis_size("gx")
    n_token = lax.axis_size(TOKEN_AXES)
    width = gate_weight.shape[1] // n_gx

    held = fetch(gate_weight, up_weight, 3, width)
    features = jnp.concatenate(
        [tokens] + [swap(tokens, TOKEN_AXES, n_token, r) for r in range(1, n_token)], axis=0
    )
    rows = features.shape[0]

    def blocks_for(distances, blocks, after):
        return gate_up_stream(features, gate_weight, up_weight, distances, blocks, width, after)

    relayed = gate_up_held(features, held)
    arrived = swap(relayed, "gx", n_gx, 1)
    across, beside = blocks_for((2, 1), ((0, 1), (0,)), relayed)
    across = lax.optimization_barrier(add(across, arrived).astype(jnp.bfloat16))
    far = swap(across, "gx", n_gx, 2)
    near = [swap(beside, "gx", n_gx, 1)]
    (beside,) = blocks_for((1,), ((1,),), across)
    near.append(swap(beside, "gx", n_gx, 1))
    (own,) = blocks_for((0,), ((0, 1),), beside)
    hidden = activate_packed(own, far, near, rows, width)

    opposite = swap(hidden, "gx", n_gx, 2)
    first = [hidden, swap(hidden, "gx", n_gx, 1), opposite]
    second = [swap(opposite, "gx", n_gx, 1)]
    (partial_sum,) = down(first, (0, 1, 2), None, down_weight, rows, width, 1)
    outs = down(second, (3,), partial_sum, down_weight, rows, width, n_token)
    terms = [outs[0]] + [swap(outs[r], TOKEN_AXES, n_token, r) for r in range(1, n_token)]
    return finish(terms, tokens.shape)


def offloaded(tokens, gate_weight, up_weight, down_weight):
    features = lax.all_gather(tokens, TOKEN_AXES, axis=0, tiled=True)
    hidden_width = gate_weight.shape[1]
    gate_part = jnp.dot(features, gate_weight, preferred_element_type=jnp.float32)
    up_part = jnp.dot(features, up_weight, preferred_element_type=jnp.float32)
    summed = lax.psum(
        jnp.concatenate([gate_part, up_part], axis=1).astype(jnp.bfloat16), "gx"
    ).astype(jnp.float32)
    hidden = activate(summed[:, :hidden_width], summed[:, hidden_width:])
    partial_value = jnp.dot(hidden, down_weight, preferred_element_type=jnp.float32)
    return lax.psum_scatter(
        partial_value.astype(jnp.bfloat16), TOKEN_AXES, scatter_dimension=0, tiled=True
    )


def shards(tokens, gate_weight, up_weight, down_weight):
    n_gx = lax.axis_size("gx")
    n_token = lax.axis_size(TOKEN_AXES)
    rows = tokens.shape[0] * n_token
    tokens_fit = n_token > 1 and n_token & (n_token - 1) == 0 and rows % 4 == 0
    weights_fit = gate_weight.shape[1] % (128 * 4) == 0 and gate_weight.shape[0] % STEP == 0
    columns_fit = down_weight.shape[1] % (128 * 8) == 0
    if n_gx == 4 and tokens_fit and weights_fit and columns_fit:
        return direct(tokens, gate_weight, up_weight, down_weight)
    return offloaded(tokens, gate_weight, up_weight, down_weight)


def solution(mesh):
    return jax.shard_map(
        shards,
        mesh=mesh,
        in_specs=(
            P(("grp", "gy", "gz"), "gx"),
            P("gx", ("gy", "gz")),
            P("gx", ("gy", "gz")),
            P(("gy", "gz"), "gx"),
        ),
        out_specs=P(("grp", "gy", "gz"), "gx"),
        check_vma=False,
    )
```

```python
import functools

import jax
import jax.numpy as jnp
from jax import lax
from jax.experimental import pallas as pl
from jax.experimental.pallas import tpu as pltpu
from jax.sharding import PartitionSpec as P

MIB = 1 << 20
STEP = 256
COPY_STEP = 512
IN_FLIGHT = 6
DOWN_STEP = 512
TOKEN_AXES = ("gy", "gz")
IN_HBM = pl.BlockSpec(memory_space=pltpu.HBM)
ANY = pl.BlockSpec(memory_space=pl.ANY)
WHOLE = pl.BlockSpec(memory_space=pltpu.VMEM)


def activate(gate, up):
    return (jax.nn.silu(gate) * up).astype(jnp.bfloat16)


def pieces_of(total, step):
    return [(start, min(step, total - start)) for start in range(0, total, step)]


def in_hbm(value):
    return pltpu.with_memory_space_constraint(value, pltpu.HBM)


def in_vmem(value):
    return pltpu.with_memory_space_constraint(value, pltpu.VMEM)


SMALL = pl.CostEstimate(flops=0, bytes_accessed=MIB, transcendentals=0)


def block_start(distance, width):
    return pl.multiple_of((lax.axis_index("gx") ^ distance) * width, 128)


def params(mib):
    return pltpu.CompilerParams(vmem_limit_bytes=mib * MIB)


def packed_pair_width(rows, width):
    return (rows // 8) * 2 * width + (width if rows % 8 else 0)


def pack_pair(out, gate, up):
    rows, width = gate.shape
    for g in range(rows // 8):
        for w, value in enumerate((gate, up)):
            at = (2 * g + w) * width
            out[:, at : at + width] = value[8 * g : 8 * g + 8].astype(out.dtype)
    if rows % 8:
        at = (rows // 8) * 2 * width
        tail = jnp.concatenate([gate[rows - 4 :], up[rows - 4 :]], axis=0)
        out[:, at : at + width] = tail.astype(out.dtype)


def block_copies(width, distance, weights, held, sems):
    columns = pl.ds(block_start(distance, width), width)
    copies = []
    for k, (row, rows) in enumerate(pieces_of(held.shape[1], COPY_STEP)):
        for w, weight in enumerate(weights):
            copy = pltpu.make_async_copy(
                weight.at[pl.ds(row, rows), columns], held.at[w, pl.ds(row, rows)], sems.at[w, k]
            )
            copies.append((w, row, rows, copy))
    return copies


def fetch_kernel(width, distance, gate_ref, up_ref, held, sems):
    copies = block_copies(width, distance, (gate_ref, up_ref), held, sems)
    for _, _, _, copy in copies:
        copy.start()
    for _, _, _, copy in copies:
        copy.wait()


def fetch(gate_weight, up_weight, distance, width):
    depth = gate_weight.shape[0]
    return pl.pallas_call(
        functools.partial(fetch_kernel, width, distance),
        out_shape=pltpu.VMEM((2, depth, width), jnp.bfloat16),
        in_specs=[IN_HBM, IN_HBM],
        out_specs=WHOLE,
        scratch_shapes=[pltpu.SemaphoreType.DMA((2, len(pieces_of(depth, COPY_STEP))))],
        compiler_params=params(4),
        cost_estimate=SMALL,
    )(in_hbm(gate_weight), in_hbm(up_weight))


def multiply(x_ref, held, total, steps, waiting=()):
    for w, first, tall, copy in steps:
        if copy is not None:
            copy.wait()
        if waiting:
            waiting.pop(0).start()
        for row, rows in pieces_of(tall, STEP):
            rows = slice(first + row, first + row + rows)
            term = jnp.dot(x_ref[:, rows], held[w, rows, :], preferred_element_type=jnp.float32)
            if rows.start == 0:
                total[w] = term
            else:
                total[w] += term


def held_kernel(x_ref, held, out, total):
    parts = pieces_of(x_ref.shape[1], STEP)
    multiply(x_ref, held, total, [(w, row, rows, None) for w in range(2) for row, rows in parts])
    pack_pair(out, total[0], total[1])


def gate_up_held(features, held):
    rows, width = features.shape[0], held.shape[2]
    return pl.pallas_call(
        held_kernel,
        out_shape=jax.ShapeDtypeStruct((8, packed_pair_width(rows, width)), jnp.bfloat16),
        in_specs=[WHOLE, WHOLE],
        out_specs=WHOLE,
        scratch_shapes=[pltpu.VMEM((2, rows, width), jnp.float32)],
        compiler_params=params(8),
        cost_estimate=SMALL,
    )(features, in_vmem(held))


def stream_kernel(width, blocks, distances, x_ref, gate_ref, up_ref, _, *refs):
    outs, refs = refs[: len(blocks)], refs[len(blocks) :]
    work = []
    for b, which in enumerate(blocks):
        held, total, sems = refs[3 * b : 3 * b + 3]
        weights = [(gate_ref, up_ref)[w] for w in which]
        copies = block_copies(width, distances[b], weights, held, sems)
        work.append((outs[b], held, total, copies))
    waiting = [step[-1] for block in work for step in block[-1]]
    in_flight = IN_FLIGHT if len(blocks) > 1 else len(waiting)
    for copy in waiting[:in_flight]:
        copy.start()
    waiting = waiting[in_flight:]
    for (out, held, total, copies), which in zip(work, blocks):
        multiply(x_ref, held, total, copies, waiting)
        if len(which) == 2:
            pack_pair(out, total[0], total[1])
        else:
            pack_single(out, total[0])


def gate_up_stream(features, gate_weight, up_weight, distances, blocks, width, after):
    rows, depth = features.shape
    scratch, shapes = [], []
    for which in blocks:
        packed = packed_pair_width(rows, width) if len(which) == 2 else packed_width(rows, width)
        shapes.append(jax.ShapeDtypeStruct((8, packed), jnp.bfloat16))
        scratch += [
            pltpu.VMEM((len(which), depth, width), jnp.bfloat16),
            pltpu.VMEM((len(which), rows, width), jnp.float32),
            pltpu.SemaphoreType.DMA((len(which), len(pieces_of(depth, COPY_STEP)))),
        ]
    held_mib = -(-depth * width * 2 * sum(len(which) for which in blocks) // MIB)
    return pl.pallas_call(
        functools.partial(stream_kernel, width, blocks, distances),
        out_shape=shapes,
        in_specs=[WHOLE, IN_HBM, IN_HBM, ANY],
        out_specs=[WHOLE] * len(blocks),
        scratch_shapes=scratch,
        compiler_params=params(5 + held_mib),
        cost_estimate=SMALL,
    )(features, in_hbm(gate_weight), in_hbm(up_weight), after)


def hidden_tail(rows, width):
    half = pl.cdiv(width // 2, 128) * 128
    return half if rows % 8 else 0


def packed_width(rows, width):
    return (rows // 8) * width + hidden_tail(rows, width)


def pack_single(out, value):
    rows, width = value.shape
    for g in range(rows // 8):
        out[:, g * width : (g + 1) * width] = value[8 * g : 8 * g + 8].astype(out.dtype)
    if rows % 8:
        at, half = (rows // 8) * width, hidden_tail(rows, width)
        left, right = value[rows - 4 :, :half], value[rows - 4 :, half:]
        if 2 * half > width:
            right = jnp.concatenate([right, jnp.zeros((4, 2 * half - width), jnp.float32)], axis=1)
        out[:, at : at + half] = jnp.concatenate([left, right], axis=0).astype(out.dtype)


def last_rows(packed, rows, width):
    at, half = (rows // 8) * width, hidden_tail(rows, width)
    tail = packed[:, at : at + half].astype(jnp.float32)
    return jnp.concatenate([tail[:4], tail[4:, : width - half]], axis=1)


def activate_kernel(rows, width, own, far, gate_near, up_near, out):
    def pair(at):
        columns = slice(at, at + width)
        return own[:, columns].astype(jnp.float32) + far[:, columns].astype(jnp.float32)

    for g in range(rows // 8):
        near = slice(g * width, (g + 1) * width)
        out[:, near] = activate(
            pair(2 * g * width) + gate_near[:, near].astype(jnp.float32),
            pair((2 * g + 1) * width) + up_near[:, near].astype(jnp.float32),
        )
    if rows % 8:
        half = hidden_tail(rows, width)
        last = pair((rows // 8) * 2 * width)
        value = activate(
            last[:4] + last_rows(gate_near, rows, width),
            last[4:] + last_rows(up_near, rows, width),
        ).astype(jnp.float32)
        right = jnp.concatenate([value[:, half:], jnp.zeros((4, 2 * half - width), jnp.float32)], axis=1)
        at = (rows // 8) * width
        out[:, at : at + half] = jnp.concatenate([value[:, :half], right], axis=0).astype(out.dtype)


def activate_packed(own, far, near, rows, width):
    return pl.pallas_call(
        functools.partial(activate_kernel, rows, width),
        out_shape=jax.ShapeDtypeStruct((8, packed_width(rows, width)), jnp.bfloat16),
        in_specs=[WHOLE] * 4,
        out_specs=WHOLE,
        compiler_params=params(8),
        cost_estimate=SMALL,
    )(own, far, *near)


def pack_rows(out, value):
    rows, width = value.shape
    for g in range(rows // 8):
        out[:, g * width : (g + 1) * width] = value[8 * g : 8 * g + 8].astype(out.dtype)
    piece = width // 8
    for r in range(rows // 8 * 8, rows):
        at = (rows // 8) * width + (r % 8) * piece
        row = jnp.concatenate(
            [value[r : r + 1, i * piece : (i + 1) * piece] for i in range(8)], axis=0
        )
        out[:, at : at + piece] = row.astype(out.dtype)


def unpack_rows(out, packed):
    rows, width = out.shape
    for g in range(rows // 8):
        out[8 * g : 8 * g + 8, :] = packed[:, g * width : (g + 1) * width]
    piece = width // 8
    for r in range(rows // 8 * 8, rows):
        at = (rows // 8) * width + (r % 8) * piece
        for i in range(8):
            out[r : r + 1, i * piece : (i + 1) * piece] = packed[i : i + 1, at : at + piece]


def down_kernel(first, last, rows, width, distances, *refs):
    blocks = len(distances)
    hidden, refs = refs[:blocks], refs[blocks:]
    if not first:
        before, refs = refs[0], refs[1:]
    held, outs, (plain, total) = refs[0], refs[1:-2], refs[-2:]
    if not last:
        total = outs[0]
    for b in range(blocks):
        for g in range(rows // 8):
            plain[8 * g : 8 * g + 8, :] = hidden[b][:, g * width : (g + 1) * width].astype(jnp.float32)
        if rows % 8:
            plain[rows - 4 :, :] = last_rows(hidden[b], rows, width)
        for row, tall in pieces_of(width, DOWN_STEP):
            term = jnp.dot(
                plain[:, row : row + tall].astype(jnp.bfloat16),
                held[pl.ds(pl.multiple_of(block_start(distances[b], width) + row, 128), tall), :],
                preferred_element_type=jnp.float32,
            )
            if b == 0 and row == 0:
                total[...] = term if first else before[...] + term
            else:
                total[...] += term
    if last:
        tall = rows // len(outs)
        for r, out in enumerate(outs):
            pack_rows(out, total[r * tall : (r + 1) * tall, :])


def down(hidden, distances, before, weight, rows, width, outs):
    columns = weight.shape[1]
    if outs == 1:
        shapes = [jax.ShapeDtypeStruct((rows, columns), jnp.float32)]
    else:
        packed = (8, rows // outs * columns // 8)
        shapes = [jax.ShapeDtypeStruct(packed, jnp.bfloat16 if r else jnp.float32) for r in range(outs)]
    carried = [] if before is None else [before]
    return pl.pallas_call(
        functools.partial(down_kernel, before is None, outs > 1, rows, width, distances),
        out_shape=shapes,
        in_specs=[WHOLE] * (len(hidden) + len(carried) + 1),
        out_specs=[WHOLE] * len(shapes),
        scratch_shapes=[
            pltpu.VMEM((rows, width), jnp.float32),
            pltpu.VMEM((rows, columns), jnp.float32),
        ],
        compiler_params=params(8),
        cost_estimate=SMALL,
    )(*hidden, *carried, in_vmem(weight))


def finish_kernel(*refs):
    terms, out, plain = refs[:-2], refs[-2], refs[-1]
    packed = terms[0][...]
    for term in terms[1:]:
        packed = packed + term[...].astype(jnp.float32)
    unpack_rows(plain, packed)
    out[...] = plain[...].astype(out.dtype)


def finish(terms, shape):
    return pl.pallas_call(
        finish_kernel,
        out_shape=jax.ShapeDtypeStruct(shape, jnp.bfloat16),
        in_specs=[WHOLE] * len(terms),
        out_specs=WHOLE,
        scratch_shapes=[pltpu.VMEM(shape, jnp.float32)],
        compiler_params=params(4),
        cost_estimate=SMALL,
    )(*terms)


def swap(value, axes, size, distance):
    return lax.ppermute(value, axes, [(i, i ^ distance) for i in range(size)])


def add(a, b):
    return a.astype(jnp.float32) + b.astype(jnp.float32)


def direct(tokens, gate_weight, up_weight, down_weight):
    n_gx = lax.axis_size("gx")
    n_token = lax.axis_size(TOKEN_AXES)
    width = gate_weight.shape[1] // n_gx

    held = fetch(gate_weight, up_weight, 3, width)
    features = jnp.concatenate(
        [tokens] + [swap(tokens, TOKEN_AXES, n_token, r) for r in range(1, n_token)], axis=0
    )
    rows = features.shape[0]

    def blocks_for(distances, blocks, after):
        return gate_up_stream(features, gate_weight, up_weight, distances, blocks, width, after)

    relayed = gate_up_held(features, held)
    arrived = swap(relayed, "gx", n_gx, 1)
    across, beside = blocks_for((2, 1), ((0, 1), (0,)), relayed)
    across = lax.optimization_barrier(add(across, arrived).astype(jnp.bfloat16))
    far = swap(across, "gx", n_gx, 2)
    near = [swap(beside, "gx", n_gx, 1)]
    (beside,) = blocks_for((1,), ((1,),), across)
    near.append(swap(beside, "gx", n_gx, 1))
    (own,) = blocks_for((0,), ((0, 1),), beside)
    hidden = activate_packed(own, far, near, rows, width)

    neighbour = swap(hidden, "gx", n_gx, 1)
    opposite = swap(hidden, "gx", n_gx, 2)
    (total,) = down([hidden, neighbour], (0, 1), None, down_weight, rows, width, 1)
    opposite, total = lax.optimization_barrier((opposite, total))
    diagonal = swap(opposite, "gx", n_gx, 1)
    (total,) = down([opposite], (2,), total, down_weight, rows, width, 1)
    outs = down([diagonal], (3,), total, down_weight, rows, width, n_token)
    terms = [outs[0]] + [swap(outs[r], TOKEN_AXES, n_token, r) for r in range(1, n_token)]
    return finish(terms, tokens.shape)


def offloaded(tokens, gate_weight, up_weight, down_weight):
    features = lax.all_gather(tokens, TOKEN_AXES, axis=0, tiled=True)
    hidden_width = gate_weight.shape[1]
    gate_part = jnp.dot(features, gate_weight, preferred_element_type=jnp.float32)
    up_part = jnp.dot(features, up_weight, preferred_element_type=jnp.float32)
    summed = lax.psum(
        jnp.concatenate([gate_part, up_part], axis=1).astype(jnp.bfloat16), "gx"
    ).astype(jnp.float32)
    hidden = activate(summed[:, :hidden_width], summed[:, hidden_width:])
    partial_value = jnp.dot(hidden, down_weight, preferred_element_type=jnp.float32)
    return lax.psum_scatter(
        partial_value.astype(jnp.bfloat16), TOKEN_AXES, scatter_dimension=0, tiled=True
    )


def shards(tokens, gate_weight, up_weight, down_weight):
    n_gx = lax.axis_size("gx")
    n_token = lax.axis_size(TOKEN_AXES)
    rows = tokens.shape[0] * n_token
    tokens_fit = n_token > 1 and n_token & (n_token - 1) == 0 and rows % 4 == 0
    weights_fit = gate_weight.shape[1] % (128 * 4) == 0 and gate_weight.shape[0] % STEP == 0
    columns_fit = down_weight.shape[1] % (128 * 8) == 0
    if n_gx == 4 and tokens_fit and weights_fit and columns_fit:
        return direct(tokens, gate_weight, up_weight, down_weight)
    return offloaded(tokens, gate_weight, up_weight, down_weight)


def solution(mesh):
    return jax.shard_map(
        shards,
        mesh=mesh,
        in_specs=(
            P(("grp", "gy", "gz"), "gx"),
            P("gx", ("gy", "gz")),
            P("gx", ("gy", "gz")),
            P(("gy", "gz"), "gx"),
        ),
        out_specs=P(("grp", "gy", "gz"), "gx"),
        check_vma=False,
    )
```

```python
import functools

import jax
import jax.numpy as jnp
from jax import lax
from jax.experimental import pallas as pl
from jax.experimental.pallas import tpu as pltpu
from jax.sharding import PartitionSpec as P

MIB = 1 << 20
STEP = 256
COPY_STEP = 512
IN_FLIGHT = 6
DOWN_STEP = 512
TOKEN_AXES = ("gy", "gz")
IN_HBM = pl.BlockSpec(memory_space=pltpu.HBM)
ANY = pl.BlockSpec(memory_space=pl.ANY)
WHOLE = pl.BlockSpec(memory_space=pltpu.VMEM)


def activate(gate, up):
    return (jax.nn.silu(gate) * up).astype(jnp.bfloat16)


def pieces_of(total, step):
    return [(start, min(step, total - start)) for start in range(0, total, step)]


def in_hbm(value):
    return pltpu.with_memory_space_constraint(value, pltpu.HBM)


def in_vmem(value):
    return pltpu.with_memory_space_constraint(value, pltpu.VMEM)


SMALL = pl.CostEstimate(flops=0, bytes_accessed=MIB, transcendentals=0)


def block_start(distance, width):
    return pl.multiple_of((lax.axis_index("gx") ^ distance) * width, 128)


def params(mib):
    return pltpu.CompilerParams(vmem_limit_bytes=mib * MIB)


def packed_pair_width(rows, width):
    return (rows // 8) * 2 * width + (width if rows % 8 else 0)


def pack_pair(out, gate, up):
    rows, width = gate.shape
    for g in range(rows // 8):
        for w, value in enumerate((gate, up)):
            at = (2 * g + w) * width
            out[:, at : at + width] = value[8 * g : 8 * g + 8].astype(out.dtype)
    if rows % 8:
        at = (rows // 8) * 2 * width
        tail = jnp.concatenate([gate[rows - 4 :], up[rows - 4 :]], axis=0)
        out[:, at : at + width] = tail.astype(out.dtype)


def block_copies(width, distance, weights, first, held, sems):
    columns = pl.ds(block_start(distance, width), width)
    copies = []
    for k, (row, rows) in enumerate(pieces_of(held.shape[1], COPY_STEP)):
        for w, weight in enumerate(weights):
            copy = pltpu.make_async_copy(
                weight.at[pl.ds(first + row, rows), columns],
                held.at[w, pl.ds(row, rows)],
                sems.at[w, k],
            )
            copies.append((w, row, rows, copy))
    return copies


def copy_sems(weights, depth):
    return pltpu.SemaphoreType.DMA((weights, len(pieces_of(depth, COPY_STEP))))


def fetch_kernel(width, distance, gate_ref, up_ref, held, sems):
    copies = block_copies(width, distance, (gate_ref, up_ref), 0, held, sems)
    for _, _, _, copy in copies:
        copy.start()
    for _, _, _, copy in copies:
        copy.wait()


def fetch(gate_weight, up_weight, distance, width):
    depth = gate_weight.shape[0]
    return pl.pallas_call(
        functools.partial(fetch_kernel, width, distance),
        out_shape=pltpu.VMEM((2, depth, width), jnp.bfloat16),
        in_specs=[IN_HBM, IN_HBM],
        out_specs=WHOLE,
        scratch_shapes=[copy_sems(2, depth)],
        compiler_params=params(4),
        cost_estimate=SMALL,
    )(in_hbm(gate_weight), in_hbm(up_weight))


def multiply(x_ref, first, held, total, steps, waiting=()):
    for w, top, tall, copy in steps:
        if copy is not None:
            copy.wait()
        if waiting:
            waiting.pop(0).start()
        for row, rows in pieces_of(tall, STEP):
            at = first + top + row
            term = jnp.dot(
                x_ref[:, at : at + rows],
                held[w, top + row : top + row + rows, :],
                preferred_element_type=jnp.float32,
            )
            if at == 0:
                total[w] = term
            else:
                total[w] += term


def held_steps(held):
    return [(w, row, rows, None) for row, rows in pieces_of(held.shape[1], STEP) for w in range(2)]


def held_kernel(width, distance, x_ref, held, gate_ref, up_ref, out, ahead, total, sems):
    copies = block_copies(width, distance, (gate_ref, up_ref), 0, ahead, sems)
    for _, _, _, copy in copies:
        copy.start()
    multiply(x_ref, 0, held, total, held_steps(held))
    pack_pair(out, total[0], total[1])
    for _, _, _, copy in copies:
        copy.wait()


def gate_up_held(features, held, gate_weight, up_weight, distance, ahead):
    rows, width = features.shape[0], held.shape[2]
    return pl.pallas_call(
        functools.partial(held_kernel, width, distance),
        out_shape=(
            jax.ShapeDtypeStruct((8, packed_pair_width(rows, width)), jnp.bfloat16),
            jax.ShapeDtypeStruct((2, ahead, width), jnp.bfloat16),
        ),
        in_specs=[WHOLE, WHOLE, IN_HBM, IN_HBM],
        out_specs=(WHOLE, WHOLE),
        scratch_shapes=[pltpu.VMEM((2, rows, width), jnp.float32), copy_sems(2, ahead)],
        compiler_params=params(8),
        cost_estimate=SMALL,
    )(features, in_vmem(held), in_hbm(gate_weight), in_hbm(up_weight))


def stream_kernel(width, blocks, distances, has_held, x_ref, *refs):
    refs = list(refs)
    held_top = refs.pop(0) if has_held else None
    gate_ref, up_ref, _ = refs[:3]
    outs, refs = refs[3 : 3 + len(blocks)], refs[3 + len(blocks) :]
    work = []
    for b, which in enumerate(blocks):
        held, total, sems = refs[3 * b : 3 * b + 3]
        weights = [(gate_ref, up_ref)[w] for w in which]
        first = x_ref.shape[1] - held.shape[1]
        copies = block_copies(width, distances[b], weights, first, held, sems)
        work.append((outs[b], first, held, total, copies))
    waiting = [step[-1] for block in work for step in block[-1]]
    in_flight = IN_FLIGHT if len(blocks) > 1 else len(waiting)
    for copy in waiting[:in_flight]:
        copy.start()
    waiting = waiting[in_flight:]
    if has_held:
        multiply(x_ref, 0, held_top, work[0][3], held_steps(held_top))
    for (out, first, held, total, copies), which in zip(work, blocks):
        multiply(x_ref, first, held, total, copies, waiting)
        if len(which) == 2:
            pack_pair(out, total[0], total[1])
        else:
            pack_single(out, total[0])


def gate_up_stream(features, gate_weight, up_weight, distances, blocks, width, after, held=None):
    rows, depth = features.shape
    scratch, shapes, held_bytes = [], [], 0
    for b, which in enumerate(blocks):
        packed = packed_pair_width(rows, width) if len(which) == 2 else packed_width(rows, width)
        shapes.append(jax.ShapeDtypeStruct((8, packed), jnp.bfloat16))
        below = depth - (held.shape[1] if held is not None and b == 0 else 0)
        held_bytes += len(which) * below * width * 2
        scratch += [
            pltpu.VMEM((len(which), below, width), jnp.bfloat16),
            pltpu.VMEM((len(which), rows, width), jnp.float32),
            copy_sems(len(which), below),
        ]
    before = [] if held is None else [held]
    return pl.pallas_call(
        functools.partial(stream_kernel, width, blocks, distances, held is not None),
        out_shape=shapes,
        in_specs=[WHOLE] * (1 + len(before)) + [IN_HBM, IN_HBM, ANY],
        out_specs=[WHOLE] * len(blocks),
        scratch_shapes=scratch,
        compiler_params=params(8 + -(-held_bytes // MIB)),
        cost_estimate=SMALL,
    )(features, *before, in_hbm(gate_weight), in_hbm(up_weight), after)


def hidden_tail(rows, width):
    half = pl.cdiv(width // 2, 128) * 128
    return half if rows % 8 else 0


def packed_width(rows, width):
    return (rows // 8) * width + hidden_tail(rows, width)


def pack_single(out, value):
    rows, width = value.shape
    for g in range(rows // 8):
        out[:, g * width : (g + 1) * width] = value[8 * g : 8 * g + 8].astype(out.dtype)
    if rows % 8:
        at, half = (rows // 8) * width, hidden_tail(rows, width)
        left, right = value[rows - 4 :, :half], value[rows - 4 :, half:]
        if 2 * half > width:
            right = jnp.concatenate([right, jnp.zeros((4, 2 * half - width), jnp.float32)], axis=1)
        out[:, at : at + half] = jnp.concatenate([left, right], axis=0).astype(out.dtype)


def last_rows(packed, rows, width):
    at, half = (rows // 8) * width, hidden_tail(rows, width)
    tail = packed[:, at : at + half].astype(jnp.float32)
    return jnp.concatenate([tail[:4], tail[4:, : width - half]], axis=1)


def activate_kernel(rows, width, own, far, gate_near, up_near, out):
    def pair(at):
        columns = slice(at, at + width)
        return own[:, columns].astype(jnp.float32) + far[:, columns].astype(jnp.float32)

    for g in range(rows // 8):
        near = slice(g * width, (g + 1) * width)
        out[:, near] = activate(
            pair(2 * g * width) + gate_near[:, near].astype(jnp.float32),
            pair((2 * g + 1) * width) + up_near[:, near].astype(jnp.float32),
        )
    if rows % 8:
        half = hidden_tail(rows, width)
        last = pair((rows // 8) * 2 * width)
        value = activate(
            last[:4] + last_rows(gate_near, rows, width),
            last[4:] + last_rows(up_near, rows, width),
        ).astype(jnp.float32)
        right = jnp.concatenate([value[:, half:], jnp.zeros((4, 2 * half - width), jnp.float32)], axis=1)
        at = (rows // 8) * width
        out[:, at : at + half] = jnp.concatenate([value[:, :half], right], axis=0).astype(out.dtype)


def activate_packed(own, far, near, rows, width):
    return pl.pallas_call(
        functools.partial(activate_kernel, rows, width),
        out_shape=jax.ShapeDtypeStruct((8, packed_width(rows, width)), jnp.bfloat16),
        in_specs=[WHOLE] * 4,
        out_specs=WHOLE,
        compiler_params=params(8),
        cost_estimate=SMALL,
    )(own, far, *near)


def pack_rows(out, value):
    rows, width = value.shape
    for g in range(rows // 8):
        out[:, g * width : (g + 1) * width] = value[8 * g : 8 * g + 8].astype(out.dtype)
    piece = width // 8
    for r in range(rows // 8 * 8, rows):
        at = (rows // 8) * width + (r % 8) * piece
        row = jnp.concatenate(
            [value[r : r + 1, i * piece : (i + 1) * piece] for i in range(8)], axis=0
        )
        out[:, at : at + piece] = row.astype(out.dtype)


def unpack_rows(out, packed):
    rows, width = out.shape
    for g in range(rows // 8):
        out[8 * g : 8 * g + 8, :] = packed[:, g * width : (g + 1) * width]
    piece = width // 8
    for r in range(rows // 8 * 8, rows):
        at = (rows // 8) * width + (r % 8) * piece
        for i in range(8):
            out[r : r + 1, i * piece : (i + 1) * piece] = packed[i : i + 1, at : at + piece]


def down_kernel(first, rows, width, distances, *refs):
    blocks = len(distances)
    hidden, refs = refs[:blocks], refs[blocks:]
    if not first:
        before, refs = refs[0], refs[1:]
    held, outs, (plain, total) = refs[0], refs[1:-2], refs[-2:]
    if first:
        total = outs[0]
    for b in range(blocks):
        for g in range(rows // 8):
            plain[8 * g : 8 * g + 8, :] = hidden[b][:, g * width : (g + 1) * width].astype(jnp.float32)
        if rows % 8:
            at, half = (rows // 8) * width, hidden_tail(rows, width)
            tail = hidden[b][:, at : at + half].astype(jnp.float32)
            plain[rows - 4 :, :half] = tail[:4]
            plain[rows - 4 :, half:] = tail[4:, : width - half]
        for row, tall in pieces_of(width, DOWN_STEP):
            term = jnp.dot(
                plain[:, row : row + tall].astype(jnp.bfloat16),
                held[pl.ds(pl.multiple_of(block_start(distances[b], width) + row, 128), tall), :],
                preferred_element_type=jnp.float32,
            )
            if b == 0 and row == 0:
                total[...] = term if first else before[...] + term
            else:
                total[...] += term
    if not first:
        tall = rows // len(outs)
        for r, out in enumerate(outs):
            pack_rows(out, total[r * tall : (r + 1) * tall, :])


def down(hidden, distances, before, weight, rows, width, outs):
    columns = weight.shape[1]
    if before is None:
        shapes = [jax.ShapeDtypeStruct((rows, columns), jnp.float32)]
    else:
        packed = (8, rows // outs * columns // 8)
        shapes = [jax.ShapeDtypeStruct(packed, jnp.bfloat16 if r else jnp.float32) for r in range(outs)]
    carried = [] if before is None else [before]
    return pl.pallas_call(
        functools.partial(down_kernel, before is None, rows, width, distances),
        out_shape=shapes,
        in_specs=[WHOLE] * (len(hidden) + len(carried) + 1),
        out_specs=[WHOLE] * len(shapes),
        scratch_shapes=[
            pltpu.VMEM((rows, width), jnp.float32),
            pltpu.VMEM((rows, columns), jnp.float32),
        ],
        compiler_params=params(8),
        cost_estimate=SMALL,
    )(*hidden, *carried, in_vmem(weight))


def finish_kernel(*refs):
    terms, out, plain = refs[:-2], refs[-2], refs[-1]
    packed = terms[0][...]
    for term in terms[1:]:
        packed = packed + term[...].astype(jnp.float32)
    unpack_rows(plain, packed)
    out[...] = plain[...].astype(out.dtype)


def finish(terms, shape):
    return pl.pallas_call(
        finish_kernel,
        out_shape=jax.ShapeDtypeStruct(shape, jnp.bfloat16),
        in_specs=[WHOLE] * len(terms),
        out_specs=WHOLE,
        scratch_shapes=[pltpu.VMEM(shape, jnp.float32)],
        compiler_params=params(4),
        cost_estimate=SMALL,
    )(*terms)


def swap(value, axes, size, distance):
    return lax.ppermute(value, axes, [(i, i ^ distance) for i in range(size)])


def add(a, b):
    return a.astype(jnp.float32) + b.astype(jnp.float32)


def direct(tokens, gate_weight, up_weight, down_weight):
    n_gx = lax.axis_size("gx")
    n_token = lax.axis_size(TOKEN_AXES)
    width = gate_weight.shape[1] // n_gx

    held = fetch(gate_weight, up_weight, 3, width)
    features = jnp.concatenate(
        [tokens] + [swap(tokens, TOKEN_AXES, n_token, r) for r in range(1, n_token)], axis=0
    )
    rows = features.shape[0]

    def blocks_for(distances, blocks, after, held=None):
        return gate_up_stream(
            features, gate_weight, up_weight, distances, blocks, width, after, held
        )

    ahead = gate_weight.shape[0] // 4 // STEP * STEP
    relayed, held = gate_up_held(features, held, gate_weight, up_weight, 2, ahead)
    arrived = swap(relayed, "gx", n_gx, 1)
    across, beside = blocks_for((2, 1), ((0, 1), (0,)), relayed, held)
    across = lax.optimization_barrier(add(across, arrived).astype(jnp.bfloat16))
    far = swap(across, "gx", n_gx, 2)
    near = [swap(beside, "gx", n_gx, 1)]
    (beside,) = blocks_for((1,), ((1,),), across)
    near.append(swap(beside, "gx", n_gx, 1))
    (own,) = blocks_for((0,), ((0, 1),), beside)
    hidden = activate_packed(own, far, near, rows, width)

    opposite = swap(hidden, "gx", n_gx, 2)
    first = [hidden, swap(hidden, "gx", n_gx, 1), opposite]
    second = [swap(opposite, "gx", n_gx, 1)]
    (partial_sum,) = down(first, (0, 1, 2), None, down_weight, rows, width, 1)
    outs = down(second, (3,), partial_sum, down_weight, rows, width, n_token)
    terms = [outs[0]] + [swap(outs[r], TOKEN_AXES, n_token, r) for r in range(1, n_token)]
    return finish(terms, tokens.shape)


def offloaded(tokens, gate_weight, up_weight, down_weight):
    features = lax.all_gather(tokens, TOKEN_AXES, axis=0, tiled=True)
    hidden_width = gate_weight.shape[1]
    gate_part = jnp.dot(features, gate_weight, preferred_element_type=jnp.float32)
    up_part = jnp.dot(features, up_weight, preferred_element_type=jnp.float32)
    summed = lax.psum(
        jnp.concatenate([gate_part, up_part], axis=1).astype(jnp.bfloat16), "gx"
    ).astype(jnp.float32)
    hidden = activate(summed[:, :hidden_width], summed[:, hidden_width:])
    partial_value = jnp.dot(hidden, down_weight, preferred_element_type=jnp.float32)
    return lax.psum_scatter(
        partial_value.astype(jnp.bfloat16), TOKEN_AXES, scatter_dimension=0, tiled=True
    )


def shards(tokens, gate_weight, up_weight, down_weight):
    n_gx = lax.axis_size("gx")
    n_token = lax.axis_size(TOKEN_AXES)
    rows = tokens.shape[0] * n_token
    tokens_fit = n_token > 1 and n_token & (n_token - 1) == 0 and rows % 4 == 0
    weights_fit = gate_weight.shape[1] % (128 * 4) == 0 and gate_weight.shape[0] % (4 * STEP) == 0
    columns_fit = down_weight.shape[1] % (128 * 8) == 0
    if n_gx == 4 and tokens_fit and weights_fit and columns_fit:
        return direct(tokens, gate_weight, up_weight, down_weight)
    return offloaded(tokens, gate_weight, up_weight, down_weight)


def solution(mesh):
    return jax.shard_map(
        shards,
        mesh=mesh,
        in_specs=(
            P(("grp", "gy", "gz"), "gx"),
            P("gx", ("gy", "gz")),
            P("gx", ("gy", "gz")),
            P(("gy", "gz"), "gx"),
        ),
        out_specs=P(("grp", "gy", "gz"), "gx"),
        check_vma=False,
    )
```

```python
import functools

import jax
import jax.numpy as jnp
from jax import lax
from jax.experimental import pallas as pl
from jax.experimental.pallas import tpu as pltpu
from jax.sharding import PartitionSpec as P

MIB = 1 << 20
STEP = 256
COPY_STEP = 512
IN_FLIGHT = 6
DOWN_STEP = 512
TOKEN_AXES = ("gy", "gz")
IN_HBM = pl.BlockSpec(memory_space=pltpu.HBM)
ANY = pl.BlockSpec(memory_space=pl.ANY)
WHOLE = pl.BlockSpec(memory_space=pltpu.VMEM)


def activate(gate, up):
    return (jax.nn.silu(gate) * up).astype(jnp.bfloat16)


def pieces_of(total, step):
    return [(start, min(step, total - start)) for start in range(0, total, step)]


def in_hbm(value):
    return pltpu.with_memory_space_constraint(value, pltpu.HBM)


def in_vmem(value):
    return pltpu.with_memory_space_constraint(value, pltpu.VMEM)


SMALL = pl.CostEstimate(flops=0, bytes_accessed=MIB, transcendentals=0)


def block_start(distance, width):
    return pl.multiple_of((lax.axis_index("gx") ^ distance) * width, 128)


def params(mib):
    return pltpu.CompilerParams(vmem_limit_bytes=mib * MIB)


def packed_pair_width(rows, width):
    return (rows // 8) * 2 * width + (width if rows % 8 else 0)


def pack_pair(out, gate, up):
    rows, width = gate.shape
    for g in range(rows // 8):
        for w, value in enumerate((gate, up)):
            at = (2 * g + w) * width
            out[:, at : at + width] = value[8 * g : 8 * g + 8].astype(out.dtype)
    if rows % 8:
        at = (rows // 8) * 2 * width
        tail = jnp.concatenate([gate[rows - 4 :], up[rows - 4 :]], axis=0)
        out[:, at : at + width] = tail.astype(out.dtype)


def block_copies(width, distance, weights, held, sems):
    columns = pl.ds(block_start(distance, width), width)
    copies = []
    for k, (row, rows) in enumerate(pieces_of(held.shape[1], COPY_STEP)):
        for w, weight in enumerate(weights):
            copy = pltpu.make_async_copy(
                weight.at[pl.ds(row, rows), columns], held.at[w, pl.ds(row, rows)], sems.at[w, k]
            )
            copies.append((w, row, rows, copy))
    return copies


def fetch_kernel(width, distance, gate_ref, up_ref, held, sems):
    copies = block_copies(width, distance, (gate_ref, up_ref), held, sems)
    for _, _, _, copy in copies:
        copy.start()
    for _, _, _, copy in copies:
        copy.wait()


def fetch(gate_weight, up_weight, distance, width):
    depth = gate_weight.shape[0]
    return pl.pallas_call(
        functools.partial(fetch_kernel, width, distance),
        out_shape=pltpu.VMEM((2, depth, width), jnp.bfloat16),
        in_specs=[IN_HBM, IN_HBM],
        out_specs=WHOLE,
        scratch_shapes=[pltpu.SemaphoreType.DMA((2, len(pieces_of(depth, COPY_STEP))))],
        compiler_params=params(4),
        cost_estimate=SMALL,
    )(in_hbm(gate_weight), in_hbm(up_weight))


def multiply(x_ref, held, total, steps, waiting=()):
    for w, first, tall, copy in steps:
        if copy is not None:
            copy.wait()
        if waiting:
            waiting.pop(0).start()
        for row, rows in pieces_of(tall, STEP):
            rows = slice(first + row, first + row + rows)
            term = jnp.dot(x_ref[:, rows], held[w, rows, :], preferred_element_type=jnp.float32)
            if rows.start == 0:
                total[w] = term
            else:
                total[w] += term


def held_kernel(x_ref, held, out, total):
    parts = pieces_of(x_ref.shape[1], STEP)
    multiply(x_ref, held, total, [(w, row, rows, None) for w in range(2) for row, rows in parts])
    pack_pair(out, total[0], total[1])


def gate_up_held(features, held):
    rows, width = features.shape[0], held.shape[2]
    return pl.pallas_call(
        held_kernel,
        out_shape=jax.ShapeDtypeStruct((8, packed_pair_width(rows, width)), jnp.bfloat16),
        in_specs=[WHOLE, WHOLE],
        out_specs=WHOLE,
        scratch_shapes=[pltpu.VMEM((2, rows, width), jnp.float32)],
        compiler_params=params(8),
        cost_estimate=SMALL,
    )(features, in_vmem(held))


def stream_kernel(width, blocks, distances, x_ref, gate_ref, up_ref, _, *refs):
    outs, refs = refs[: len(blocks)], refs[len(blocks) :]
    work = []
    for b, which in enumerate(blocks):
        held, total, sems = refs[3 * b : 3 * b + 3]
        weights = [(gate_ref, up_ref)[w] for w in which]
        copies = block_copies(width, distances[b], weights, held, sems)
        work.append((outs[b], held, total, copies))
    waiting = [step[-1] for block in work for step in block[-1]]
    in_flight = IN_FLIGHT if len(blocks) > 1 else len(waiting)
    for copy in waiting[:in_flight]:
        copy.start()
    waiting = waiting[in_flight:]
    for (out, held, total, copies), which in zip(work, blocks):
        multiply(x_ref, held, total, copies, waiting)
        if len(which) == 2:
            pack_pair(out, total[0], total[1])
        else:
            pack_single(out, total[0])


def gate_up_stream(features, gate_weight, up_weight, distances, blocks, width, after):
    rows, depth = features.shape
    scratch, shapes = [], []
    for which in blocks:
        packed = packed_pair_width(rows, width) if len(which) == 2 else packed_width(rows, width)
        shapes.append(jax.ShapeDtypeStruct((8, packed), jnp.bfloat16))
        scratch += [
            pltpu.VMEM((len(which), depth, width), jnp.bfloat16),
            pltpu.VMEM((len(which), rows, width), jnp.float32),
            pltpu.SemaphoreType.DMA((len(which), len(pieces_of(depth, COPY_STEP)))),
        ]
    held_mib = -(-depth * width * 2 * sum(len(which) for which in blocks) // MIB)
    return pl.pallas_call(
        functools.partial(stream_kernel, width, blocks, distances),
        out_shape=shapes,
        in_specs=[WHOLE, IN_HBM, IN_HBM, ANY],
        out_specs=[WHOLE] * len(blocks),
        scratch_shapes=scratch,
        compiler_params=params(5 + held_mib),
        cost_estimate=SMALL,
    )(features, in_hbm(gate_weight), in_hbm(up_weight), after)


def hidden_tail(rows, width):
    half = pl.cdiv(width // 2, 128) * 128
    return half if rows % 8 else 0


def packed_width(rows, width):
    return (rows // 8) * width + hidden_tail(rows, width)


def pack_single(out, value):
    rows, width = value.shape
    for g in range(rows // 8):
        out[:, g * width : (g + 1) * width] = value[8 * g : 8 * g + 8].astype(out.dtype)
    if rows % 8:
        at, half = (rows // 8) * width, hidden_tail(rows, width)
        left, right = value[rows - 4 :, :half], value[rows - 4 :, half:]
        if 2 * half > width:
            right = jnp.concatenate([right, jnp.zeros((4, 2 * half - width), jnp.float32)], axis=1)
        out[:, at : at + half] = jnp.concatenate([left, right], axis=0).astype(out.dtype)


def last_rows(packed, rows, width):
    at, half = (rows // 8) * width, hidden_tail(rows, width)
    tail = packed[:, at : at + half].astype(jnp.float32)
    return jnp.concatenate([tail[:4], tail[4:, : width - half]], axis=1)


def activate_kernel(rows, width, own, far, gate_near, up_near, out):
    def pair(at):
        columns = slice(at, at + width)
        return own[:, columns].astype(jnp.float32) + far[:, columns].astype(jnp.float32)

    for g in range(rows // 8):
        near = slice(g * width, (g + 1) * width)
        out[:, near] = activate(
            pair(2 * g * width) + gate_near[:, near].astype(jnp.float32),
            pair((2 * g + 1) * width) + up_near[:, near].astype(jnp.float32),
        )
    if rows % 8:
        half = hidden_tail(rows, width)
        last = pair((rows // 8) * 2 * width)
        value = activate(
            last[:4] + last_rows(gate_near, rows, width),
            last[4:] + last_rows(up_near, rows, width),
        ).astype(jnp.float32)
        right = jnp.concatenate([value[:, half:], jnp.zeros((4, 2 * half - width), jnp.float32)], axis=1)
        at = (rows // 8) * width
        out[:, at : at + half] = jnp.concatenate([value[:, :half], right], axis=0).astype(out.dtype)


def activate_packed(own, far, near, rows, width):
    return pl.pallas_call(
        functools.partial(activate_kernel, rows, width),
        out_shape=jax.ShapeDtypeStruct((8, packed_width(rows, width)), jnp.bfloat16),
        in_specs=[WHOLE] * 4,
        out_specs=WHOLE,
        compiler_params=params(8),
        cost_estimate=SMALL,
    )(own, far, *near)


def pack_rows(out, value):
    rows, width = value.shape
    for g in range(rows // 8):
        out[:, g * width : (g + 1) * width] = value[8 * g : 8 * g + 8].astype(out.dtype)
    piece = width // 8
    for r in range(rows // 8 * 8, rows):
        at = (rows // 8) * width + (r % 8) * piece
        row = jnp.concatenate(
            [value[r : r + 1, i * piece : (i + 1) * piece] for i in range(8)], axis=0
        )
        out[:, at : at + piece] = row.astype(out.dtype)


def unpack_rows(out, packed):
    rows, width = out.shape
    for g in range(rows // 8):
        out[8 * g : 8 * g + 8, :] = packed[:, g * width : (g + 1) * width]
    piece = width // 8
    for r in range(rows // 8 * 8, rows):
        at = (rows // 8) * width + (r % 8) * piece
        for i in range(8):
            out[r : r + 1, i * piece : (i + 1) * piece] = packed[i : i + 1, at : at + piece]


def down_kernel(first, rows, width, distances, counts, *refs):
    refs = list(refs)
    hidden = [[refs.pop(0) for _ in range(count)] for count in counts]
    before = None if first else refs.pop(0)
    held, outs, (plain, total) = refs[0], refs[1:-2], refs[-2:]
    if first:
        total = outs[0]
    for b, parts in enumerate(hidden):
        packed = parts[0][...].astype(jnp.float32)
        for part in parts[1:]:
            packed = packed + part[...].astype(jnp.float32)
        for g in range(rows // 8):
            plain[8 * g : 8 * g + 8, :] = packed[:, g * width : (g + 1) * width]
        if rows % 8:
            at, half = (rows // 8) * width, hidden_tail(rows, width)
            plain[rows - 4 :, :half] = packed[:4, at : at + half]
            plain[rows - 4 :, half:] = packed[4:, at : at + width - half]
        for row, tall in pieces_of(width, DOWN_STEP):
            term = jnp.dot(
                plain[:, row : row + tall].astype(jnp.bfloat16),
                held[pl.ds(pl.multiple_of(block_start(distances[b], width) + row, 128), tall), :],
                preferred_element_type=jnp.float32,
            )
            if b == 0 and row == 0:
                total[...] = term if first else before[...] + term
            else:
                total[...] += term
    if not first:
        tall = rows // len(outs)
        for r, out in enumerate(outs):
            pack_rows(out, total[r * tall : (r + 1) * tall, :])


def down(hidden, distances, before, weight, rows, width, outs):
    columns = weight.shape[1]
    if before is None:
        shapes = [jax.ShapeDtypeStruct((rows, columns), jnp.float32)]
    else:
        packed = (8, rows // outs * columns // 8)
        shapes = [jax.ShapeDtypeStruct(packed, jnp.bfloat16 if r else jnp.float32) for r in range(outs)]
    carried = [] if before is None else [before]
    counts = [len(parts) for parts in hidden]
    arrays = [part for parts in hidden for part in parts]
    return pl.pallas_call(
        functools.partial(down_kernel, before is None, rows, width, distances, counts),
        out_shape=shapes,
        in_specs=[WHOLE] * (len(arrays) + len(carried) + 1),
        out_specs=[WHOLE] * len(shapes),
        scratch_shapes=[
            pltpu.VMEM((rows, width), jnp.float32),
            pltpu.VMEM((rows, columns), jnp.float32),
        ],
        compiler_params=params(8),
        cost_estimate=SMALL,
    )(*arrays, *carried, in_vmem(weight))


def finish_kernel(*refs):
    terms, out, plain = refs[:-2], refs[-2], refs[-1]
    packed = terms[0][...]
    for term in terms[1:]:
        packed = packed + term[...].astype(jnp.float32)
    unpack_rows(plain, packed)
    out[...] = plain[...].astype(out.dtype)


def finish(terms, shape):
    return pl.pallas_call(
        finish_kernel,
        out_shape=jax.ShapeDtypeStruct(shape, jnp.bfloat16),
        in_specs=[WHOLE] * len(terms),
        out_specs=WHOLE,
        scratch_shapes=[pltpu.VMEM(shape, jnp.float32)],
        compiler_params=params(4),
        cost_estimate=SMALL,
    )(*terms)


def send(value, axes, pairs):
    return lax.ppermute(value, axes, pairs)


def swap(value, axes, size, distance):
    return lax.ppermute(value, axes, [(i, i ^ distance) for i in range(size)])


def add(a, b):
    return a.astype(jnp.float32) + b.astype(jnp.float32)


def direct(tokens, gate_weight, up_weight, down_weight):
    n_gx = lax.axis_size("gx")
    n_token = lax.axis_size(TOKEN_AXES)
    width = gate_weight.shape[1] // n_gx

    held = fetch(gate_weight, up_weight, 3, width)
    features = jnp.concatenate(
        [tokens] + [swap(tokens, TOKEN_AXES, n_token, r) for r in range(1, n_token)], axis=0
    )
    rows = features.shape[0]

    def blocks_for(distances, blocks, after):
        return gate_up_stream(features, gate_weight, up_weight, distances, blocks, width, after)

    relayed = gate_up_held(features, held)
    arrived = swap(relayed, "gx", n_gx, 1)
    across, beside = blocks_for((2, 1), ((0, 1), (0,)), relayed)
    across = lax.optimization_barrier(add(across, arrived).astype(jnp.bfloat16))
    far = swap(across, "gx", n_gx, 2)
    near = [swap(beside, "gx", n_gx, 1)]
    (beside,) = blocks_for((1,), ((1,),), across)
    near.append(swap(beside, "gx", n_gx, 1))
    (own,) = blocks_for((0,), ((0, 1),), beside)
    hidden = activate_packed(own, far, near, rows, width)

    inner, outer = (1, 2), (0, 3)
    outward = send(hidden, "gx", [(i, i ^ 2) for i in inner])
    inward = send(hidden, "gx", [(i, i ^ 2) for i in outer])
    first = [(hidden,), (swap(hidden, "gx", n_gx, 1),), (outward, inward)]
    second = [
        (
            send(outward, "gx", [(i, i ^ 1) for i in outer]),
            send(inward, "gx", [(i, i ^ 1) for i in inner]),
        )
    ]
    (partial_sum,) = down(first, (0, 1, 2), None, down_weight, rows, width, 1)
    outs = down(second, (3,), partial_sum, down_weight, rows, width, n_token)
    terms = [outs[0]] + [swap(outs[r], TOKEN_AXES, n_token, r) for r in range(1, n_token)]
    return finish(terms, tokens.shape)


def offloaded(tokens, gate_weight, up_weight, down_weight):
    features = lax.all_gather(tokens, TOKEN_AXES, axis=0, tiled=True)
    hidden_width = gate_weight.shape[1]
    gate_part = jnp.dot(features, gate_weight, preferred_element_type=jnp.float32)
    up_part = jnp.dot(features, up_weight, preferred_element_type=jnp.float32)
    summed = lax.psum(
        jnp.concatenate([gate_part, up_part], axis=1).astype(jnp.bfloat16), "gx"
    ).astype(jnp.float32)
    hidden = activate(summed[:, :hidden_width], summed[:, hidden_width:])
    partial_value = jnp.dot(hidden, down_weight, preferred_element_type=jnp.float32)
    return lax.psum_scatter(
        partial_value.astype(jnp.bfloat16), TOKEN_AXES, scatter_dimension=0, tiled=True
    )


def shards(tokens, gate_weight, up_weight, down_weight):
    n_gx = lax.axis_size("gx")
    n_token = lax.axis_size(TOKEN_AXES)
    rows = tokens.shape[0] * n_token
    tokens_fit = n_token > 1 and n_token & (n_token - 1) == 0 and rows % 4 == 0
    weights_fit = gate_weight.shape[1] % (128 * 4) == 0 and gate_weight.shape[0] % STEP == 0
    columns_fit = down_weight.shape[1] % (128 * 8) == 0
    if n_gx == 4 and tokens_fit and weights_fit and columns_fit:
        return direct(tokens, gate_weight, up_weight, down_weight)
    return offloaded(tokens, gate_weight, up_weight, down_weight)


def solution(mesh):
    return jax.shard_map(
        shards,
        mesh=mesh,
        in_specs=(
            P(("grp", "gy", "gz"), "gx"),
            P("gx", ("gy", "gz")),
            P("gx", ("gy", "gz")),
            P(("gy", "gz"), "gx"),
        ),
        out_specs=P(("grp", "gy", "gz"), "gx"),
        check_vma=False,
    )
```

```python
import functools

import jax
import jax.numpy as jnp
from jax import lax
from jax.experimental import pallas as pl
from jax.experimental.pallas import tpu as pltpu
from jax.sharding import PartitionSpec as P

MIB = 1 << 20
STEP = 256
COPY_STEP = 512
IN_FLIGHT = 6
DOWN_STEP = 512
TOKEN_AXES = ("gy", "gz")
IN_HBM = pl.BlockSpec(memory_space=pltpu.HBM)
ANY = pl.BlockSpec(memory_space=pl.ANY)
WHOLE = pl.BlockSpec(memory_space=pltpu.VMEM)


def activate(gate, up):
    return (jax.nn.silu(gate) * up).astype(jnp.bfloat16)


def pieces_of(total, step):
    return [(start, min(step, total - start)) for start in range(0, total, step)]


def in_hbm(value):
    return pltpu.with_memory_space_constraint(value, pltpu.HBM)


def in_vmem(value):
    return pltpu.with_memory_space_constraint(value, pltpu.VMEM)


SMALL = pl.CostEstimate(flops=0, bytes_accessed=MIB, transcendentals=0)


def block_start(distance, width):
    return pl.multiple_of((lax.axis_index("gx") ^ distance) * width, 128)


def params(mib):
    return pltpu.CompilerParams(vmem_limit_bytes=mib * MIB)


def packed_pair_width(rows, width):
    return (rows // 8) * 2 * width + (width if rows % 8 else 0)


def pack_pair(out, gate, up):
    rows, width = gate.shape
    for g in range(rows // 8):
        for w, value in enumerate((gate, up)):
            at = (2 * g + w) * width
            out[:, at : at + width] = value[8 * g : 8 * g + 8].astype(out.dtype)
    if rows % 8:
        at = (rows // 8) * 2 * width
        tail = jnp.concatenate([gate[rows - 4 :], up[rows - 4 :]], axis=0)
        out[:, at : at + width] = tail.astype(out.dtype)


def block_copies(width, distance, weights, held, sems):
    columns = pl.ds(block_start(distance, width), width)
    copies = []
    for k, (row, rows) in enumerate(pieces_of(held.shape[1], COPY_STEP)):
        for w, weight in enumerate(weights):
            copy = pltpu.make_async_copy(
                weight.at[pl.ds(row, rows), columns], held.at[w, pl.ds(row, rows)], sems.at[w, k]
            )
            copies.append((w, row, rows, copy))
    return copies


def fetch_kernel(width, distance, gate_ref, up_ref, held, sems):
    copies = block_copies(width, distance, (gate_ref, up_ref), held, sems)
    for _, _, _, copy in copies:
        copy.start()
    for _, _, _, copy in copies:
        copy.wait()


def fetch(gate_weight, up_weight, distance, width):
    depth = gate_weight.shape[0]
    return pl.pallas_call(
        functools.partial(fetch_kernel, width, distance),
        out_shape=pltpu.VMEM((2, depth, width), jnp.bfloat16),
        in_specs=[IN_HBM, IN_HBM],
        out_specs=WHOLE,
        scratch_shapes=[pltpu.SemaphoreType.DMA((2, len(pieces_of(depth, COPY_STEP))))],
        compiler_params=params(4),
        cost_estimate=SMALL,
    )(in_hbm(gate_weight), in_hbm(up_weight))


def multiply(x_ref, held, total, steps, waiting=()):
    for w, first, tall, copy in steps:
        if copy is not None:
            copy.wait()
        if waiting:
            waiting.pop(0).start()
        for row, rows in pieces_of(tall, STEP):
            rows = slice(first + row, first + row + rows)
            term = jnp.dot(x_ref[:, rows], held[w, rows, :], preferred_element_type=jnp.float32)
            if rows.start == 0:
                total[w] = term
            else:
                total[w] += term


def held_kernel(x_ref, held, out, total):
    parts = pieces_of(x_ref.shape[1], STEP)
    multiply(x_ref, held, total, [(w, row, rows, None) for w in range(2) for row, rows in parts])
    pack_pair(out, total[0], total[1])


def gate_up_held(features, held):
    rows, width = features.shape[0], held.shape[2]
    return pl.pallas_call(
        held_kernel,
        out_shape=jax.ShapeDtypeStruct((8, packed_pair_width(rows, width)), jnp.bfloat16),
        in_specs=[WHOLE, WHOLE],
        out_specs=WHOLE,
        scratch_shapes=[pltpu.VMEM((2, rows, width), jnp.float32)],
        compiler_params=params(8),
        cost_estimate=SMALL,
    )(features, in_vmem(held))


def stream_kernel(width, blocks, distances, x_ref, gate_ref, up_ref, _, *refs):
    outs, refs = refs[: len(blocks)], refs[len(blocks) :]
    work = []
    for b, which in enumerate(blocks):
        held, total, sems = refs[3 * b : 3 * b + 3]
        weights = [(gate_ref, up_ref)[w] for w in which]
        copies = block_copies(width, distances[b], weights, held, sems)
        work.append((outs[b], held, total, copies))
    waiting = [step[-1] for block in work for step in block[-1]]
    in_flight = IN_FLIGHT if len(blocks) > 1 else len(waiting)
    for copy in waiting[:in_flight]:
        copy.start()
    waiting = waiting[in_flight:]
    for (out, held, total, copies), which in zip(work, blocks):
        multiply(x_ref, held, total, copies, waiting)
        if len(which) == 2:
            pack_pair(out, total[0], total[1])
        else:
            pack_single(out, total[0])


def gate_up_stream(features, gate_weight, up_weight, distances, blocks, width, after):
    rows, depth = features.shape
    scratch, shapes = [], []
    for which in blocks:
        packed = packed_pair_width(rows, width) if len(which) == 2 else packed_width(rows, width)
        shapes.append(jax.ShapeDtypeStruct((8, packed), jnp.bfloat16))
        scratch += [
            pltpu.VMEM((len(which), depth, width), jnp.bfloat16),
            pltpu.VMEM((len(which), rows, width), jnp.float32),
            pltpu.SemaphoreType.DMA((len(which), len(pieces_of(depth, COPY_STEP)))),
        ]
    held_mib = -(-depth * width * 2 * sum(len(which) for which in blocks) // MIB)
    return pl.pallas_call(
        functools.partial(stream_kernel, width, blocks, distances),
        out_shape=shapes,
        in_specs=[WHOLE, IN_HBM, IN_HBM, ANY],
        out_specs=[WHOLE] * len(blocks),
        scratch_shapes=scratch,
        compiler_params=params(5 + held_mib),
        cost_estimate=SMALL,
    )(features, in_hbm(gate_weight), in_hbm(up_weight), after)


def hidden_tail(rows, width):
    half = pl.cdiv(width // 2, 128) * 128
    return half if rows % 8 else 0


def packed_width(rows, width):
    return (rows // 8) * width + hidden_tail(rows, width)


def pack_single(out, value):
    rows, width = value.shape
    for g in range(rows // 8):
        out[:, g * width : (g + 1) * width] = value[8 * g : 8 * g + 8].astype(out.dtype)
    if rows % 8:
        at, half = (rows // 8) * width, hidden_tail(rows, width)
        left, right = value[rows - 4 :, :half], value[rows - 4 :, half:]
        if 2 * half > width:
            right = jnp.concatenate([right, jnp.zeros((4, 2 * half - width), jnp.float32)], axis=1)
        out[:, at : at + half] = jnp.concatenate([left, right], axis=0).astype(out.dtype)


def last_rows(packed, rows, width):
    at, half = (rows // 8) * width, hidden_tail(rows, width)
    tail = packed[:, at : at + half].astype(jnp.float32)
    return jnp.concatenate([tail[:4], tail[4:, : width - half]], axis=1)


def activate_kernel(rows, width, own, far, gate_near, up_near, out):
    def pair(at):
        columns = slice(at, at + width)
        return own[:, columns].astype(jnp.float32) + far[:, columns].astype(jnp.float32)

    for g in range(rows // 8):
        near = slice(g * width, (g + 1) * width)
        out[:, near] = activate(
            pair(2 * g * width) + gate_near[:, near].astype(jnp.float32),
            pair((2 * g + 1) * width) + up_near[:, near].astype(jnp.float32),
        )
    if rows % 8:
        half = hidden_tail(rows, width)
        last = pair((rows // 8) * 2 * width)
        value = activate(
            last[:4] + last_rows(gate_near, rows, width),
            last[4:] + last_rows(up_near, rows, width),
        ).astype(jnp.float32)
        right = jnp.concatenate([value[:, half:], jnp.zeros((4, 2 * half - width), jnp.float32)], axis=1)
        at = (rows // 8) * width
        out[:, at : at + half] = jnp.concatenate([value[:, :half], right], axis=0).astype(out.dtype)


def activate_packed(own, far, near, rows, width):
    return pl.pallas_call(
        functools.partial(activate_kernel, rows, width),
        out_shape=jax.ShapeDtypeStruct((8, packed_width(rows, width)), jnp.bfloat16),
        in_specs=[WHOLE] * 4,
        out_specs=WHOLE,
        compiler_params=params(8),
        cost_estimate=SMALL,
    )(own, far, *near)


def pack_rows(out, value):
    rows, width = value.shape
    for g in range(rows // 8):
        out[:, g * width : (g + 1) * width] = value[8 * g : 8 * g + 8].astype(out.dtype)
    piece = width // 8
    for r in range(rows // 8 * 8, rows):
        at = (rows // 8) * width + (r % 8) * piece
        row = jnp.concatenate(
            [value[r : r + 1, i * piece : (i + 1) * piece] for i in range(8)], axis=0
        )
        out[:, at : at + piece] = row.astype(out.dtype)


def unpack_rows(out, packed):
    rows, width = out.shape
    for g in range(rows // 8):
        out[8 * g : 8 * g + 8, :] = packed[:, g * width : (g + 1) * width]
    piece = width // 8
    for r in range(rows // 8 * 8, rows):
        at = (rows // 8) * width + (r % 8) * piece
        for i in range(8):
            out[r : r + 1, i * piece : (i + 1) * piece] = packed[i : i + 1, at : at + piece]


def down_kernel(first, rows, width, distances, *refs):
    blocks = len(distances)
    hidden, refs = refs[:blocks], refs[blocks:]
    if not first:
        before, refs = refs[0], refs[1:]
    held, outs, (plain, total) = refs[0], refs[1:-2], refs[-2:]
    if first:
        total = outs[0]
    for b in range(blocks):
        for g in range(rows // 8):
            plain[8 * g : 8 * g + 8, :] = hidden[b][:, g * width : (g + 1) * width].astype(jnp.float32)
        if rows % 8:
            at, half = (rows // 8) * width, hidden_tail(rows, width)
            tail = hidden[b][:, at : at + half].astype(jnp.float32)
            plain[rows - 4 :, :half] = tail[:4]
            plain[rows - 4 :, half:] = tail[4:, : width - half]
        for row, tall in pieces_of(width, DOWN_STEP):
            term = jnp.dot(
                plain[:, row : row + tall].astype(jnp.bfloat16),
                held[pl.ds(pl.multiple_of(block_start(distances[b], width) + row, 128), tall), :],
                preferred_element_type=jnp.float32,
            )
            if b == 0 and row == 0:
                total[...] = term if first else before[...] + term
            else:
                total[...] += term
    if not first:
        tall = rows // len(outs)
        for r, out in enumerate(outs):
            pack_rows(out, total[r * tall : (r + 1) * tall, :])


def down(hidden, distances, before, weight, rows, width, outs):
    columns = weight.shape[1]
    if before is None:
        shapes = [jax.ShapeDtypeStruct((rows, columns), jnp.float32)]
    else:
        packed = (8, rows // outs * columns // 8)
        shapes = [jax.ShapeDtypeStruct(packed, jnp.bfloat16 if r else jnp.float32) for r in range(outs)]
    carried = [] if before is None else [before]
    return pl.pallas_call(
        functools.partial(down_kernel, before is None, rows, width, distances),
        out_shape=shapes,
        in_specs=[WHOLE] * (len(hidden) + len(carried) + 1),
        out_specs=[WHOLE] * len(shapes),
        scratch_shapes=[
            pltpu.VMEM((rows, width), jnp.float32),
            pltpu.VMEM((rows, columns), jnp.float32),
        ],
        compiler_params=params(8),
        cost_estimate=SMALL,
    )(*hidden, *carried, in_vmem(weight))


def finish_kernel(*refs):
    terms, out, plain = refs[:-2], refs[-2], refs[-1]
    packed = terms[0][...]
    for term in terms[1:]:
        packed = packed + term[...].astype(jnp.float32)
    unpack_rows(plain, packed)
    out[...] = plain[...].astype(out.dtype)


def finish(terms, shape):
    return pl.pallas_call(
        finish_kernel,
        out_shape=jax.ShapeDtypeStruct(shape, jnp.bfloat16),
        in_specs=[WHOLE] * len(terms),
        out_specs=WHOLE,
        scratch_shapes=[pltpu.VMEM(shape, jnp.float32)],
        compiler_params=params(4),
        cost_estimate=SMALL,
    )(*terms)


def swap(value, axes, size, distance):
    return lax.ppermute(value, axes, [(i, i ^ distance) for i in range(size)])


def add(a, b):
    return a.astype(jnp.float32) + b.astype(jnp.float32)


def direct(tokens, gate_weight, up_weight, down_weight):
    n_gx = lax.axis_size("gx")
    n_token = lax.axis_size(TOKEN_AXES)
    width = gate_weight.shape[1] // n_gx

    held = fetch(gate_weight, up_weight, 2, width)
    features = jnp.concatenate(
        [tokens] + [swap(tokens, TOKEN_AXES, n_token, r) for r in range(1, n_token)], axis=0
    )
    rows = features.shape[0]

    def blocks_for(distances, blocks, after):
        return gate_up_stream(features, gate_weight, up_weight, distances, blocks, width, after)

    relayed = gate_up_held(features, held)
    arrived = swap(relayed, "gx", n_gx, 1)
    across, beside = blocks_for((3, 1), ((0, 1), (0,)), relayed)
    across = lax.optimization_barrier(add(across, arrived).astype(jnp.bfloat16))
    far = swap(across, "gx", n_gx, 3)
    near = [swap(beside, "gx", n_gx, 1)]
    (beside,) = blocks_for((1,), ((1,),), across)
    near.append(swap(beside, "gx", n_gx, 1))
    (own,) = blocks_for((0,), ((0, 1),), beside)
    hidden = activate_packed(own, far, near, rows, width)

    opposite = swap(hidden, "gx", n_gx, 3)
    first = [hidden, swap(hidden, "gx", n_gx, 1), opposite]
    second = [swap(opposite, "gx", n_gx, 1)]
    (partial_sum,) = down(first, (0, 1, 3), None, down_weight, rows, width, 1)
    outs = down(second, (2,), partial_sum, down_weight, rows, width, n_token)
    terms = [outs[0]] + [swap(outs[r], TOKEN_AXES, n_token, r) for r in range(1, n_token)]
    return finish(terms, tokens.shape)


def offloaded(tokens, gate_weight, up_weight, down_weight):
    features = lax.all_gather(tokens, TOKEN_AXES, axis=0, tiled=True)
    hidden_width = gate_weight.shape[1]
    gate_part = jnp.dot(features, gate_weight, preferred_element_type=jnp.float32)
    up_part = jnp.dot(features, up_weight, preferred_element_type=jnp.float32)
    summed = lax.psum(
        jnp.concatenate([gate_part, up_part], axis=1).astype(jnp.bfloat16), "gx"
    ).astype(jnp.float32)
    hidden = activate(summed[:, :hidden_width], summed[:, hidden_width:])
    partial_value = jnp.dot(hidden, down_weight, preferred_element_type=jnp.float32)
    return lax.psum_scatter(
        partial_value.astype(jnp.bfloat16), TOKEN_AXES, scatter_dimension=0, tiled=True
    )


def shards(tokens, gate_weight, up_weight, down_weight):
    n_gx = lax.axis_size("gx")
    n_token = lax.axis_size(TOKEN_AXES)
    rows = tokens.shape[0] * n_token
    tokens_fit = n_token > 1 and n_token & (n_token - 1) == 0 and rows % 4 == 0
    weights_fit = gate_weight.shape[1] % (128 * 4) == 0 and gate_weight.shape[0] % STEP == 0
    columns_fit = down_weight.shape[1] % (128 * 8) == 0
    if n_gx == 4 and tokens_fit and weights_fit and columns_fit:
        return direct(tokens, gate_weight, up_weight, down_weight)
    return offloaded(tokens, gate_weight, up_weight, down_weight)


def solution(mesh):
    return jax.shard_map(
        shards,
        mesh=mesh,
        in_specs=(
            P(("grp", "gy", "gz"), "gx"),
            P("gx", ("gy", "gz")),
            P("gx", ("gy", "gz")),
            P(("gy", "gz"), "gx"),
        ),
        out_specs=P(("grp", "gy", "gz"), "gx"),
        check_vma=False,
    )
```

```python
import functools

import jax
import jax.numpy as jnp
from jax import lax
from jax.experimental import pallas as pl
from jax.experimental.pallas import tpu as pltpu
from jax.sharding import PartitionSpec as P

MIB = 1 << 20
STEP = 256
COPY_STEP = 512
IN_FLIGHT = 6
DOWN_STEP = 512
TOKEN_AXES = ("gy", "gz")
IN_HBM = pl.BlockSpec(memory_space=pltpu.HBM)
ANY = pl.BlockSpec(memory_space=pl.ANY)
WHOLE = pl.BlockSpec(memory_space=pltpu.VMEM)


def activate(gate, up):
    return (jax.nn.silu(gate) * up).astype(jnp.bfloat16)


def pieces_of(total, step):
    return [(start, min(step, total - start)) for start in range(0, total, step)]


def in_hbm(value):
    return pltpu.with_memory_space_constraint(value, pltpu.HBM)


def in_vmem(value):
    return pltpu.with_memory_space_constraint(value, pltpu.VMEM)


SMALL = pl.CostEstimate(flops=0, bytes_accessed=MIB, transcendentals=0)


def block_start(distance, width):
    return pl.multiple_of((lax.axis_index("gx") ^ distance) * width, 128)


def params(mib):
    return pltpu.CompilerParams(vmem_limit_bytes=mib * MIB)


def packed_pair_width(rows, width):
    return (rows // 8) * 2 * width + (width if rows % 8 else 0)


def pack_pair(out, gate, up):
    rows, width = gate.shape
    for g in range(rows // 8):
        for w, value in enumerate((gate, up)):
            at = (2 * g + w) * width
            out[:, at : at + width] = value[8 * g : 8 * g + 8].astype(out.dtype)
    if rows % 8:
        at = (rows // 8) * 2 * width
        tail = jnp.concatenate([gate[rows - 4 :], up[rows - 4 :]], axis=0)
        out[:, at : at + width] = tail.astype(out.dtype)


def block_copies(width, distance, weights, held, sems):
    columns = pl.ds(block_start(distance, width), width)
    copies = []
    for k, (row, rows) in enumerate(pieces_of(held.shape[1], COPY_STEP)):
        for w, weight in enumerate(weights):
            copy = pltpu.make_async_copy(
                weight.at[pl.ds(row, rows), columns], held.at[w, pl.ds(row, rows)], sems.at[w, k]
            )
            copies.append((w, row, rows, copy))
    return copies


def fetch_kernel(width, distance, gate_ref, up_ref, held, sems):
    copies = block_copies(width, distance, (gate_ref, up_ref), held, sems)
    for _, _, _, copy in copies:
        copy.start()
    for _, _, _, copy in copies:
        copy.wait()


def fetch(gate_weight, up_weight, distance, width):
    depth = gate_weight.shape[0]
    return pl.pallas_call(
        functools.partial(fetch_kernel, width, distance),
        out_shape=pltpu.VMEM((2, depth, width), jnp.bfloat16),
        in_specs=[IN_HBM, IN_HBM],
        out_specs=WHOLE,
        scratch_shapes=[pltpu.SemaphoreType.DMA((2, len(pieces_of(depth, COPY_STEP))))],
        compiler_params=params(4),
        cost_estimate=SMALL,
    )(in_hbm(gate_weight), in_hbm(up_weight))


def multiply(x_ref, held, total, steps, waiting=()):
    for w, first, tall, copy in steps:
        if copy is not None:
            copy.wait()
        if waiting:
            waiting.pop(0).start()
        for row, rows in pieces_of(tall, STEP):
            rows = slice(first + row, first + row + rows)
            term = jnp.dot(x_ref[:, rows], held[w, rows, :], preferred_element_type=jnp.float32)
            if rows.start == 0:
                total[w] = term
            else:
                total[w] += term


def held_kernel(x_ref, held, out, total):
    parts = pieces_of(x_ref.shape[1], STEP)
    multiply(x_ref, held, total, [(w, row, rows, None) for w in range(2) for row, rows in parts])
    pack_pair(out, total[0], total[1])


def gate_up_held(features, held):
    rows, width = features.shape[0], held.shape[2]
    return pl.pallas_call(
        held_kernel,
        out_shape=jax.ShapeDtypeStruct((8, packed_pair_width(rows, width)), jnp.bfloat16),
        in_specs=[WHOLE, WHOLE],
        out_specs=WHOLE,
        scratch_shapes=[pltpu.VMEM((2, rows, width), jnp.float32)],
        compiler_params=params(8),
        cost_estimate=SMALL,
    )(features, in_vmem(held))


def stream_kernel(width, blocks, distances, x_ref, gate_ref, up_ref, _, *refs):
    outs, refs = refs[: len(blocks)], refs[len(blocks) :]
    work = []
    for b, which in enumerate(blocks):
        held, total, sems = refs[3 * b : 3 * b + 3]
        weights = [(gate_ref, up_ref)[w] for w in which]
        copies = block_copies(width, distances[b], weights, held, sems)
        work.append((outs[b], held, total, copies))
    waiting = [step[-1] for block in work for step in block[-1]]
    in_flight = IN_FLIGHT if len(blocks) > 1 else len(waiting)
    for copy in waiting[:in_flight]:
        copy.start()
    waiting = waiting[in_flight:]
    for (out, held, total, copies), which in zip(work, blocks):
        multiply(x_ref, held, total, copies, waiting)
        if len(which) == 2:
            pack_pair(out, total[0], total[1])
        else:
            pack_single(out, total[0])


def gate_up_stream(features, gate_weight, up_weight, distances, blocks, width, after):
    rows, depth = features.shape
    scratch, shapes = [], []
    for which in blocks:
        packed = packed_pair_width(rows, width) if len(which) == 2 else packed_width(rows, width)
        shapes.append(jax.ShapeDtypeStruct((8, packed), jnp.bfloat16))
        scratch += [
            pltpu.VMEM((len(which), depth, width), jnp.bfloat16),
            pltpu.VMEM((len(which), rows, width), jnp.float32),
            pltpu.SemaphoreType.DMA((len(which), len(pieces_of(depth, COPY_STEP)))),
        ]
    held_mib = -(-depth * width * 2 * sum(len(which) for which in blocks) // MIB)
    return pl.pallas_call(
        functools.partial(stream_kernel, width, blocks, distances),
        out_shape=shapes,
        in_specs=[WHOLE, IN_HBM, IN_HBM, ANY],
        out_specs=[WHOLE] * len(blocks),
        scratch_shapes=scratch,
        compiler_params=params(5 + held_mib),
        cost_estimate=SMALL,
    )(features, in_hbm(gate_weight), in_hbm(up_weight), after)


def hidden_tail(rows, width):
    half = pl.cdiv(width // 2, 128) * 128
    return half if rows % 8 else 0


def packed_width(rows, width):
    return (rows // 8) * width + hidden_tail(rows, width)


def pack_single(out, value):
    rows, width = value.shape
    for g in range(rows // 8):
        out[:, g * width : (g + 1) * width] = value[8 * g : 8 * g + 8].astype(out.dtype)
    if rows % 8:
        at, half = (rows // 8) * width, hidden_tail(rows, width)
        left, right = value[rows - 4 :, :half], value[rows - 4 :, half:]
        if 2 * half > width:
            right = jnp.concatenate([right, jnp.zeros((4, 2 * half - width), jnp.float32)], axis=1)
        out[:, at : at + half] = jnp.concatenate([left, right], axis=0).astype(out.dtype)


def last_rows(packed, rows, width):
    at, half = (rows // 8) * width, hidden_tail(rows, width)
    tail = packed[:, at : at + half].astype(jnp.float32)
    return jnp.concatenate([tail[:4], tail[4:, : width - half]], axis=1)


def activate_kernel(rows, width, own, far, gate_near, up_near, out):
    def pair(at):
        columns = slice(at, at + width)
        return own[:, columns].astype(jnp.float32) + far[:, columns].astype(jnp.float32)

    for g in range(rows // 8):
        near = slice(g * width, (g + 1) * width)
        out[:, near] = activate(
            pair(2 * g * width) + gate_near[:, near].astype(jnp.float32),
            pair((2 * g + 1) * width) + up_near[:, near].astype(jnp.float32),
        )
    if rows % 8:
        half = hidden_tail(rows, width)
        last = pair((rows // 8) * 2 * width)
        value = activate(
            last[:4] + last_rows(gate_near, rows, width),
            last[4:] + last_rows(up_near, rows, width),
        ).astype(jnp.float32)
        right = jnp.concatenate([value[:, half:], jnp.zeros((4, 2 * half - width), jnp.float32)], axis=1)
        at = (rows // 8) * width
        out[:, at : at + half] = jnp.concatenate([value[:, :half], right], axis=0).astype(out.dtype)


def activate_packed(own, far, near, rows, width):
    return pl.pallas_call(
        functools.partial(activate_kernel, rows, width),
        out_shape=jax.ShapeDtypeStruct((8, packed_width(rows, width)), jnp.bfloat16),
        in_specs=[WHOLE] * 4,
        out_specs=WHOLE,
        compiler_params=params(8),
        cost_estimate=SMALL,
    )(own, far, *near)


def pack_rows(out, value):
    rows, width = value.shape
    for g in range(rows // 8):
        out[:, g * width : (g + 1) * width] = value[8 * g : 8 * g + 8].astype(out.dtype)
    piece = width // 8
    for r in range(rows // 8 * 8, rows):
        at = (rows // 8) * width + (r % 8) * piece
        row = jnp.concatenate(
            [value[r : r + 1, i * piece : (i + 1) * piece] for i in range(8)], axis=0
        )
        out[:, at : at + piece] = row.astype(out.dtype)


def unpack_rows(out, packed):
    rows, width = out.shape
    for g in range(rows // 8):
        out[8 * g : 8 * g + 8, :] = packed[:, g * width : (g + 1) * width]
    piece = width // 8
    for r in range(rows // 8 * 8, rows):
        at = (rows // 8) * width + (r % 8) * piece
        for i in range(8):
            out[r : r + 1, i * piece : (i + 1) * piece] = packed[i : i + 1, at : at + piece]


def down_kernel(first, rows, width, distances, *refs):
    blocks = len(distances)
    hidden, refs = refs[:blocks], refs[blocks:]
    if not first:
        before, refs = refs[0], refs[1:]
    held, outs, (plain, total) = refs[0], refs[1:-2], refs[-2:]
    if first:
        total = outs[0]
    for b in range(blocks):
        for g in range(rows // 8):
            plain[8 * g : 8 * g + 8, :] = hidden[b][:, g * width : (g + 1) * width].astype(jnp.float32)
        if rows % 8:
            at, half = (rows // 8) * width, hidden_tail(rows, width)
            tail = hidden[b][:, at : at + half].astype(jnp.float32)
            plain[rows - 4 :, :half] = tail[:4]
            plain[rows - 4 :, half:] = tail[4:, : width - half]
        for row, tall in pieces_of(width, DOWN_STEP):
            term = jnp.dot(
                plain[:, row : row + tall].astype(jnp.bfloat16),
                held[pl.ds(pl.multiple_of(block_start(distances[b], width) + row, 128), tall), :],
                preferred_element_type=jnp.float32,
            )
            if b == 0 and row == 0:
                total[...] = term if first else before[...] + term
            else:
                total[...] += term
    if not first:
        tall = rows // len(outs)
        for r, out in enumerate(outs):
            pack_rows(out, total[r * tall : (r + 1) * tall, :])


def down(hidden, distances, before, weight, rows, width, outs):
    columns = weight.shape[1]
    if before is None:
        shapes = [jax.ShapeDtypeStruct((rows, columns), jnp.float32)]
    else:
        packed = (8, rows // outs * columns // 8)
        shapes = [jax.ShapeDtypeStruct(packed, jnp.bfloat16 if r else jnp.float32) for r in range(outs)]
    carried = [] if before is None else [before]
    return pl.pallas_call(
        functools.partial(down_kernel, before is None, rows, width, distances),
        out_shape=shapes,
        in_specs=[WHOLE] * (len(hidden) + len(carried) + 1),
        out_specs=[WHOLE] * len(shapes),
        scratch_shapes=[
            pltpu.VMEM((rows, width), jnp.float32),
            pltpu.VMEM((rows, columns), jnp.float32),
        ],
        compiler_params=params(8),
        cost_estimate=SMALL,
    )(*hidden, *carried, in_vmem(weight))


def finish_kernel(*refs):
    terms, out, plain = refs[:-2], refs[-2], refs[-1]
    packed = terms[0][...]
    for term in terms[1:]:
        packed = packed + term[...].astype(jnp.float32)
    unpack_rows(plain, packed)
    out[...] = plain[...].astype(out.dtype)


def finish(terms, shape):
    return pl.pallas_call(
        finish_kernel,
        out_shape=jax.ShapeDtypeStruct(shape, jnp.bfloat16),
        in_specs=[WHOLE] * len(terms),
        out_specs=WHOLE,
        scratch_shapes=[pltpu.VMEM(shape, jnp.float32)],
        compiler_params=params(4),
        cost_estimate=SMALL,
    )(*terms)


def swap(value, axes, size, distance):
    return lax.ppermute(value, axes, [(i, i ^ distance) for i in range(size)])


def add(a, b):
    return a.astype(jnp.float32) + b.astype(jnp.float32)


def direct(tokens, gate_weight, up_weight, down_weight):
    n_gx = lax.axis_size("gx")
    n_token = lax.axis_size(TOKEN_AXES)
    width = gate_weight.shape[1] // n_gx

    held = fetch(gate_weight, up_weight, 2, width)
    features = jnp.concatenate(
        [tokens] + [swap(tokens, TOKEN_AXES, n_token, r) for r in range(1, n_token)], axis=0
    )
    rows = features.shape[0]

    def blocks_for(distances, blocks, after):
        return gate_up_stream(features, gate_weight, up_weight, distances, blocks, width, after)

    relayed = gate_up_held(features, held)
    arrived = swap(relayed, "gx", n_gx, 1)
    across, beside = blocks_for((3, 1), ((0, 1), (0,)), relayed)
    across = lax.optimization_barrier(add(across, arrived).astype(jnp.bfloat16))
    far = swap(across, "gx", n_gx, 3)
    near = [swap(beside, "gx", n_gx, 1)]
    (beside,) = blocks_for((1,), ((1,),), across)
    near.append(swap(beside, "gx", n_gx, 1))
    (own,) = blocks_for((0,), ((0, 1),), beside)
    hidden = activate_packed(own, far, near, rows, width)

    opposite = swap(hidden, "gx", n_gx, 2)
    first = [hidden, swap(hidden, "gx", n_gx, 1), opposite]
    second = [swap(opposite, "gx", n_gx, 1)]
    (partial_sum,) = down(first, (0, 1, 2), None, down_weight, rows, width, 1)
    outs = down(second, (3,), partial_sum, down_weight, rows, width, n_token)
    terms = [outs[0]] + [swap(outs[r], TOKEN_AXES, n_token, r) for r in range(1, n_token)]
    return finish(terms, tokens.shape)


def offloaded(tokens, gate_weight, up_weight, down_weight):
    features = lax.all_gather(tokens, TOKEN_AXES, axis=0, tiled=True)
    hidden_width = gate_weight.shape[1]
    gate_part = jnp.dot(features, gate_weight, preferred_element_type=jnp.float32)
    up_part = jnp.dot(features, up_weight, preferred_element_type=jnp.float32)
    summed = lax.psum(
        jnp.concatenate([gate_part, up_part], axis=1).astype(jnp.bfloat16), "gx"
    ).astype(jnp.float32)
    hidden = activate(summed[:, :hidden_width], summed[:, hidden_width:])
    partial_value = jnp.dot(hidden, down_weight, preferred_element_type=jnp.float32)
    return lax.psum_scatter(
        partial_value.astype(jnp.bfloat16), TOKEN_AXES, scatter_dimension=0, tiled=True
    )


def shards(tokens, gate_weight, up_weight, down_weight):
    n_gx = lax.axis_size("gx")
    n_token = lax.axis_size(TOKEN_AXES)
    rows = tokens.shape[0] * n_token
    tokens_fit = n_token > 1 and n_token & (n_token - 1) == 0 and rows % 4 == 0
    weights_fit = gate_weight.shape[1] % (128 * 4) == 0 and gate_weight.shape[0] % STEP == 0
    columns_fit = down_weight.shape[1] % (128 * 8) == 0
    if n_gx == 4 and tokens_fit and weights_fit and columns_fit:
        return direct(tokens, gate_weight, up_weight, down_weight)
    return offloaded(tokens, gate_weight, up_weight, down_weight)


def solution(mesh):
    return jax.shard_map(
        shards,
        mesh=mesh,
        in_specs=(
            P(("grp", "gy", "gz"), "gx"),
            P("gx", ("gy", "gz")),
            P("gx", ("gy", "gz")),
            P(("gy", "gz"), "gx"),
        ),
        out_specs=P(("grp", "gy", "gz"), "gx"),
        check_vma=False,
    )
```

```python
import functools

import jax
import jax.numpy as jnp
from jax import lax
from jax.experimental import pallas as pl
from jax.experimental.pallas import tpu as pltpu
from jax.sharding import PartitionSpec as P

MIB = 1 << 20
STEP = 256
COPY_STEP = 512
IN_FLIGHT = 6
DOWN_STEP = 512
LARGE_STEP = 1024
TOKEN_AXES = ("gy", "gz")
IN_HBM = pl.BlockSpec(memory_space=pltpu.HBM)
ANY = pl.BlockSpec(memory_space=pl.ANY)
WHOLE = pl.BlockSpec(memory_space=pltpu.VMEM)


def activate(gate, up):
    return (jax.nn.silu(gate) * up).astype(jnp.bfloat16)


def pieces_of(total, step):
    return [(start, min(step, total - start)) for start in range(0, total, step)]


def in_hbm(value):
    return pltpu.with_memory_space_constraint(value, pltpu.HBM)


def in_vmem(value):
    return pltpu.with_memory_space_constraint(value, pltpu.VMEM)


SMALL = pl.CostEstimate(flops=0, bytes_accessed=MIB, transcendentals=0)


def block_start(distance, width):
    return pl.multiple_of((lax.axis_index("gx") ^ distance) * width, 128)


def params(mib):
    return pltpu.CompilerParams(vmem_limit_bytes=mib * MIB)


def packed_pair_width(rows, width):
    return (rows // 8) * 2 * width + (width if rows % 8 else 0)


def pack_pair(out, gate, up):
    rows, width = gate.shape
    for g in range(rows // 8):
        for w, value in enumerate((gate, up)):
            at = (2 * g + w) * width
            out[:, at : at + width] = value[8 * g : 8 * g + 8].astype(out.dtype)
    if rows % 8:
        at = (rows // 8) * 2 * width
        tail = jnp.concatenate([gate[rows - 4 :], up[rows - 4 :]], axis=0)
        out[:, at : at + width] = tail.astype(out.dtype)


def block_copies(width, distance, weights, held, sems, step, first=0):
    columns = pl.ds(block_start(distance, width), width)
    copies = []
    for k, (row, rows) in enumerate(pieces_of(held.shape[1], step)):
        for w, weight in enumerate(weights):
            copy = pltpu.make_async_copy(
                weight.at[pl.ds(first + row, rows), columns],
                held.at[w, pl.ds(row, rows)],
                sems.at[w, k],
            )
            copies.append((w, row, rows, copy))
    return copies


def copy_sems(weights, depth, step):
    return pltpu.SemaphoreType.DMA((weights, len(pieces_of(depth, step))))


def fetch_kernel(width, distance, gate_ref, up_ref, held, sems):
    copies = block_copies(width, distance, (gate_ref, up_ref), held, sems, COPY_STEP)
    for _, _, _, copy in copies:
        copy.start()
    for _, _, _, copy in copies:
        copy.wait()


def fetch(gate_weight, up_weight, distance, depth, width):
    return pl.pallas_call(
        functools.partial(fetch_kernel, width, distance),
        out_shape=pltpu.VMEM((2, depth, width), jnp.bfloat16),
        in_specs=[IN_HBM, IN_HBM],
        out_specs=WHOLE,
        scratch_shapes=[copy_sems(2, depth, COPY_STEP)],
        compiler_params=params(4),
        cost_estimate=SMALL,
    )(in_hbm(gate_weight), in_hbm(up_weight))


def multiply(x_ref, held, total, steps, waiting=(), first=0):
    for w, top, tall, copy in steps:
        if copy is not None:
            copy.wait()
        if waiting:
            waiting.pop(0).start()
        for row, rows in pieces_of(tall, STEP):
            at = first + top + row
            term = jnp.dot(
                x_ref[:, at : at + rows],
                held[w, top + row : top + row + rows, :],
                preferred_element_type=jnp.float32,
            )
            if at == 0:
                total[w] = term
            else:
                total[w] += term


def held_kernel(width, distance, x_ref, held, gate_ref, up_ref, out, stream, total, sems):
    first = held.shape[1]
    copies = block_copies(width, distance, (gate_ref, up_ref), stream, sems, COPY_STEP, first)
    for _, _, _, copy in copies:
        copy.start()
    steps = [(w, row, rows, None) for row, rows in pieces_of(first, STEP) for w in range(2)]
    multiply(x_ref, held, total, steps)
    multiply(x_ref, stream, total, copies, first=first)
    pack_pair(out, total[0], total[1])


def gate_up_held(features, held, gate_weight, up_weight, distance):
    rows, depth = features.shape
    width = held.shape[2]
    below = depth - held.shape[1]
    return pl.pallas_call(
        functools.partial(held_kernel, width, distance),
        out_shape=jax.ShapeDtypeStruct((8, packed_pair_width(rows, width)), jnp.bfloat16),
        in_specs=[WHOLE, WHOLE, IN_HBM, IN_HBM],
        out_specs=WHOLE,
        scratch_shapes=[
            pltpu.VMEM((2, below, width), jnp.bfloat16),
            pltpu.VMEM((2, rows, width), jnp.float32),
            copy_sems(2, below, COPY_STEP),
        ],
        compiler_params=params(5 + -(-below * width * 4 // MIB)),
        cost_estimate=SMALL,
    )(features, in_vmem(held), in_hbm(gate_weight), in_hbm(up_weight))


def stream_step(blocks):
    return LARGE_STEP if blocks == ((0, 1),) else COPY_STEP


def stream_kernel(width, blocks, distances, x_ref, gate_ref, up_ref, _, *refs):
    outs, refs = refs[: len(blocks)], refs[len(blocks) :]
    work = []
    for b, which in enumerate(blocks):
        held, total, sems = refs[3 * b : 3 * b + 3]
        weights = [(gate_ref, up_ref)[w] for w in which]
        copies = block_copies(width, distances[b], weights, held, sems, stream_step(blocks))
        work.append((outs[b], held, total, copies))
    waiting = [step[-1] for block in work for step in block[-1]]
    in_flight = IN_FLIGHT if len(blocks) > 1 else len(waiting)
    for copy in waiting[:in_flight]:
        copy.start()
    waiting = waiting[in_flight:]
    for (out, held, total, copies), which in zip(work, blocks):
        multiply(x_ref, held, total, copies, waiting)
        if len(which) == 2:
            pack_pair(out, total[0], total[1])
        else:
            pack_single(out, total[0])


def gate_up_stream(features, gate_weight, up_weight, distances, blocks, width, after):
    rows, depth = features.shape
    scratch, shapes = [], []
    for which in blocks:
        packed = packed_pair_width(rows, width) if len(which) == 2 else packed_width(rows, width)
        shapes.append(jax.ShapeDtypeStruct((8, packed), jnp.bfloat16))
        scratch += [
            pltpu.VMEM((len(which), depth, width), jnp.bfloat16),
            pltpu.VMEM((len(which), rows, width), jnp.float32),
            copy_sems(len(which), depth, stream_step(blocks)),
        ]
    held_mib = -(-depth * width * 2 * sum(len(which) for which in blocks) // MIB)
    return pl.pallas_call(
        functools.partial(stream_kernel, width, blocks, distances),
        out_shape=shapes,
        in_specs=[WHOLE, IN_HBM, IN_HBM, ANY],
        out_specs=[WHOLE] * len(blocks),
        scratch_shapes=scratch,
        compiler_params=params(5 + held_mib),
        cost_estimate=SMALL,
    )(features, in_hbm(gate_weight), in_hbm(up_weight), after)


def hidden_tail(rows, width):
    half = pl.cdiv(width // 2, 128) * 128
    return half if rows % 8 else 0


def packed_width(rows, width):
    return (rows // 8) * width + hidden_tail(rows, width)


def pack_single(out, value):
    rows, width = value.shape
    for g in range(rows // 8):
        out[:, g * width : (g + 1) * width] = value[8 * g : 8 * g + 8].astype(out.dtype)
    if rows % 8:
        at, half = (rows // 8) * width, hidden_tail(rows, width)
        left, right = value[rows - 4 :, :half], value[rows - 4 :, half:]
        if 2 * half > width:
            right = jnp.concatenate([right, jnp.zeros((4, 2 * half - width), jnp.float32)], axis=1)
        out[:, at : at + half] = jnp.concatenate([left, right], axis=0).astype(out.dtype)


def last_rows(packed, rows, width):
    at, half = (rows // 8) * width, hidden_tail(rows, width)
    tail = packed[:, at : at + half].astype(jnp.float32)
    return jnp.concatenate([tail[:4], tail[4:, : width - half]], axis=1)


def activate_kernel(rows, width, own, far, gate_near, up_near, out):
    def pair(at):
        columns = slice(at, at + width)
        return own[:, columns].astype(jnp.float32) + far[:, columns].astype(jnp.float32)

    for g in range(rows // 8):
        near = slice(g * width, (g + 1) * width)
        out[:, near] = activate(
            pair(2 * g * width) + gate_near[:, near].astype(jnp.float32),
            pair((2 * g + 1) * width) + up_near[:, near].astype(jnp.float32),
        )
    if rows % 8:
        half = hidden_tail(rows, width)
        last = pair((rows // 8) * 2 * width)
        value = activate(
            last[:4] + last_rows(gate_near, rows, width),
            last[4:] + last_rows(up_near, rows, width),
        ).astype(jnp.float32)
        right = jnp.concatenate([value[:, half:], jnp.zeros((4, 2 * half - width), jnp.float32)], axis=1)
        at = (rows // 8) * width
        out[:, at : at + half] = jnp.concatenate([value[:, :half], right], axis=0).astype(out.dtype)


def activate_packed(own, far, near, rows, width):
    return pl.pallas_call(
        functools.partial(activate_kernel, rows, width),
        out_shape=jax.ShapeDtypeStruct((8, packed_width(rows, width)), jnp.bfloat16),
        in_specs=[WHOLE] * 4,
        out_specs=WHOLE,
        compiler_params=params(8),
        cost_estimate=SMALL,
    )(own, far, *near)


def pack_rows(out, value):
    rows, width = value.shape
    for g in range(rows // 8):
        out[:, g * width : (g + 1) * width] = value[8 * g : 8 * g + 8].astype(out.dtype)
    piece = width // 8
    for r in range(rows // 8 * 8, rows):
        at = (rows // 8) * width + (r % 8) * piece
        row = jnp.concatenate(
            [value[r : r + 1, i * piece : (i + 1) * piece] for i in range(8)], axis=0
        )
        out[:, at : at + piece] = row.astype(out.dtype)


def unpack_rows(out, packed):
    rows, width = out.shape
    for g in range(rows // 8):
        out[8 * g : 8 * g + 8, :] = packed[:, g * width : (g + 1) * width]
    piece = width // 8
    for r in range(rows // 8 * 8, rows):
        at = (rows // 8) * width + (r % 8) * piece
        for i in range(8):
            out[r : r + 1, i * piece : (i + 1) * piece] = packed[i : i + 1, at : at + piece]


def down_kernel(first, rows, width, distances, *refs):
    blocks = len(distances)
    hidden, refs = refs[:blocks], refs[blocks:]
    if not first:
        before, refs = refs[0], refs[1:]
    held, outs, (plain, total) = refs[0], refs[1:-2], refs[-2:]
    if first:
        total = outs[0]
    for b in range(blocks):
        for g in range(rows // 8):
            plain[8 * g : 8 * g + 8, :] = hidden[b][:, g * width : (g + 1) * width].astype(jnp.float32)
        if rows % 8:
            at, half = (rows // 8) * width, hidden_tail(rows, width)
            tail = hidden[b][:, at : at + half].astype(jnp.float32)
            plain[rows - 4 :, :half] = tail[:4]
            plain[rows - 4 :, half:] = tail[4:, : width - half]
        for row, tall in pieces_of(width, DOWN_STEP):
            term = jnp.dot(
                plain[:, row : row + tall].astype(jnp.bfloat16),
                held[pl.ds(pl.multiple_of(block_start(distances[b], width) + row, 128), tall), :],
                preferred_element_type=jnp.float32,
            )
            if b == 0 and row == 0:
                total[...] = term if first else before[...] + term
            else:
                total[...] += term
    if not first:
        tall = rows // len(outs)
        for r, out in enumerate(outs):
            pack_rows(out, total[r * tall : (r + 1) * tall, :])


def down(hidden, distances, before, weight, rows, width, outs):
    columns = weight.shape[1]
    if before is None:
        shapes = [jax.ShapeDtypeStruct((rows, columns), jnp.float32)]
    else:
        packed = (8, rows // outs * columns // 8)
        shapes = [jax.ShapeDtypeStruct(packed, jnp.bfloat16 if r else jnp.float32) for r in range(outs)]
    carried = [] if before is None else [before]
    return pl.pallas_call(
        functools.partial(down_kernel, before is None, rows, width, distances),
        out_shape=shapes,
        in_specs=[WHOLE] * (len(hidden) + len(carried) + 1),
        out_specs=[WHOLE] * len(shapes),
        scratch_shapes=[
            pltpu.VMEM((rows, width), jnp.float32),
            pltpu.VMEM((rows, columns), jnp.float32),
        ],
        compiler_params=params(8),
        cost_estimate=SMALL,
    )(*hidden, *carried, in_vmem(weight))


def finish_kernel(*refs):
    terms, out, plain = refs[:-2], refs[-2], refs[-1]
    packed = terms[0][...]
    for term in terms[1:]:
        packed = packed + term[...].astype(jnp.float32)
    unpack_rows(plain, packed)
    out[...] = plain[...].astype(out.dtype)


def finish(terms, shape):
    return pl.pallas_call(
        finish_kernel,
        out_shape=jax.ShapeDtypeStruct(shape, jnp.bfloat16),
        in_specs=[WHOLE] * len(terms),
        out_specs=WHOLE,
        scratch_shapes=[pltpu.VMEM(shape, jnp.float32)],
        compiler_params=params(4),
        cost_estimate=SMALL,
    )(*terms)


def swap(value, axes, size, distance):
    return lax.ppermute(value, axes, [(i, i ^ distance) for i in range(size)])


def add(a, b):
    return a.astype(jnp.float32) + b.astype(jnp.float32)


def direct(tokens, gate_weight, up_weight, down_weight):
    n_gx = lax.axis_size("gx")
    n_token = lax.axis_size(TOKEN_AXES)
    width = gate_weight.shape[1] // n_gx

    early = gate_weight.shape[0] // 4 * 3 // STEP * STEP
    held = fetch(gate_weight, up_weight, 2, early, width)
    features = jnp.concatenate(
        [tokens] + [swap(tokens, TOKEN_AXES, n_token, r) for r in range(1, n_token)], axis=0
    )
    rows = features.shape[0]

    def blocks_for(distances, blocks, after):
        return gate_up_stream(features, gate_weight, up_weight, distances, blocks, width, after)

    relayed = gate_up_held(features, held, gate_weight, up_weight, 2)
    arrived = swap(relayed, "gx", n_gx, 1)
    across, beside = blocks_for((3, 1), ((0, 1), (0,)), relayed)
    across = lax.optimization_barrier(add(across, arrived).astype(jnp.bfloat16))
    far = swap(across, "gx", n_gx, 3)
    near = [swap(beside, "gx", n_gx, 1)]
    (beside,) = blocks_for((1,), ((1,),), across)
    near.append(swap(beside, "gx", n_gx, 1))
    (own,) = blocks_for((0,), ((0, 1),), beside)
    hidden = activate_packed(own, far, near, rows, width)

    opposite = swap(hidden, "gx", n_gx, 2)
    first = [hidden, swap(hidden, "gx", n_gx, 1), opposite]
    second = [swap(opposite, "gx", n_gx, 1)]
    (partial_sum,) = down(first, (0, 1, 2), None, down_weight, rows, width, 1)
    outs = down(second, (3,), partial_sum, down_weight, rows, width, n_token)
    terms = [outs[0]] + [swap(outs[r], TOKEN_AXES, n_token, r) for r in range(1, n_token)]
    return finish(terms, tokens.shape)


def offloaded(tokens, gate_weight, up_weight, down_weight):
    features = lax.all_gather(tokens, TOKEN_AXES, axis=0, tiled=True)
    hidden_width = gate_weight.shape[1]
    gate_part = jnp.dot(features, gate_weight, preferred_element_type=jnp.float32)
    up_part = jnp.dot(features, up_weight, preferred_element_type=jnp.float32)
    summed = lax.psum(
        jnp.concatenate([gate_part, up_part], axis=1).astype(jnp.bfloat16), "gx"
    ).astype(jnp.float32)
    hidden = activate(summed[:, :hidden_width], summed[:, hidden_width:])
    partial_value = jnp.dot(hidden, down_weight, preferred_element_type=jnp.float32)
    return lax.psum_scatter(
        partial_value.astype(jnp.bfloat16), TOKEN_AXES, scatter_dimension=0, tiled=True
    )


def shards(tokens, gate_weight, up_weight, down_weight):
    n_gx = lax.axis_size("gx")
    n_token = lax.axis_size(TOKEN_AXES)
    rows = tokens.shape[0] * n_token
    tokens_fit = n_token > 1 and n_token & (n_token - 1) == 0 and rows % 4 == 0
    weights_fit = gate_weight.shape[1] % (128 * 4) == 0 and gate_weight.shape[0] % (4 * STEP) == 0
    columns_fit = down_weight.shape[1] % (128 * 8) == 0
    if n_gx == 4 and tokens_fit and weights_fit and columns_fit:
        return direct(tokens, gate_weight, up_weight, down_weight)
    return offloaded(tokens, gate_weight, up_weight, down_weight)


def solution(mesh):
    return jax.shard_map(
        shards,
        mesh=mesh,
        in_specs=(
            P(("grp", "gy", "gz"), "gx"),
            P("gx", ("gy", "gz")),
            P("gx", ("gy", "gz")),
            P(("gy", "gz"), "gx"),
        ),
        out_specs=P(("grp", "gy", "gz"), "gx"),
        check_vma=False,
    )
```

```python
import functools

import jax
import jax.numpy as jnp
from jax import lax
from jax.experimental import pallas as pl
from jax.experimental.pallas import tpu as pltpu
from jax.sharding import PartitionSpec as P

MIB = 1 << 20
STEP = 256
COPY_STEP = 512
IN_FLIGHT = 5
DOWN_STEP = 512
TOKEN_AXES = ("gy", "gz")
IN_HBM = pl.BlockSpec(memory_space=pltpu.HBM)
ANY = pl.BlockSpec(memory_space=pl.ANY)
WHOLE = pl.BlockSpec(memory_space=pltpu.VMEM)


def activate(gate, up):
    return (jax.nn.silu(gate) * up).astype(jnp.bfloat16)


def pieces_of(total, step):
    return [(start, min(step, total - start)) for start in range(0, total, step)]


def in_hbm(value):
    return pltpu.with_memory_space_constraint(value, pltpu.HBM)


def in_vmem(value):
    return pltpu.with_memory_space_constraint(value, pltpu.VMEM)


SMALL = pl.CostEstimate(flops=0, bytes_accessed=MIB, transcendentals=0)


def block_start(distance, width):
    return pl.multiple_of((lax.axis_index("gx") ^ distance) * width, 128)


def params(mib):
    return pltpu.CompilerParams(vmem_limit_bytes=mib * MIB)


def packed_pair_width(rows, width):
    return (rows // 8) * 2 * width + (width if rows % 8 else 0)


def pack_pair(out, gate, up):
    rows, width = gate.shape
    for g in range(rows // 8):
        for w, value in enumerate((gate, up)):
            at = (2 * g + w) * width
            out[:, at : at + width] = value[8 * g : 8 * g + 8].astype(out.dtype)
    if rows % 8:
        at = (rows // 8) * 2 * width
        tail = jnp.concatenate([gate[rows - 4 :], up[rows - 4 :]], axis=0)
        out[:, at : at + width] = tail.astype(out.dtype)


def block_copies(width, distance, weights, held, sems):
    columns = pl.ds(block_start(distance, width), width)
    copies = []
    for k, (row, rows) in enumerate(pieces_of(held.shape[1], COPY_STEP)):
        for w, weight in enumerate(weights):
            copy = pltpu.make_async_copy(
                weight.at[pl.ds(row, rows), columns], held.at[w, pl.ds(row, rows)], sems.at[w, k]
            )
            copies.append((w, row, rows, copy))
    return copies


def fetch_kernel(width, distance, gate_ref, up_ref, held, sems):
    copies = block_copies(width, distance, (gate_ref, up_ref), held, sems)
    for _, _, _, copy in copies:
        copy.start()
    for _, _, _, copy in copies:
        copy.wait()


def fetch(gate_weight, up_weight, distance, width):
    depth = gate_weight.shape[0]
    return pl.pallas_call(
        functools.partial(fetch_kernel, width, distance),
        out_shape=pltpu.VMEM((2, depth, width), jnp.bfloat16),
        in_specs=[IN_HBM, IN_HBM],
        out_specs=WHOLE,
        scratch_shapes=[pltpu.SemaphoreType.DMA((2, len(pieces_of(depth, COPY_STEP))))],
        compiler_params=params(4),
        cost_estimate=SMALL,
    )(in_hbm(gate_weight), in_hbm(up_weight))


def multiply(x_ref, held, total, steps, waiting=()):
    for w, first, tall, copy in steps:
        if copy is not None:
            copy.wait()
        if waiting:
            waiting.pop(0).start()
        for row, rows in pieces_of(tall, STEP):
            rows = slice(first + row, first + row + rows)
            term = jnp.dot(x_ref[:, rows], held[w, rows, :], preferred_element_type=jnp.float32)
            if rows.start == 0:
                total[w] = term
            else:
                total[w] += term


def held_kernel(x_ref, held, out, total):
    parts = pieces_of(x_ref.shape[1], STEP)
    multiply(x_ref, held, total, [(w, row, rows, None) for w in range(2) for row, rows in parts])
    pack_pair(out, total[0], total[1])


def gate_up_held(features, held):
    rows, width = features.shape[0], held.shape[2]
    return pl.pallas_call(
        held_kernel,
        out_shape=jax.ShapeDtypeStruct((8, packed_pair_width(rows, width)), jnp.bfloat16),
        in_specs=[WHOLE, WHOLE],
        out_specs=WHOLE,
        scratch_shapes=[pltpu.VMEM((2, rows, width), jnp.float32)],
        compiler_params=params(8),
        cost_estimate=SMALL,
    )(features, in_vmem(held))


def stream_kernel(width, blocks, distances, x_ref, gate_ref, up_ref, _, *refs):
    outs, refs = refs[: len(blocks)], refs[len(blocks) :]
    work = []
    for b, which in enumerate(blocks):
        held, total, sems = refs[3 * b : 3 * b + 3]
        weights = [(gate_ref, up_ref)[w] for w in which]
        copies = block_copies(width, distances[b], weights, held, sems)
        work.append((outs[b], held, total, copies))
    waiting = [step[-1] for block in work for step in block[-1]]
    in_flight = IN_FLIGHT if len(blocks) > 1 else len(waiting)
    for copy in waiting[:in_flight]:
        copy.start()
    waiting = waiting[in_flight:]
    for (out, held, total, copies), which in zip(work, blocks):
        multiply(x_ref, held, total, copies, waiting)
        if len(which) == 2:
            pack_pair(out, total[0], total[1])
        else:
            pack_single(out, total[0])


def gate_up_stream(features, gate_weight, up_weight, distances, blocks, width, after):
    rows, depth = features.shape
    scratch, shapes = [], []
    for which in blocks:
        packed = packed_pair_width(rows, width) if len(which) == 2 else packed_width(rows, width)
        shapes.append(jax.ShapeDtypeStruct((8, packed), jnp.bfloat16))
        scratch += [
            pltpu.VMEM((len(which), depth, width), jnp.bfloat16),
            pltpu.VMEM((len(which), rows, width), jnp.float32),
            pltpu.SemaphoreType.DMA((len(which), len(pieces_of(depth, COPY_STEP)))),
        ]
    held_mib = -(-depth * width * 2 * sum(len(which) for which in blocks) // MIB)
    return pl.pallas_call(
        functools.partial(stream_kernel, width, blocks, distances),
        out_shape=shapes,
        in_specs=[WHOLE, IN_HBM, IN_HBM, ANY],
        out_specs=[WHOLE] * len(blocks),
        scratch_shapes=scratch,
        compiler_params=params(5 + held_mib),
        cost_estimate=SMALL,
    )(features, in_hbm(gate_weight), in_hbm(up_weight), after)


def hidden_tail(rows, width):
    half = pl.cdiv(width // 2, 128) * 128
    return half if rows % 8 else 0


def packed_width(rows, width):
    return (rows // 8) * width + hidden_tail(rows, width)


def pack_single(out, value):
    rows, width = value.shape
    for g in range(rows // 8):
        out[:, g * width : (g + 1) * width] = value[8 * g : 8 * g + 8].astype(out.dtype)
    if rows % 8:
        at, half = (rows // 8) * width, hidden_tail(rows, width)
        left, right = value[rows - 4 :, :half], value[rows - 4 :, half:]
        if 2 * half > width:
            right = jnp.concatenate([right, jnp.zeros((4, 2 * half - width), jnp.float32)], axis=1)
        out[:, at : at + half] = jnp.concatenate([left, right], axis=0).astype(out.dtype)


def last_rows(packed, rows, width):
    at, half = (rows // 8) * width, hidden_tail(rows, width)
    tail = packed[:, at : at + half].astype(jnp.float32)
    return jnp.concatenate([tail[:4], tail[4:, : width - half]], axis=1)


def activate_kernel(rows, width, own, far, gate_near, up_near, out):
    def pair(at):
        columns = slice(at, at + width)
        return own[:, columns].astype(jnp.float32) + far[:, columns].astype(jnp.float32)

    for g in range(rows // 8):
        near = slice(g * width, (g + 1) * width)
        out[:, near] = activate(
            pair(2 * g * width) + gate_near[:, near].astype(jnp.float32),
            pair((2 * g + 1) * width) + up_near[:, near].astype(jnp.float32),
        )
    if rows % 8:
        half = hidden_tail(rows, width)
        last = pair((rows // 8) * 2 * width)
        value = activate(
            last[:4] + last_rows(gate_near, rows, width),
            last[4:] + last_rows(up_near, rows, width),
        ).astype(jnp.float32)
        right = jnp.concatenate([value[:, half:], jnp.zeros((4, 2 * half - width), jnp.float32)], axis=1)
        at = (rows // 8) * width
        out[:, at : at + half] = jnp.concatenate([value[:, :half], right], axis=0).astype(out.dtype)


def activate_packed(own, far, near, rows, width):
    return pl.pallas_call(
        functools.partial(activate_kernel, rows, width),
        out_shape=jax.ShapeDtypeStruct((8, packed_width(rows, width)), jnp.bfloat16),
        in_specs=[WHOLE] * 4,
        out_specs=WHOLE,
        compiler_params=params(8),
        cost_estimate=SMALL,
    )(own, far, *near)


def pack_rows(out, value):
    rows, width = value.shape
    for g in range(rows // 8):
        out[:, g * width : (g + 1) * width] = value[8 * g : 8 * g + 8].astype(out.dtype)
    piece = width // 8
    for r in range(rows // 8 * 8, rows):
        at = (rows // 8) * width + (r % 8) * piece
        row = jnp.concatenate(
            [value[r : r + 1, i * piece : (i + 1) * piece] for i in range(8)], axis=0
        )
        out[:, at : at + piece] = row.astype(out.dtype)


def unpack_rows(out, packed):
    rows, width = out.shape
    for g in range(rows // 8):
        out[8 * g : 8 * g + 8, :] = packed[:, g * width : (g + 1) * width]
    piece = width // 8
    for r in range(rows // 8 * 8, rows):
        at = (rows // 8) * width + (r % 8) * piece
        for i in range(8):
            out[r : r + 1, i * piece : (i + 1) * piece] = packed[i : i + 1, at : at + piece]


def down_kernel(first, rows, width, distances, *refs):
    blocks = len(distances)
    hidden, refs = refs[:blocks], refs[blocks:]
    if not first:
        before, refs = refs[0], refs[1:]
    held, outs, (plain, total) = refs[0], refs[1:-2], refs[-2:]
    if first:
        total = outs[0]
    for b in range(blocks):
        for g in range(rows // 8):
            plain[8 * g : 8 * g + 8, :] = hidden[b][:, g * width : (g + 1) * width].astype(jnp.float32)
        if rows % 8:
            at, half = (rows // 8) * width, hidden_tail(rows, width)
            tail = hidden[b][:, at : at + half].astype(jnp.float32)
            plain[rows - 4 :, :half] = tail[:4]
            plain[rows - 4 :, half:] = tail[4:, : width - half]
        for row, tall in pieces_of(width, DOWN_STEP):
            term = jnp.dot(
                plain[:, row : row + tall].astype(jnp.bfloat16),
                held[pl.ds(pl.multiple_of(block_start(distances[b], width) + row, 128), tall), :],
                preferred_element_type=jnp.float32,
            )
            if b == 0 and row == 0:
                total[...] = term if first else before[...] + term
            else:
                total[...] += term
    if not first:
        tall = rows // len(outs)
        for r, out in enumerate(outs):
            pack_rows(out, total[r * tall : (r + 1) * tall, :])


def down(hidden, distances, before, weight, rows, width, outs):
    columns = weight.shape[1]
    if before is None:
        shapes = [jax.ShapeDtypeStruct((rows, columns), jnp.float32)]
    else:
        packed = (8, rows // outs * columns // 8)
        shapes = [jax.ShapeDtypeStruct(packed, jnp.bfloat16 if r else jnp.float32) for r in range(outs)]
    carried = [] if before is None else [before]
    return pl.pallas_call(
        functools.partial(down_kernel, before is None, rows, width, distances),
        out_shape=shapes,
        in_specs=[WHOLE] * (len(hidden) + len(carried) + 1),
        out_specs=[WHOLE] * len(shapes),
        scratch_shapes=[
            pltpu.VMEM((rows, width), jnp.float32),
            pltpu.VMEM((rows, columns), jnp.float32),
        ],
        compiler_params=params(8),
        cost_estimate=SMALL,
    )(*hidden, *carried, in_vmem(weight))


def finish_kernel(*refs):
    terms, out, plain = refs[:-2], refs[-2], refs[-1]
    packed = terms[0][...]
    for term in terms[1:]:
        packed = packed + term[...].astype(jnp.float32)
    unpack_rows(plain, packed)
    out[...] = plain[...].astype(out.dtype)


def finish(terms, shape):
    return pl.pallas_call(
        finish_kernel,
        out_shape=jax.ShapeDtypeStruct(shape, jnp.bfloat16),
        in_specs=[WHOLE] * len(terms),
        out_specs=WHOLE,
        scratch_shapes=[pltpu.VMEM(shape, jnp.float32)],
        compiler_params=params(4),
        cost_estimate=SMALL,
    )(*terms)


def swap(value, axes, size, distance):
    return lax.ppermute(value, axes, [(i, i ^ distance) for i in range(size)])


def add(a, b):
    return a.astype(jnp.float32) + b.astype(jnp.float32)


def direct(tokens, gate_weight, up_weight, down_weight):
    n_gx = lax.axis_size("gx")
    n_token = lax.axis_size(TOKEN_AXES)
    width = gate_weight.shape[1] // n_gx

    held = fetch(gate_weight, up_weight, 2, width)
    features = jnp.concatenate(
        [tokens] + [swap(tokens, TOKEN_AXES, n_token, r) for r in range(1, n_token)], axis=0
    )
    rows = features.shape[0]

    def blocks_for(distances, blocks, after):
        return gate_up_stream(features, gate_weight, up_weight, distances, blocks, width, after)

    relayed = gate_up_held(features, held)
    arrived = swap(relayed, "gx", n_gx, 1)
    across, beside = blocks_for((3, 1), ((0, 1), (0,)), relayed)
    across = lax.optimization_barrier(add(across, arrived).astype(jnp.bfloat16))
    far = swap(across, "gx", n_gx, 3)
    near = [swap(beside, "gx", n_gx, 1)]
    (beside,) = blocks_for((1,), ((1,),), across)
    near.append(swap(beside, "gx", n_gx, 1))
    (own,) = blocks_for((0,), ((0, 1),), beside)
    hidden = activate_packed(own, far, near, rows, width)

    opposite = swap(hidden, "gx", n_gx, 2)
    first = [hidden, swap(hidden, "gx", n_gx, 1), opposite]
    second = [swap(opposite, "gx", n_gx, 1)]
    (partial_sum,) = down(first, (0, 1, 2), None, down_weight, rows, width, 1)
    outs = down(second, (3,), partial_sum, down_weight, rows, width, n_token)
    terms = [outs[0]] + [swap(outs[r], TOKEN_AXES, n_token, r) for r in range(1, n_token)]
    return finish(terms, tokens.shape)


def offloaded(tokens, gate_weight, up_weight, down_weight):
    features = lax.all_gather(tokens, TOKEN_AXES, axis=0, tiled=True)
    hidden_width = gate_weight.shape[1]
    gate_part = jnp.dot(features, gate_weight, preferred_element_type=jnp.float32)
    up_part = jnp.dot(features, up_weight, preferred_element_type=jnp.float32)
    summed = lax.psum(
        jnp.concatenate([gate_part, up_part], axis=1).astype(jnp.bfloat16), "gx"
    ).astype(jnp.float32)
    hidden = activate(summed[:, :hidden_width], summed[:, hidden_width:])
    partial_value = jnp.dot(hidden, down_weight, preferred_element_type=jnp.float32)
    return lax.psum_scatter(
        partial_value.astype(jnp.bfloat16), TOKEN_AXES, scatter_dimension=0, tiled=True
    )


def shards(tokens, gate_weight, up_weight, down_weight):
    n_gx = lax.axis_size("gx")
    n_token = lax.axis_size(TOKEN_AXES)
    rows = tokens.shape[0] * n_token
    tokens_fit = n_token > 1 and n_token & (n_token - 1) == 0 and rows % 4 == 0
    weights_fit = gate_weight.shape[1] % (128 * 4) == 0 and gate_weight.shape[0] % STEP == 0
    columns_fit = down_weight.shape[1] % (128 * 8) == 0
    if n_gx == 4 and tokens_fit and weights_fit and columns_fit:
        return direct(tokens, gate_weight, up_weight, down_weight)
    return offloaded(tokens, gate_weight, up_weight, down_weight)


def solution(mesh):
    return jax.shard_map(
        shards,
        mesh=mesh,
        in_specs=(
            P(("grp", "gy", "gz"), "gx"),
            P("gx", ("gy", "gz")),
            P("gx", ("gy", "gz")),
            P(("gy", "gz"), "gx"),
        ),
        out_specs=P(("grp", "gy", "gz"), "gx"),
        check_vma=False,
    )
```
